32 devices in a mesh: grp: 4 (over x, core), blk: 8 (over z, y).
Axes of the slice: x: 2, y: 2, z: 4, core: 2. Of those that a mesh axis runs over, the one named last changes fastest.
Arguments:
- layer_input: bfloat16 [2, 8, 512, 768], P(None, 'blk', 'grp'), may hold values from -6 to 6
- w_query: bfloat16 [2, 768, 768], P(None, 'blk', 'grp'), may hold values from -0.21875 to 0.21875
- w_key: bfloat16 [2, 768, 768], P(None, 'blk', 'grp'), may hold values from -0.21875 to 0.21875
- w_value: bfloat16 [2, 768, 768], P(None, 'blk', 'grp'), may hold values from -0.21875 to 0.21875
- b_query: bfloat16 [2, 768], P(None, ('grp', 'blk')), may hold values from -3 to 3
- b_value: bfloat16 [2, 768], P(None, ('grp', 'blk')), may hold values from -3 to 3
- w_out: bfloat16 [2, 768, 768], P(None, ('grp', 'blk')), may hold values from -3 to 3
- b_out: bfloat16 [2, 768], P(None, ('grp', 'blk')), may hold values from -2 to 2
- gain_one: bfloat16 [2, 768], P(None, ('grp', 'blk')), may hold values from 0.5 to 1.5
- bias_one: bfloat16 [2, 768], P(None, ('grp', 'blk')), may hold values from -2 to 2
- w_up: bfloat16 [2, 768, 3072], P(None, 'blk', 'grp'), may hold values from -0.21875 to 0.21875
- b_up: bfloat16 [2, 3072], P(None, ('grp', 'blk')), may hold values from -2 to 2
- w_down: bfloat16 [2, 3072, 768], P(None, ('grp', 'blk')), may hold values from -0.109375 to 0.109375
- b_down: bfloat16 [2, 768], P(None, ('grp', 'blk')), may hold values from -2 to 2
- gain_two: bfloat16 [2, 768], P(None, ('grp', 'blk')), may hold values from 0.5 to 1.5
- bias_two: bfloat16 [2, 768], P(None, ('grp', 'blk')), may hold values from -2 to 2
- head_table: int32 [2, 12, 2], replicated, may hold values from 0 to 1, as said below
- grad_top: bfloat16 [2, 8, 512, 768], P(None, 'blk', 'grp'), may hold values from -6 to 6
Outputs:
- layer_outputs: bfloat16 [2, 2, 8, 512, 768], P(None, None, 'blk', 'grp')
- grad_input: float32 [2, 8, 512, 768], P(None, 'blk', 'grp')
- grad_w_query: float32 [2, 768, 768], P(None, 'blk', 'grp')
- grad_w_key: float32 [2, 768, 768], P(None, 'blk', 'grp')
- grad_w_value: float32 [2, 768, 768], P(None, 'blk', 'grp')
- grad_b_query: float32 [2, 768], P(None, ('grp', 'blk'))
- grad_b_value: float32 [2, 768], P(None, ('grp', 'blk'))
- grad_w_out: float32 [2, 768, 768], P(None, ('grp', 'blk'))
- grad_b_out: float32 [2, 768], P(None, ('grp', 'blk'))
- grad_gain_one: float32 [2, 768], P(None, ('grp', 'blk'))
- grad_bias_one: float32 [2, 768], P(None, ('grp', 'blk'))
- grad_w_up: float32 [2, 768, 3072], P(None, 'blk', 'grp')
- grad_b_up: float32 [2, 3072], P(None, ('grp', 'blk'))
- grad_w_down: float32 [2, 3072, 768], P(None, ('grp', 'blk'))
- grad_b_down: float32 [2, 768], P(None, ('grp', 'blk'))
- grad_gain_two: float32 [2, 768], P(None, ('grp', 'blk'))
- grad_bias_two: float32 [2, 768], P(None, ('grp', 'blk'))
The draws below stay inside these ranges and needn't reach their ends.
Inputs may be any that keep to these rules, and one draw needn't show every extreme that they name: Each row head_table[l, h, :] is a permutation of the 2 blocks: the identity or its shift by one, drawn independently for each layer and head.
All inputs are finite; a program needn't handle non-finite values.
Results may differ from the reference program's by a relative error of at most 0.03.
Values may be sent and summed in bfloat16 or wider, within the bound.
No kernel may reach another device: no remote copies, remote signals or barrier semaphores. Data moves between devices by JAX's collectives and lax.ppermute only.
A program may use at most 192 MiB of HBM per device.

```python
import jax
import jax.numpy as jnp
from jax import lax

D = 768
HEADS = 12
HEAD = 64
FF = 3072
BLOCK = 512
NB = 2
LAYERS = 2
MICRO = 2
BLOCKS = 8
SEQS = 4


def draw_head_table(key, part):
    key = jax.random.fold_in(key, 7)
    flips = jax.random.randint(key, (LAYERS, HEADS, 1), 0, 2, dtype=jnp.int32)
    return (jnp.arange(NB, dtype=jnp.int32)[None, None, :] + flips) % NB


def strengthened(drawn, stream_key, source, target, blocks, factor):
    owner, partner = [(jnp.arange(drawn.shape[dim]) // (drawn.shape[dim] // blocks)).reshape([-1 if axis == dim else 1 for axis in range(drawn.ndim)]) for dim in (source, target)]
    chosen = jax.random.permutation(stream_key, blocks)[partner]
    strong = (owner == chosen) | (owner == (partner + blocks // 2) % blocks)
    return jnp.where(strong, factor * drawn, drawn)


def shard_levels(stream_key, dims, split, least, high):
    loudness, own = 1.0, jax.random.fold_in(stream_key, 6)
    for position, parts in split:
        heights = jnp.exp(jax.random.uniform(jax.random.fold_in(own, position), (parts,), jnp.float32, least / len(split), high / len(split)))
        loudness = loudness * jnp.repeat(heights, dims[position] // parts).reshape([-1 if axis == position else 1 for axis in range(len(dims))])
    return loudness


def noise(own_key, extent, scale, limit, cuts=(), held_as=jnp.bfloat16):
    values = jax.random.normal(own_key, extent, jnp.float32) * scale
    if len(cuts) > 0:
        values = shard_levels(own_key, extent, cuts, -0.22, 0.18) * values
    return jnp.clip(values, min=-limit, max=limit).astype(held_as)


def bell_draw_with(own_key, shape, width, limit, cuts, heavy, kind=jnp.bfloat16):
    entries = width * jax.random.normal(own_key, shape, jnp.float32)
    if cuts:
        entries = entries * shard_levels(own_key, shape, cuts, -0.22, 0.18)
    return jnp.clip(strengthened(entries, jax.random.fold_in(own_key, 3), *heavy), -limit, limit).astype(kind)


def setup_inputs(seed: int = 0) -> dict:
    key_of = jax.random.split(jax.random.key(seed), 19)
    return {
        "layer_input": noise(key_of[0], (MICRO, BLOCKS, BLOCK, D), 1.0, 6.0, ((1, 8), (2, 4))),
        "w_query": noise(key_of[1], (LAYERS, D, D), D ** -0.5, 0.21875, ((1, 8), (2, 4))),
        "w_key": noise(key_of[2], (LAYERS, D, D), D ** -0.5, 0.21875, ((1, 8), (2, 4))),
        "w_value": noise(key_of[3], (LAYERS, D, D), D ** -0.5, 0.21875, ((1, 8), (2, 4))),
        "b_query": noise(key_of[4], (LAYERS, D), 0.5, 3.0, ((1, 32),)),
        "b_value": noise(key_of[5], (LAYERS, D), 0.5, 3.0, ((1, 32),)),
        "w_out": noise(key_of[6], (LAYERS, D, D), (3 * D // BLOCK) ** -0.5, 3.0, ((1, 32),)),
        "b_out": noise(key_of[7], (LAYERS, D), 0.3, 2.0, ((1, 32),)),
        "gain_one": jnp.clip(1.0 + 0.1 * jax.random.normal(key_of[8], (LAYERS, D), jnp.float32), 0.5, 1.5).astype(jnp.bfloat16),
        "bias_one": noise(key_of[9], (LAYERS, D), 0.3, 2.0, ((1, 32),)),
        "w_up": noise(key_of[10], (LAYERS, D, FF), D ** -0.5, 0.21875, ((1, 8), (2, 4))),
        "b_up": noise(key_of[11], (LAYERS, FF), 0.3, 2.0, ((1, 32),)),
        "w_down": noise(key_of[12], (LAYERS, FF, D), FF ** -0.5, 0.109375, ((1, 32),)),
        "b_down": noise(key_of[13], (LAYERS, D), 0.3, 2.0, ((1, 32),)),
        "gain_two": jnp.clip(1.0 + 0.1 * jax.random.normal(key_of[14], (LAYERS, D), jnp.float32), 0.5, 1.5).astype(jnp.bfloat16),
        "bias_two": noise(key_of[15], (LAYERS, D), 0.3, 2.0, ((1, 32),)),
        "head_table": draw_head_table(jax.random.fold_in(key_of[18], 71), 0),
        "grad_top": bell_draw_with(key_of[17], (MICRO, BLOCKS, BLOCK, D), 1.0, 6.0, ((1, 8), (2, 4)), (1, 3, 8, 2.0)),
    }


@jax.custom_vjp
def low(v):
    return lax.optimization_barrier(v.astype(jnp.bfloat16)).astype(jnp.float32)

@jax.custom_vjp
def low_back(v):
    return v

def low_keep(v):
    return (low(v), None)

def low_pass(kept, grad):
    return (grad,)

def back_keep(v):
    return (v, None)

def back_low(kept, grad):
    return (low(grad),)
low.defvjp(low_keep, low_pass)
low_back.defvjp(back_keep, back_low)
epsilon = 1e-05
highest = lax.Precision.HIGHEST

def rounded_both(value):
    return low(low_back(value))

def product(left, right):
    return jnp.einsum('...d,de->...e', left, right, precision=highest)

def layer_norm(residual, gain_vec, shift_vec):
    middle = lax.optimization_barrier(jnp.mean(residual, -1, keepdims=True))
    center = residual - middle
    spread = lax.optimization_barrier(jnp.mean(center * center, -1, keepdims=True))
    return center * lax.rsqrt(spread + epsilon) * gain_vec + shift_vec

def head_attend(query_head, key_head, value_head, choose):
    key_used = jnp.einsum('ji,sitd->sjtd', choose, key_head, precision=highest)
    value_used = jnp.einsum('ji,sitd->sjtd', choose, value_head, precision=highest)
    scores = jnp.einsum('sjqd,sjkd->sjqk', query_head, key_used, precision=highest) * HEAD ** (-0.5)
    scores = low_back(scores)
    attn_probs = low(jax.nn.softmax(scores, axis=-1))
    return jnp.einsum('sjqk,sjkd->sjqd', attn_probs, value_used, precision=highest)

def by_heads(tensor):
    return jnp.moveaxis(tensor.reshape(tensor.shape[:-1] + (HEADS, HEAD)), -2, 0)

def layer_forward(inputs, weights, choose_all):
    w_query, w_key, w_value, b_query, b_value, w_out, b_out, gain_one, bias_one, w_up, b_up, w_down, b_down, gain_two, bias_two = weights
    queries = rounded_both(product(inputs, w_query) + b_query)
    key_rows = rounded_both(product(inputs, w_key))
    value_rows = rounded_both(product(inputs, w_value) + b_value)
    attend = jax.checkpoint(head_attend)

    def one_head(pieces):
        return attend(pieces[0], pieces[1], pieces[2], pieces[3])
    mixed_heads = lax.map(one_head, (by_heads(queries), by_heads(key_rows), by_heads(value_rows), choose_all))
    mixed_heads = rounded_both(jnp.moveaxis(mixed_heads, 0, -2).reshape(inputs.shape))
    resid_one = inputs + low_back(product(mixed_heads, w_out)) + b_out
    hidden_one = layer_norm(resid_one, gain_one, bias_one)
    pre_act = low_back(product(low(hidden_one), w_up) + b_up)
    activated = low(jax.nn.gelu(pre_act, approximate=False))
    resid_two = hidden_one + low_back(product(activated, w_down)) + b_down
    return low(layer_norm(resid_two, gain_two, bias_two))

def reference(layer_input, w_query, w_key, w_value, b_query, b_value, w_out, b_out, gain_one, bias_one, w_up, b_up, w_down, b_down, gain_two, bias_two, head_table, grad_top):
    weights = tuple((tensor.astype(jnp.float32) for tensor in (w_query, w_key, w_value, b_query, b_value, w_out, b_out, gain_one, bias_one, w_up, b_up, w_down, b_down, gain_two, bias_two)))
    choose = (head_table[..., None] == jnp.arange(NB, dtype=jnp.int32)).astype(jnp.float32)
    group_seqs = max(1, min(SEQS, 4096 // (NB * BLOCK)))
    while SEQS % group_seqs:
        group_seqs = group_seqs - 1
    group_count = SEQS // group_seqs
    group_shape = (MICRO * group_count, group_seqs, NB, BLOCK, D)
    inputs_all = layer_input.astype(jnp.float32).reshape(group_shape)
    grads_all = grad_top.astype(jnp.float32).reshape(group_shape)

    def forward(params, inputs):
        outputs = []
        hidden = inputs
        for layer_idx in range(LAYERS):
            hidden = layer_forward(hidden, tuple((tensor[layer_idx] for tensor in params)), choose[layer_idx])
            outputs.append(hidden)
        return jnp.stack(outputs)

    def scan_step(totals, pieces):
        outputs, pull_back = jax.vjp(forward, weights, pieces[0])
        cotangent = jnp.concatenate([jnp.zeros((LAYERS - 1,) + pieces[1].shape, jnp.float32), pieces[1][None]])
        grad_weights, grad_inputs = pull_back(cotangent)
        return (jax.tree.map(jnp.add, totals, grad_weights), (outputs, grad_inputs))
    zero_grads = tuple((jnp.zeros(tensor.shape, jnp.float32) for tensor in weights))
    totals, (outputs, grad_inputs) = lax.scan(scan_step, zero_grads, (inputs_all, grads_all))
    layer_outputs = jnp.moveaxis(outputs.reshape((MICRO, group_count, LAYERS, group_seqs, NB, BLOCK, D)), 2, 0)
    layer_outputs = layer_outputs.reshape((LAYERS, MICRO, SEQS * NB, BLOCK, D)).astype(jnp.bfloat16)
    grad_input = grad_inputs.reshape((MICRO, SEQS * NB, BLOCK, D))
    return (layer_outputs, grad_input, totals[0], totals[1], totals[2], totals[3], totals[4], totals[5], totals[6], totals[7], totals[8], totals[9], totals[10], totals[11], totals[12], totals[13], totals[14])
```

```python
import jax
import jax.numpy as jnp
from jax import lax
from jax.experimental import pallas as pl
from jax.experimental.pallas import tpu as pltpu
from jax.sharding import PartitionSpec as P

HEAD = 64
NB = 2
LAYERS = 2
EPS = 1e-05
SCALE = HEAD ** -0.5
BF = jnp.bfloat16
F32 = jnp.float32
SMALLS = 6
HINT = 200000000
def LAST(sum_feed, start_sum, sum_attend, sums_of, add_small, chain):
    a = lambda: SUM_EARLY or sum_feed(0)
    b = lambda: start_sum("feed", ("feed",), 0, ORDER_F)
    c = lambda: sum_attend(0)
    d = lambda: start_sum("attend", ("attend",), 0, [1, 2, 4])
    o = lambda: sums_of["one"].halve(chain)
    m = add_small
    f = lambda: sums_of["feed"].halve(chain)
    g = lambda: sums_of["attend"].halve(chain)
    return [dict(a=a,b=b,c=c,d=d,o=o,m=m,f=f,g=g)[x] for x in TAIL]
TAIL_FREE = False
SUM_EARLY = True
KEEP = False
HALVE = False
TAIL = "mcdabofgofg"
ORDER_F = [1, 2, 4]
ORDER_ONE = [2, 4, 1]
WEIGHTS = True
WEIGHT = {"qkv": .9, "choose": .5, "attend": 2.5, "feed": 2.6, "norm_two_qkv": 1.6, "norm_two": .6, "back_feed": 3.6,
          "back_attend": 5, "add_crossed": .6, "back_qkv": 1.2, "grad_feed": 5.5, "grad_attend": 3.7, "split": 1.8,
          "halve": .8, "assemble": 1.8, "place": 2, "pack": 1.2, "small": .8}
B_OUT, GAIN_ONE, BIAS_ONE, B_DOWN, GAIN_TWO, BIAS_TWO = [LAYERS * (2 + i) for i in range(SMALLS)]


def send_xor(block, axis, mask):
    count = lax.axis_size(axis)
    return lax.ppermute(block, axis, [(i, i ^ mask) for i in range(count)])


def dot(left, right):
    return lax.dot_general(left, right, (((1,), (0,)), ((), ())), preferred_element_type=F32)


def dot_tn(left, right):
    return lax.dot_general(left, right, (((0,), (0,)), ((), ())), preferred_element_type=F32)


def dot_nt(left, right):
    return lax.dot_general(left, right, (((1,), (1,)), ((), ())), preferred_element_type=F32)


def pick(array, index):
    tail = array.shape[1:]
    return array, pl.BlockSpec((None,) + tail, lambda i: (index,) + (0,) * len(tail))


def saved(out):
    return out + ("saved",)


def in_hbm(operand):
    array, spec = operand if isinstance(operand, tuple) else whole(operand)
    return (pltpu.with_memory_space_constraint(array, pltpu.HBM) if WEIGHTS else array), spec


def whole(array):
    return array, pl.BlockSpec(array.shape, lambda i: (0,) * array.ndim)


class Order:
    token = None
    on = True


def run(body, operands, outs, name, mib=16, scratch=(), chain=None):
    operands = [o if isinstance(o, tuple) else whole(o) for o in operands]
    reads = len(operands)
    outs = list(outs)
    writes = len(outs)
    extra = []
    if chain is not None and chain.token is not None:
        extra = [(chain.token, pl.BlockSpec(memory_space=pl.ANY))]
    if chain is not None and not chain.on:
        chain = None
    if chain is not None:
        outs.append(((8, 128), F32))
    kernel_outs = [pltpu.HBM(*o[:2]) if len(o) > 2 and KEEP else jax.ShapeDtypeStruct(*o[:2]) for o in outs]
    out_shape = [jax.ShapeDtypeStruct(*o[:2]) for o in outs]

    def trimmed(*refs):
        results = refs[reads + len(extra):]
        if chain is not None:
            results[writes][...] = jnp.zeros((8, 128), F32)
            results = results[:writes] + results[writes + 1:]
        body(*refs[:reads], *results)

    results = pl.pallas_call(
        trimmed,
        out_shape=kernel_outs,
        grid=(1,),
        in_specs=[spec for _, spec in operands + extra],
        out_specs=[pl.BlockSpec(o.shape, lambda i, nd=len(o.shape): (0,) * nd) for o in out_shape],
        scratch_shapes=list(scratch),
        compiler_params=pltpu.CompilerParams(vmem_limit_bytes=mib * 2 ** 20),
        cost_estimate=pl.CostEstimate(flops=int(HINT * WEIGHT.get(name, 1)), bytes_accessed=1, transcendentals=0),
        name=name,
    )(*[array for array, _ in operands + extra])
    if chain is not None:
        chain.token = results[writes]
    return results[:writes]


def deal(where, chunk, order, keep, send, index, value):
    distance = jnp.bitwise_xor(where[0], chunk)
    spot = 0
    for bit in order[1:]:
        spot = spot * 2 + (jnp.bitwise_and(distance, bit) // bit)
    gone = jnp.bitwise_and(distance, order[0]) != 0

    @pl.when(gone)
    def _():
        send[(spot,) + index] = value

    @pl.when(jnp.logical_not(gone))
    def _():
        keep[(spot,) + index] = value


def halve_kernel(kept, came, keep, send):
    count = keep.shape[0]
    for i in range(count):
        keep[i] = (kept[i].astype(F32) + came[i].astype(F32)).astype(BF)
        send[i] = (kept[count + i].astype(F32) + came[count + i].astype(F32)).astype(BF)


def unit_of(resid):
    middle = jnp.mean(resid, -1, keepdims=True)
    center = resid - middle
    spread = jnp.mean(center * center, -1, keepdims=True)
    root = lax.rsqrt(spread + EPS)
    return center * root, root


def summed(near, came, part):
    half = near.shape[0] // 2
    here = near[pl.ds(part * half, half), :].astype(F32)
    return here + came[pl.ds((1 - part) * half, half), :].astype(F32)


def parts_of(rows):
    return [(part, pl.ds(part * (rows // 2), rows // 2)) for part in range(2)]


def at_row(vec, row):
    return vec[pl.ds(row, 1), :]


def project(layer, at, rows, weights, biases, kv_out, q_out):
    split = kv_out.shape[2]
    cols = pl.ds(0, split + q_out.shape[2])
    for g in range(2):
        acc = dot(rows, weights[g][:, cols]) + biases[g][pl.ds(layer, 1), cols]
        kv_out[g, at, :] = acc[:, :split].astype(BF)
        q_out[g, at, :] = (acc[:, split:].astype(BF) * SCALE).astype(BF)


def qkv_kernel(layer, rows, w_own, w_other, b_own, b_other, kv_out, q_out):
    for _, at in parts_of(rows.shape[0]):
        project(layer, at, rows[at, :], (w_own, w_other), (b_own, b_other), kv_out, q_out)


def norm_two_rows(layer, part, at, near, came, resid_one, vec, resid_out, out):
    unit, _ = unit_of(resid_one[at, :])
    hidden = unit * at_row(vec, layer + GAIN_ONE) + at_row(vec, layer + BIAS_ONE)
    resid = hidden + summed(near, came, part) + at_row(vec, layer + B_DOWN)
    resid_out[at, :] = resid
    unit, _ = unit_of(resid)
    out[at, :] = (unit * at_row(vec, layer + GAIN_TWO) + at_row(vec, layer + BIAS_TWO)).astype(BF)


def norm_two_kernel(layer, near, came, resid_one, vec, resid_out, out):
    for part, at in parts_of(out.shape[0]):
        norm_two_rows(layer, part, at, near, came, resid_one, vec, resid_out, out)


def norm_two_qkv_kernel(layer, near, came, resid_one, vec, w_own, w_other, b_own, b_other,
                        resid_out, out, kv_out, q_out):
    for part, at in parts_of(out.shape[0]):
        norm_two_rows(layer, part, at, near, came, resid_one, vec, resid_out, out)
        project(layer + 1, at, out[at, :], (w_own, w_other), (b_own, b_other), kv_out, q_out)


def choose_kernel(kv, kv_far, far, *outs):
    width = outs[0].shape[1]
    for g in range(2):
        for k in range(2):
            cols = pl.ds(k * width, width)
            outs[2 * g + k][...] = jnp.where(
                far[g, :, cols] > 0.5, kv_far[g, :, cols].astype(F32), kv[g, :, cols].astype(F32)).astype(BF)


def attend_kernel(*refs):
    q, out_own, out_other, near, mixed, lse, used = refs[:1] + refs[9:]
    pieces, crossed = refs[1:5], refs[5:9]
    _, length, width = q.shape
    heads = width // HEAD
    for g in range(2):
        for k in range(2):
            used[2 * g + k, pl.ds(0, length), :] = pieces[2 * g + k][...]
            used[2 * g + k, pl.ds(length, length), :] = crossed[2 * (1 - g) + k][...]
        for head in range(heads):
            cols = pl.ds(head * HEAD, HEAD)
            key, value = used[2 * g, :, cols], used[2 * g + 1, :, cols]
            scores = dot_nt(key, q[g, :, cols])
            high = jnp.max(scores, 0, keepdims=True)
            expo = jnp.exp(scores - high)
            total = jnp.sum(expo, 0, keepdims=True)
            lse[pl.ds(g * heads + head, 1), :] = high + jnp.log(total)
            probs = (expo * (1.0 / total)).astype(BF)
            mixed[g, :, cols] = dot_tn(probs, value).astype(BF)
    near[...] = (dot(mixed[0], out_own[...]) + dot(mixed[1], out_other[...])).astype(BF)


def feed_kernel(layer, near, came, inputs, vec, up_own, up_other, down_own, down_other, b_own, b_other,
                resid_out, hidden_out, act_out, slope_out, near_out):
    ups, downs, biases = (up_own, up_other), (down_own, down_other), (b_own, b_other)
    for part, at in parts_of(near.shape[0]):
        resid = inputs[at, :].astype(F32) + summed(near, came, part) + at_row(vec, layer + B_OUT)
        resid_out[at, :] = resid
        unit, _ = unit_of(resid)
        hidden_out[at, :] = (unit * at_row(vec, layer + GAIN_ONE) + at_row(vec, layer + BIAS_ONE)).astype(BF)
        branch = 0.0
        for g in range(2):
            u = dot(hidden_out[at, :], ups[g][...]) + biases[g][pl.ds(LAYERS + layer, 1), :]
            cdf = 0.5 * (1.0 + lax.erf(u * (0.5 ** 0.5)))
            density = jnp.exp(-0.5 * u * u) * ((2.0 * jnp.pi) ** -0.5)
            act = (u * cdf).astype(BF)
            act_out[g, at, :] = act
            slope_out[g, at, :] = (cdf + u * density).astype(BF)
            branch = branch + dot(act, downs[g][...])
        near_out[at, :] = branch.astype(BF)


def norm_back(grad, resid, gain):
    unit, root = unit_of(resid)
    scaled = grad * gain
    mean_e = jnp.mean(scaled, -1, keepdims=True)
    mean_en = jnp.mean(scaled * unit, -1, keepdims=True)
    pulled = root * (scaled - mean_e - unit * mean_en)
    return pulled, (jnp.sum(grad * unit, 0, keepdims=True), jnp.sum(grad, 0, keepdims=True),
                    jnp.sum(pulled, 0, keepdims=True))


def back_norm(grads, gain_row, resid, vec, full_out, short_out, sums_out):
    sums_out[...] = jnp.zeros(sums_out.shape, F32)
    for part, at in parts_of(resid.shape[0]):
        grad = grads[-1][at, :].astype(F32)
        if len(grads) > 1:
            grad = grad + summed(grads[0], grads[1], part)
        pulled, sums = norm_back(grad, resid[at, :], at_row(vec, gain_row))
        full_out[at, :] = pulled
        short_out[at, :] = pulled.astype(BF)
        for index, s in enumerate(sums):
            sums_out[pl.ds(index, 1), :] += s


def back_feed_kernel(layer, grads, *refs):
    resid, vec, up_own, up_other, down_own, down_other, slope = refs[grads:grads + 7]
    full_out, short_out, sums_out, pre_out, bias_out, near_out = refs[grads + 7:]
    back_norm(refs[:grads], layer + GAIN_TWO, resid, vec, full_out, short_out, sums_out)
    ups, downs = (up_own, up_other), (down_own, down_other)
    totals = [0.0, 0.0]
    for _, at in parts_of(resid.shape[0]):
        branch = 0.0
        for g in range(2):
            pre = (dot_nt(short_out[at, :], downs[g][...]) * slope[g, at, :].astype(F32)).astype(BF)
            pre_out[g, at, :] = pre
            totals[g] = totals[g] + jnp.sum(pre.astype(F32), 0, keepdims=True)
            branch = branch + dot_nt(pre, ups[g][...])
        near_out[at, :] = branch.astype(BF)
    for g in range(2):
        bias_out[g] = totals[g]


def back_attend_kernel(layer, *refs):
    grads, (resid, vec, out_own, out_other, q, used, lse) = refs[:3], refs[3:10]
    full_out, short_out, sums_out, dq_out, stay = refs[10:15]
    go = refs[15:19]
    back_norm(grads, layer + GAIN_ONE, resid, vec, full_out, short_out, sums_out)
    _, length, width = q.shape
    heads = width // HEAD
    for g in range(2):
        d_mixed_all = dot_nt(short_out[...], (out_own, out_other)[g][...]).astype(BF)
        for head in range(heads):
            cols = pl.ds(head * HEAD, HEAD)
            key, value = used[2 * g, :, cols], used[2 * g + 1, :, cols]
            query = q[g, :, cols]
            d_mixed = d_mixed_all[:, head * HEAD:(head + 1) * HEAD]
            probs = jnp.exp(dot_nt(key, query) - lse[pl.ds(g * heads + head, 1), :])
            d_probs = dot_nt(value, d_mixed)
            inner = jnp.sum(d_probs * probs, 0, keepdims=True)
            d_scores = (probs * (d_probs - inner)).astype(BF)
            d_value = dot(probs.astype(BF), d_mixed)
            d_key = dot(d_scores, query)
            dq_out[g, :, cols] = (dot_tn(d_scores, key) * SCALE).astype(BF)
            for k, grad in enumerate((d_key, d_value)):
                stay[g, :, pl.ds(k * width + head * HEAD, HEAD)] = grad[:length]
                go[2 * g + k][:, cols] = grad[length:].astype(BF)


def add_crossed_kernel(*refs):
    stay, out = refs[0], refs[-1]
    width = refs[1].shape[1]
    for g in range(2):
        for k in range(2):
            cols = pl.ds(k * width, width)
            out[g, :, cols] = (stay[g, :, cols] + refs[1 + 2 * (1 - g) + k][...].astype(F32)).astype(BF)


def back_qkv_kernel(dq, dkv, dkv_far, far, w_own, w_other, all_out, bias_out, *outs):
    split = dkv.shape[2]
    cols = pl.ds(0, all_out.shape[2])
    for g in range(2):
        all_out[g, :, pl.ds(0, split)] = jnp.where(
            far[g] > 0.5, dkv_far[g].astype(F32), dkv[g].astype(F32)).astype(BF)
        all_out[g, :, pl.ds(split, dq.shape[2])] = dq[g]
        bias_out[g] = jnp.sum(all_out[g].astype(F32), 0, keepdims=True)
    for part, at in parts_of(dq.shape[1]):
        branch = dot_nt(all_out[0, at, :], w_own[:, cols]) + dot_nt(all_out[1, at, :], w_other[:, cols])
        if len(outs) == 1:
            outs[0][at, :] = branch.astype(BF)
        else:
            outs[part][...] = branch.astype(outs[part].dtype)


def grad_feed_kernel(count, shares, *refs):
    here, away = refs[4 * count], refs[4 * count + 1:]
    feat = refs[0].shape[1]
    rows = feat // shares
    tile = feat // 2
    for g in range(2):
        for t in range(2):
            cols = pl.ds(t * tile, tile)
            up, down = 0.0, 0.0
            for m in range(count):
                hid, feed, pre, act = refs[4 * m:4 * m + 4]
                up = up + dot_tn(hid[:, cols], pre[g])
                down = down + dot_tn(act[g, :, cols], feed[...])
            for k, grad in enumerate((up, down)):
                if g == 0 or len(away) == 1:
                    (here, away[0])[g][k, cols, :] = grad.astype(BF)
                    continue
                for b in range(shares // 2):
                    away[t * (shares // 2) + b][k] = grad[b * rows:(b + 1) * rows].astype(BF)


def fold(block, width):
    return jnp.concatenate([block[:, c:c + width] for c in range(0, block.shape[1], width)], 0)


def unfold(block, rows):
    return jnp.concatenate([block[c:c + rows] for c in range(0, block.shape[0], rows)], 1)


def grad_attend_kernel(count, shares, vectors, *refs):
    smalls = refs[4 * count:4 * count + 2 * vectors]
    here, *away = refs[4 * count + 2 * vectors:]
    feat = refs[0].shape[1]
    split = refs[2].shape[2]
    width = split // 3
    rows, thin = feat // shares, width // shares
    stride = here.shape[0] // shares
    for g in range(2):
        acc, out = 0.0, 0.0
        for m in range(count):
            inputs, branch, d_qkv, mixed = refs[4 * m:4 * m + 4]
            acc = acc + dot_tn(inputs[...], d_qkv[g])
            out = out + dot_tn(mixed[g], branch[...])
        for b in range(shares):
            if g == 0 or len(away) == 1:
                ref, first = (here, away[0])[g], b * stride
            else:
                ref, first = away[b], 0
            at = pl.ds(first, rows)
            if vectors:
                ref[pl.ds(first + rows, stride - rows), :] = smalls[g][...].astype(BF)
            ref[at, pl.ds(0, split)] = acc[b * rows:(b + 1) * rows].astype(BF)
            ref[at, pl.ds(split, width)] = fold(out[b * thin:(b + 1) * thin, :], width).astype(BF)


def split_kernel(shares, order, feeds, attends, *refs):
    where, keep, send = refs[-3:]
    groups = [refs[1 + (1 + shares) * n - 1:(1 + shares) * (n + 1)] for n in range(feeds + attends)]
    for b in range(shares):
        spot = 0
        for here, *came in groups:
            rows = here.shape[-2] // shares
            for index in ((0,), (1,)) if len(here.shape) == 3 else ((),):
                mine = here[index + (pl.ds(b * rows, rows), slice(None))].astype(F32)
                value = mine + came[b][index + (slice(None), slice(None))].astype(F32)
                deal(where, b, order, keep, send, (spot,), value.astype(BF))
                spot += 1


def unfold_kernel(shares, *refs):
    for ref, out in zip(refs[:2], refs[2:]):
        width, feat = out.shape
        rows, thin = feat // shares, width // shares
        blocks = [unfold(ref[pl.ds(b * rows, rows), pl.ds(3 * width, width)].astype(F32), thin) for b in range(shares)]
        out[...] = jnp.concatenate(blocks, 0).astype(BF)


def pack_kernel(*refs):
    key, value, query, out = refs[:4]
    rows, width = key.shape
    payload = refs[-1]
    if len(refs) > 5:
        payload, small = refs[-2:]
    at = pl.ds(0, rows)
    for index, ref in enumerate((key, value, query)):
        payload[at, pl.ds(index * width, width)] = ref[...]
    payload[at, pl.ds(3 * width, width)] = fold(out[...].astype(F32), width).astype(BF)
    if len(refs) > 5:
        small[...] = jnp.zeros(small.shape, F32)
        for index, ref in enumerate(refs[4:-3]):
            small[pl.ds(LAYERS * index, LAYERS), pl.ds(0, ref.shape[1])] = ref[...].astype(F32)
        up = refs[-3]
        small[pl.ds(0, LAYERS), pl.ds(128, up.shape[1])] = up[...].astype(F32)
        payload[pl.ds(rows, small.shape[0]), :] = small[...].astype(BF)


def shares_kernel(key, value, query, out, up_early, down_early, up_late, down_late, early, late):
    early[0] = up_early[...]
    early[1] = down_early[...]
    pack_kernel(key, value, query, out, early.at[2])
    late[0] = up_late[...]
    late[1] = down_late[...]


def assemble_kernel(masks, per, up_per, *refs):
    count = len(masks)
    where = refs[2 * count]
    small_outs = len(refs) - 2 * count - 1 - 5 > 0
    if small_outs:
        spread, up_spread = refs[2 * count + 1:2 * count + 3]
        outs, (table, bias_own, bias_other), scratch = refs[2 * count + 3:-4], refs[-4:-1], refs[-1]
    else:
        outs, scratch = refs[2 * count + 1:-1], refs[-1]
    blk, grp = where[0], where[1]
    width, feat = outs[2].shape
    rows, thin = feat // count, width // count
    if small_outs:
        lane = lax.broadcasted_iota(jnp.int32, table.shape, 1)
        row = lax.broadcasted_iota(jnp.int32, table.shape, 0)
        six = 0.0
    for g in range(2):
        projection, hidden = 0.0, 0.0
        for index, mask in enumerate(masks):
            ref = refs[g * count + index]
            b = jnp.bitwise_xor(blk, mask)
            outs[g][pl.ds(pl.multiple_of(b * rows, rows), rows), :] = ref[pl.ds(0, rows), pl.ds(0, 3 * width)]
            block = ref[pl.ds(0, rows), pl.ds(3 * width, width)].astype(F32)
            scratch[pl.ds(pl.multiple_of(b * thin, thin), thin), :] = unfold(block, thin)
            if not small_outs:
                continue
            small = ref[pl.ds(rows, table.shape[0]), :]
            spreaded = dot(small[:, :per], spread[...])
            at = lane - (jnp.bitwise_xor(grp, g) * count + b) * per
            six = six + jnp.where((at >= 0) & (at < per), spreaded, 0.0)
            at = lane - b * per - jnp.where(row < LAYERS, 2 * width, width)
            projection = projection + jnp.where((at >= 0) & (at < per), spreaded, 0.0)
            at = lane - b * up_per
            hidden = hidden + jnp.where((at >= 0) & (at < up_per), dot(small[:, 128:128 + up_per], up_spread[...]), 0.0)
        outs[2 + g][...] = scratch[...].astype(BF)
        if small_outs:
            bias = (bias_own, bias_other)[g]
            bias[...] = jnp.zeros(bias.shape, F32)
            bias[pl.ds(0, LAYERS), :] = projection[:LAYERS] + projection[LAYERS:2 * LAYERS]
            bias[pl.ds(LAYERS, LAYERS), :] = hidden[:LAYERS]
    if small_outs:
        table[...] = six.astype(BF)


def small_kernel(layers, *refs):
    out, other = refs[-2:]
    out[...] = jnp.zeros(out.shape, F32)
    other[...] = jnp.zeros(other.shape, F32)
    per_layer = (len(refs) - 2) // layers
    for layer in range(layers):
        mine = refs[layer * per_layer:(layer + 1) * per_layer]
        sets = [mine[i:i + 4] for i in range(0, per_layer, 4)]
        base = 8 * layer
        for row, (which, index) in enumerate(((1, 2), (1, 0), (1, 1), (0, 2), (0, 0), (0, 1))):
            total = sum(s[which][pl.ds(index, 1), :] for s in sets)
            out[pl.ds(base + row, 1), :] = total
            other[pl.ds(base + row, 1), :] = total
        cols = pl.ds(0, sets[0][3].shape[2])
        for g, ref in enumerate((out, other)):
            ref[pl.ds(base + 6, 1), :] = sum(s[2][g] for s in sets)
            ref[pl.ds(base + 7, 1), cols] = sum(s[3][g] for s in sets)


def bits_of(count):
    return list(range(count.bit_length() - 1))


class Gather:
    def __init__(self, share):
        self.pieces = {0: share}

    def step(self, bits, after):
        held = dict(self.pieces)
        for mask, piece in held.items():
            if after is not None:
                piece, _ = lax.optimization_barrier((piece, after))
            for bit in bits:
                self.pieces[mask | bit] = send_xor(piece, "blk", bit)

    def over_y(self, masks):
        for mask in masks:
            self.pieces[mask | 1] = send_xor(self.pieces[mask], "blk", 1)

    def both(self, after):
        masks = sorted(self.pieces)
        own = [self.pieces[m] for m in masks]
        if after is not None:
            ready = [lax.optimization_barrier((piece, after))[0] for piece in own]
        else:
            ready = own
        return masks, own + [send_xor(piece, "grp", 1) for piece in ready]


class Scatter:
    def __init__(self, keep, send, order):
        self.keep = keep
        self.came = send_xor(send, "blk", order[0])
        self.order = order[1:]

    def halve(self, chain):
        shape = (self.keep.shape[0] // 2,) + self.keep.shape[1:]
        self.keep, send = run(halve_kernel, [self.keep, self.came], [(shape, BF)] * 2, "halve", chain=chain)
        self.came = send_xor(send, "blk", self.order[0])
        self.order = self.order[1:]

    def total(self):
        return self.keep[0].astype(F32) + self.came[0].astype(F32)


def sum_axis(block, axis, masks):
    for mask in masks:
        block = block + send_xor(block, axis, mask)
    return block


def fold_share(block, width):
    rows = block.shape[0]
    return jnp.moveaxis(block.reshape(rows, -1, width), 1, 0).reshape(-1, width)


def unfold_shares(columns, shares, feat):
    width = columns.shape[1]
    blocks = columns.reshape(shares, feat // width, -1, width)
    return jnp.moveaxis(blocks, 1, 2).reshape(-1, feat)


def stream(rows, grad_rows, shape, hid, weights, chain, result):
    half, feat = shape
    width = feat // 4
    lse_rows = -(-(2 * width // HEAD) // 8) * 8

    def stage(body, operands, outs, name):
        return run(body, operands, outs, name, chain=chain)

    def over_x(near):
        return [near, send_xor(near, "grp", 2)]

    def over_core(pieces):
        return [send_xor(piece, "grp", 1) for piece in pieces]

    wide, short = ((half, feat), F32), ((half, feat), BF)
    projected = [((2, half, 2 * width), BF), saved(((2, half, width), BF))]
    pieces = 4 * [((half, width), BF)]
    hidden_shape = saved(((2, half, hid), BF))
    sums_shape = ((8, feat), F32)
    kept = []
    for layer in range(LAYERS):
        w = weights[layer]
        if layer == 0:
            kv, q = stage(lambda *r: qkv_kernel(layer, *r), [rows, *w["qkv"], *w["bias"]], projected, "qkv")
        kv_far = send_xor(kv, "blk", 1)
        yield "qkv", layer
        chosen = list(stage(lambda *r: choose_kernel(*r[:3], *r[4:]), [kv, kv_far, w["far"], w["vec"]], pieces, "choose"))
        chosen += over_core(chosen)
        near, mixed, lse, used = stage(
            attend_kernel, [q] + chosen + [*w["out"]],
            [short, saved(((2, half, width), BF)), saved(((lse_rows, half), F32)),
             saved(((4, 2 * half, width), BF))], "attend")
        branch = over_x(near)
        yield "attend", layer
        resid_one, hidden, act, slope, near = stage(
            lambda *r: feed_kernel(layer, *r),
            branch + [rows, w["vec"], *w["up"], *w["down"], *w["bias"]],
            [saved(wide), saved(short), hidden_shape, hidden_shape, short], "feed")
        branch = over_x(near)
        yield "feed", layer
        before = (rows, q, used, lse, mixed, resid_one, hidden, act, slope)
        if layer < LAYERS - 1:
            after = weights[layer + 1]
            resid_two, rows, kv, q = stage(
                lambda *r: norm_two_qkv_kernel(layer, *r),
                branch + [resid_one, w["vec"], *after["qkv"], *after["bias"]],
                [saved(wide), saved(short)] + projected, "norm_two_qkv")
        else:
            resid_two, rows = stage(lambda *r: norm_two_kernel(layer, *r), branch + [resid_one, w["vec"]],
                                    [wide, short], "norm_two")
        result["outputs"].append(rows[:half // 2])
        kept.append(before + (resid_two,))

    grads = [grad_rows]
    for layer in reversed(range(LAYERS)):
        w = weights[layer]
        rows, q, used, lse, mixed, resid_one, hidden, act, slope, resid_two = kept[layer]
        d_two, feed, sums_two, d_pre, g_up, near = stage(
            lambda *r: back_feed_kernel(layer, len(grads), *r),
            grads + [resid_two, w["vec"], *w["up"], *w["down"], slope],
            [wide, saved(short), saved(sums_shape), hidden_shape, saved(((2, 1, hid), F32)), short], "back_feed")
        result["feed"][layer] = [hidden, feed, d_pre, act]
        branch = over_x(near)
        yield "back_feed", layer
        d_one, branch, sums_one, dq, stay, *go = stage(
            lambda *r: back_attend_kernel(layer, *r),
            branch + [d_two, resid_one, w["vec"], *w["out"], q, used, lse],
            [wide, saved(short), saved(sums_shape), ((2, half, width), BF), ((2, half, 2 * width), F32)] + pieces, "back_attend")
        dkv, = stage(add_crossed_kernel, [stay] + over_core(go), [((2, half, 2 * width), BF)], "add_crossed")
        dkv_far = send_xor(dkv, "blk", 1)
        yield "back_attend", layer
        outs = [short] if layer else [((half // 2, feat), F32), ((half // 2, feat), BF)]
        d_qkv, g_qkv, *outs = stage(
            back_qkv_kernel, [dq, dkv, dkv_far, w["far"], *w["qkv"]],
            [saved(((2, half, 3 * width), BF)), saved(((2, 1, 3 * width), F32))] + outs, "back_qkv")
        result["attend"][layer] = [rows, branch, d_qkv, mixed]
        result["smalls"][layer] = [sums_two, sums_one, g_up, g_qkv]
        if layer:
            grads = over_x(outs[0]) + [d_one]
        else:
            came = send_xor(outs[1], "grp", 2)
            result["grad"] = d_one[:half // 2] + outs[0] + came.astype(F32)
        yield "back_qkv", layer


def per_device(layer_input, w_query, w_key, w_value, b_query, b_value, w_out, b_out, gain_one,
               bias_one, w_up, b_up, w_down, b_down, gain_two, bias_two, head_table, grad_top):
    blk_count = lax.axis_size("blk")
    grp_count = lax.axis_size("grp")
    grp = lax.axis_index("grp")
    blk = lax.axis_index("blk")
    feat = w_out.shape[2]
    share_rows = w_query.shape[1]
    width = w_query.shape[2]
    heads = width // HEAD
    hid = w_up.shape[2]
    per = b_out.shape[1]
    up_per = b_up.shape[1]
    blk_masks = [1 << bit for bit in bits_of(blk_count)[::-1]]
    packed = blk_count == 8 and share_rows % 32 == 0 and per % 8 == 0
    block_own = blk % NB
    target = jnp.where(block_own == 0, head_table[:, :, 0], head_table[:, :, 1])
    far = (target != block_own).astype(F32)
    far = jnp.stack([lax.dynamic_slice_in_dim(far, g * heads, heads, 1) for g in (grp, grp ^ 1)], 1)
    far_cols = jnp.broadcast_to(far[:, :, None, :, None], (LAYERS, 2, 2, heads, HEAD)).reshape(LAYERS, 2, 1, 2 * width)

    start = layer_input[:, 0]
    row_top = jnp.concatenate([start, send_xor(start, "grp", 2)], 1)
    grad_start = grad_top[:, 0]
    grad_rows = jnp.concatenate([grad_start, send_xor(grad_start, "grp", 2)], 1)

    micros = range(layer_input.shape[0])
    count = len(micros)
    chain = Order()
    results = [{"outputs": [], "feed": {}, "attend": {}, "smalls": {}} for _ in micros]
    weights = [{"far": pick(far_cols, layer)} for layer in range(LAYERS)]
    where = (jnp.stack([blk, grp]).astype(jnp.int32), pl.BlockSpec((2,), lambda i: (0,), memory_space=pltpu.SMEM))
    grad_feed, grad_attend, tiny = {}, {}, []
    smalls = [b_query, b_value, b_out, gain_one, bias_one, b_down, gain_two, bias_two]
    small_rows = len(smalls) * LAYERS
    vec_shape = (small_rows, feat)

    def factors(name, layer):
        return [f for r in results for f in r[name][layer]]

    chunks = blk_count if packed else 1

    def sum_feed(layer):
        rest = [((2, feat // chunks, hid), BF)] * chunks
        grad_feed[layer] = run(lambda *r: grad_feed_kernel(count, chunks, *r), factors("feed", layer),
                               [((2, feat, hid), BF)] + rest, "grad_feed", 16, chain=chain)

    def sum_attend(layer):
        vectors = tiny if packed and layer == 0 else []
        high = feat + (len(vectors) // 2) * blk_count * 8 * LAYERS
        rest = [((high // chunks, feat), BF)] * chunks
        grad_attend[layer] = run(lambda *r: grad_attend_kernel(count, blk_count, len(vectors) // 2, *r),
                                 factors("attend", layer) + vectors, [((high, feat), BF)] + rest, "grad_attend", 16,
                                 chain=chain)

    def add_small():
        sums = sum([r["smalls"][layer] for layer in range(LAYERS) for r in results], [])
        tiny.extend(run(lambda *r: small_kernel(LAYERS, *r), sums, [((8 * LAYERS, feat), F32)] * 2, "small",
                        chain=chain))

    if packed:
        def pack(layer, *more, scratch=(), order=None):
            rows = share_rows + (small_rows if more else 0)
            return run(pack_kernel, [pick(a, layer) for a in (w_key, w_value, w_query, w_out)] + list(more),
                       [((rows, feat), BF)], "pack", 60, scratch, order)[0]

        first = Gather(pack(0, *smalls, b_up, scratch=[pltpu.VMEM(vec_shape, F32)]))
        first.step([1, 2, 4, 6], None)
        first.over_y([2, 4, 6])
        early, late = run(
            shares_kernel, [pick(a, 1) for a in (w_key, w_value, w_query, w_out)]
            + [pick(a, layer) for layer in range(LAYERS) for a in (w_up, w_down)],
            [((3, share_rows, feat), BF), ((2, share_rows, feat), BF)], "shares", 60)
        gathered = {"early": lax.all_gather(early, "blk", axis=1, tiled=True)}
        lanes = jnp.arange(feat)[None, :]
        spread = (lanes % per == jnp.arange(per)[:, None]).astype(BF)
        up_spread = (lanes % up_per == jnp.arange(up_per)[:, None]).astype(BF)

        def start_feed():
            block = lax.optimization_barrier((late, chain.token))[0]
            gathered["late"] = lax.all_gather(block, "blk", axis=1, tiled=True)

        def over_cores(name):
            block = gathered[name]
            return [block, send_xor(lax.optimization_barrier((block, chain.token))[0], "grp", 1)]

        def have_early():
            both = over_cores("early")
            outs = run(lambda *r: unfold_kernel(blk_count, *r), [pick(b, 2) for b in both], [((width, feat), BF)] * 2,
                       "unfold")
            weights[0].update(up=[in_hbm(pick(b, 0)) for b in both], down=[in_hbm(pick(b, 1)) for b in both])
            weights[1].update(qkv=[in_hbm(pick(b, 2)) for b in both], out=outs)

        def have_late():
            both = over_cores("late")
            weights[1].update(up=[in_hbm(pick(b, 0)) for b in both], down=[in_hbm(pick(b, 1)) for b in both])

        def split(names, layer, order):
            groups, kinds = [], []
            for name in names:
                here, *away = (grad_feed if name == "feed" else grad_attend)[layer]
                groups += [here] + [send_xor(piece, "grp", 1) for piece in away]
            depth = 2 * ("feed" in names) + ("attend" in names)
            outs = [((blk_count // 2, depth, groups[0].shape[-2] // blk_count, feat), BF)] * 2
            keep, send = run(lambda *r: split_kernel(blk_count, order, int("feed" in names), int("attend" in names), *r),
                             groups + [where], outs, "split", 16, chain=chain)
            return Scatter(keep, send, order)

        sums_of = {}

        def start_sum(key, names, layer, order):
            sums_of[key] = split(names, layer, order)

        masks, pieces = first.both(None)
        outs = run(lambda *r: assemble_kernel(masks, per, up_per, *r), pieces + [where, spread, up_spread],
                   [((feat, 3 * width), BF)] * 2 + [((width, feat), BF)] * 2 + [(vec_shape, BF)] + [((8, feat), F32)] * 2,
                   "assemble", scratch=[pltpu.VMEM((width, feat), F32)], chain=chain)
        weights[0].update(qkv=outs[:2], out=outs[2:4])
        table, *biases = outs[4:]

        def free():
            chain.on = False
        vec = table + send_xor(table, "grp", 2)
        after = {
            ("attend", 0, 1): lambda: (have_early(), start_feed()),
            ("attend", 1, 1): have_late,
            ("back_feed", 0, 0): lambda: (sum_feed(1), sum_attend(1)),
            ("back_feed", 0, 1): lambda: start_sum("one", ("feed", "attend"), 1, ORDER_ONE),
            ("back_attend", 0, 1): lambda: SUM_EARLY and sum_feed(0),
            ("back_qkv", 0, 0): lambda: HALVE and sums_of["one"].halve(chain),
            ("back_qkv", 0, 1): lambda: [free() if TAIL_FREE else None] + [step() for step in LAST(sum_feed, start_sum, sum_attend, sums_of, add_small, chain)],
        }
    else:
        table = jnp.zeros(vec_shape, BF)
        rows = jnp.stack(smalls).reshape(small_rows, per)
        table = lax.dynamic_update_slice(table, rows, (0, (grp * blk_count + blk) * per))
        spots = jnp.zeros((8, feat), BF)
        spots = lax.dynamic_update_slice(spots, b_query, (0, 2 * width + blk * per))
        spots = lax.dynamic_update_slice(spots, b_value, (LAYERS, width + blk * per))
        spots = lax.dynamic_update_slice(spots, b_up, (2 * LAYERS, blk * up_per))
        table = sum_axis(table, "blk", blk_masks)
        spots = sum_axis(spots, "blk", blk_masks).astype(F32)
        bias = jnp.zeros((8, feat), F32)
        bias = bias.at[:LAYERS].set(spots[:LAYERS] + spots[LAYERS:2 * LAYERS])
        bias = bias.at[LAYERS:2 * LAYERS].set(spots[2 * LAYERS:3 * LAYERS])
        for layer in range(LAYERS):
            block = jnp.concatenate([w_key[layer], w_value[layer], w_query[layer],
                                     fold_share(w_out[layer], width)], 1)
            block = lax.all_gather(block, "blk", axis=0, tiled=True)
            pair = [block, send_xor(block, "grp", 1)]
            block = lax.all_gather(jnp.stack([w_up[layer], w_down[layer]]), "blk", axis=1, tiled=True)
            both = [block, send_xor(block, "grp", 1)]
            weights[layer].update(qkv=[b[:, :3 * width] for b in pair],
                                  out=[unfold_shares(b[:, 3 * width:], blk_count, feat) for b in pair],
                                  up=[pick(b, 0) for b in both], down=[pick(b, 1) for b in both])
        biases = [bias, send_xor(bias, "grp", 1)]
        vec = sum_axis(table, "grp", [2, 1])
        after = {}
        for layer in range(LAYERS):
            after["back_feed", layer, count - 1] = lambda layer=layer: sum_feed(layer)
            after["back_qkv", layer, count - 1] = lambda layer=layer: sum_attend(layer)

    vec = vec.astype(F32)
    for w in weights:
        w.update(vec=vec, bias=biases)
    streams = [stream(pick(row_top, m), pick(grad_rows, m), row_top.shape[1:], hid, weights, chain, results[m])
               for m in micros]
    done = False
    while not done:
        for m, one in enumerate(streams):
            label = next(one, None)
            done = label is None
            if not done and label + (m,) in after:
                after[label + (m,)]()
    if packed:
        one, feed, attend = [sums_of[key].total() for key in ("one", "feed", "attend")]
        grad_feed, grad_attend = {0: feed, 1: one[:2]}, {0: attend[0, :share_rows], 1: one[2]}
    else:
        for dim, sums in ((1, grad_feed), (0, grad_attend)):
            for layer in sums:
                block = sums[layer][0] + send_xor(sums[layer][1], "grp", 1)
                sums[layer] = lax.psum_scatter(block, "blk", scatter_dimension=dim, tiled=True).astype(F32)

    if packed:
        tiny = attend[0, share_rows:]
    else:
        add_small()
        tiny = sum_axis(tiny[0] + send_xor(tiny[1], "grp", 1), "blk", blk_masks)
    tiny = tiny.reshape(LAYERS, 8, feat)
    six = tiny[:, :SMALLS]
    six = lax.dynamic_slice_in_dim(six, (grp * blk_count + blk) * per, per, 2)
    g_b_up = lax.dynamic_slice_in_dim(tiny[:, 6], blk * up_per, up_per, 1)
    g_b_value = lax.dynamic_slice_in_dim(tiny[:, 7], width + blk * per, per, 1)
    g_b_query = lax.dynamic_slice_in_dim(tiny[:, 7], 2 * width + blk * per, per, 1)
    feeds = jnp.stack([grad_feed[layer] for layer in range(LAYERS)])
    attends = jnp.stack([grad_attend[layer] for layer in range(LAYERS)])
    g_out = jnp.stack([unfold_shares(attends[layer, :, 3 * width:], 1, feat) for layer in range(LAYERS)])
    return (
        jnp.stack([jnp.stack([r["outputs"][layer] for r in results]) for layer in range(LAYERS)])[:, :, None],
        jnp.stack([r["grad"] for r in results])[:, None],
        attends[:, :, 2 * width:3 * width],
        attends[:, :, :width],
        attends[:, :, width:2 * width],
        g_b_query,
        g_b_value,
        g_out,
        six[:, 0],
        six[:, 1],
        six[:, 2],
        feeds[:, 0],
        g_b_up,
        feeds[:, 1],
        six[:, 3],
        six[:, 4],
        six[:, 5],
    )


def solution(mesh):
    rows = P(None, "blk", "grp", None)
    cols = P(None, "blk", "grp")
    both = P(None, ("grp", "blk"))
    tall = P(None, ("grp", "blk"), None)
    return jax.shard_map(
        per_device,
        mesh=mesh,
        in_specs=(rows, cols, cols, cols, both, both, tall, both, both, both, cols, both, tall,
                  both, both, both, P(), rows),
        out_specs=(P(None, None, "blk", "grp", None), rows, cols, cols, cols, both, both, tall,
                   both, both, both, cols, both, tall, both, both, both),
        check_vma=False,
    )
```

```python
import jax
import jax.numpy as jnp
from jax import lax
from jax.experimental import pallas as pl
from jax.experimental.pallas import tpu as pltpu
from jax.sharding import PartitionSpec as P

HEAD = 64
NB = 2
LAYERS = 2
EPS = 1e-05
SCALE = HEAD ** -0.5
BF = jnp.bfloat16
F32 = jnp.float32
SMALLS = 6
HINT = 200000000
SLOTS = {
    ("back_feed", 1, 1): "A", ("back_qkv", 1, 0): "B", ("back_feed", 0, 0): "C", ("back_feed", 0, 1): "FD",
    ("back_attend", 0, 1): "a", ("back_qkv", 0, 0): "GF", ("back_qkv", 0, 1): "mcdbeghfGghf",
}
ORDERS = {"A": [2, 4, 1], "C": [2, 4, 1], "a": [1, 2, 4], "e": [2, 4, 1], "c": [1, 2, 4]}
KEEP = False
WEIGHTS = True
WEIGHT = {"qkv": .9, "choose": .5, "attend": 2.5, "feed": 2.6, "norm_two_qkv": 1.6, "norm_two": .6, "back_feed": 3.6,
          "back_attend": 5, "add_crossed": .6, "back_qkv": 1.2, "grad_feed": 5.5, "grad_attend": 3.7, "split": 1.8,
          "halve": .8, "assemble": 1.8, "place": 2, "pack": 1.2, "small": .8}
B_OUT, GAIN_ONE, BIAS_ONE, B_DOWN, GAIN_TWO, BIAS_TWO = [LAYERS * (2 + i) for i in range(SMALLS)]


def send_xor(block, axis, mask):
    count = lax.axis_size(axis)
    return lax.ppermute(block, axis, [(i, i ^ mask) for i in range(count)])


def dot(left, right):
    return lax.dot_general(left, right, (((1,), (0,)), ((), ())), preferred_element_type=F32)


def dot_tn(left, right):
    return lax.dot_general(left, right, (((0,), (0,)), ((), ())), preferred_element_type=F32)


def dot_nt(left, right):
    return lax.dot_general(left, right, (((1,), (1,)), ((), ())), preferred_element_type=F32)


def pick(array, index):
    tail = array.shape[1:]
    return array, pl.BlockSpec((None,) + tail, lambda i: (index,) + (0,) * len(tail))


def saved(out):
    return out + ("saved",)


def in_hbm(operand):
    array, spec = operand if isinstance(operand, tuple) else whole(operand)
    return (pltpu.with_memory_space_constraint(array, pltpu.HBM) if WEIGHTS else array), spec


def whole(array):
    return array, pl.BlockSpec(array.shape, lambda i: (0,) * array.ndim)


class Order:
    token = None
    on = True


def run(body, operands, outs, name, mib=16, scratch=(), chain=None):
    operands = [o if isinstance(o, tuple) else whole(o) for o in operands]
    reads = len(operands)
    outs = list(outs)
    writes = len(outs)
    extra = []
    if chain is not None and chain.token is not None:
        extra = [(chain.token, pl.BlockSpec(memory_space=pl.ANY))]
    if chain is not None and not chain.on:
        chain = None
    if chain is not None:
        outs.append(((8, 128), F32))
    kernel_outs = [pltpu.HBM(*o[:2]) if len(o) > 2 and KEEP else jax.ShapeDtypeStruct(*o[:2]) for o in outs]
    out_shape = [jax.ShapeDtypeStruct(*o[:2]) for o in outs]

    def trimmed(*refs):
        results = refs[reads + len(extra):]
        if chain is not None:
            results[writes][...] = jnp.zeros((8, 128), F32)
            results = results[:writes] + results[writes + 1:]
        body(*refs[:reads], *results)

    results = pl.pallas_call(
        trimmed,
        out_shape=kernel_outs,
        grid=(1,),
        in_specs=[spec for _, spec in operands + extra],
        out_specs=[pl.BlockSpec(o.shape, lambda i, nd=len(o.shape): (0,) * nd) for o in out_shape],
        scratch_shapes=list(scratch),
        compiler_params=pltpu.CompilerParams(vmem_limit_bytes=mib * 2 ** 20),
        cost_estimate=pl.CostEstimate(flops=int(HINT * WEIGHT.get(name, 1)), bytes_accessed=1, transcendentals=0),
        name=name,
    )(*[array for array, _ in operands + extra])
    if chain is not None:
        chain.token = results[writes]
    return results[:writes]


def deal(where, chunk, order, keep, send, index, value):
    distance = jnp.bitwise_xor(where[0], chunk)
    spot = 0
    for bit in order[1:]:
        spot = spot * 2 + (jnp.bitwise_and(distance, bit) // bit)
    gone = jnp.bitwise_and(distance, order[0]) != 0

    @pl.when(gone)
    def _():
        send[(spot,) + index] = value

    @pl.when(jnp.logical_not(gone))
    def _():
        keep[(spot,) + index] = value


def halve_kernel(kept, came, keep, send):
    count = keep.shape[0]
    for i in range(count):
        keep[i] = (kept[i].astype(F32) + came[i].astype(F32)).astype(BF)
        send[i] = (kept[count + i].astype(F32) + came[count + i].astype(F32)).astype(BF)


def unit_of(resid):
    middle = jnp.mean(resid, -1, keepdims=True)
    center = resid - middle
    spread = jnp.mean(center * center, -1, keepdims=True)
    root = lax.rsqrt(spread + EPS)
    return center * root, root


def summed(near, came, part):
    half = near.shape[0] // 2
    here = near[pl.ds(part * half, half), :].astype(F32)
    return here + came[pl.ds((1 - part) * half, half), :].astype(F32)


def parts_of(rows):
    return [(part, pl.ds(part * (rows // 2), rows // 2)) for part in range(2)]


def at_row(vec, row):
    return vec[pl.ds(row, 1), :]


def project(layer, at, rows, weights, biases, kv_out, q_out):
    split = kv_out.shape[2]
    cols = pl.ds(0, split + q_out.shape[2])
    for g in range(2):
        acc = dot(rows, weights[g][:, cols]) + biases[g][pl.ds(layer, 1), cols]
        kv_out[g, at, :] = acc[:, :split].astype(BF)
        q_out[g, at, :] = (acc[:, split:].astype(BF) * SCALE).astype(BF)


def qkv_kernel(layer, rows, w_own, w_other, b_own, b_other, kv_out, q_out):
    for _, at in parts_of(rows.shape[0]):
        project(layer, at, rows[at, :], (w_own, w_other), (b_own, b_other), kv_out, q_out)


def norm_two_rows(layer, part, at, near, came, resid_one, vec, resid_out, out):
    unit, _ = unit_of(resid_one[at, :])
    hidden = unit * at_row(vec, layer + GAIN_ONE) + at_row(vec, layer + BIAS_ONE)
    resid = hidden + summed(near, came, part) + at_row(vec, layer + B_DOWN)
    resid_out[at, :] = resid
    unit, _ = unit_of(resid)
    out[at, :] = (unit * at_row(vec, layer + GAIN_TWO) + at_row(vec, layer + BIAS_TWO)).astype(BF)


def norm_two_kernel(layer, near, came, resid_one, vec, resid_out, out):
    for part, at in parts_of(out.shape[0]):
        norm_two_rows(layer, part, at, near, came, resid_one, vec, resid_out, out)


def norm_two_qkv_kernel(layer, near, came, resid_one, vec, w_own, w_other, b_own, b_other,
                        resid_out, out, kv_out, q_out):
    for part, at in parts_of(out.shape[0]):
        norm_two_rows(layer, part, at, near, came, resid_one, vec, resid_out, out)
        project(layer + 1, at, out[at, :], (w_own, w_other), (b_own, b_other), kv_out, q_out)


def choose_kernel(kv, kv_far, far, *outs):
    width = outs[0].shape[1]
    for g in range(2):
        for k in range(2):
            cols = pl.ds(k * width, width)
            outs[2 * g + k][...] = jnp.where(
                far[g, :, cols] > 0.5, kv_far[g, :, cols].astype(F32), kv[g, :, cols].astype(F32)).astype(BF)


def attend_kernel(*refs):
    q, out_own, out_other, near, mixed, lse, used = refs[:1] + refs[9:]
    pieces, crossed = refs[1:5], refs[5:9]
    _, length, width = q.shape
    heads = width // HEAD
    for g in range(2):
        for k in range(2):
            used[2 * g + k, pl.ds(0, length), :] = pieces[2 * g + k][...]
            used[2 * g + k, pl.ds(length, length), :] = crossed[2 * (1 - g) + k][...]
        for head in range(heads):
            cols = pl.ds(head * HEAD, HEAD)
            key, value = used[2 * g, :, cols], used[2 * g + 1, :, cols]
            scores = dot_nt(key, q[g, :, cols])
            high = jnp.max(scores, 0, keepdims=True)
            expo = jnp.exp(scores - high)
            total = jnp.sum(expo, 0, keepdims=True)
            lse[pl.ds(g * heads + head, 1), :] = high + jnp.log(total)
            probs = (expo * (1.0 / total)).astype(BF)
            mixed[g, :, cols] = dot_tn(probs, value).astype(BF)
    near[...] = (dot(mixed[0], out_own[...]) + dot(mixed[1], out_other[...])).astype(BF)


def feed_kernel(layer, near, came, inputs, vec, up_own, up_other, down_own, down_other, b_own, b_other,
                resid_out, hidden_out, act_out, slope_out, near_out):
    ups, downs, biases = (up_own, up_other), (down_own, down_other), (b_own, b_other)
    for part, at in parts_of(near.shape[0]):
        resid = inputs[at, :].astype(F32) + summed(near, came, part) + at_row(vec, layer + B_OUT)
        resid_out[at, :] = resid
        unit, _ = unit_of(resid)
        hidden_out[at, :] = (unit * at_row(vec, layer + GAIN_ONE) + at_row(vec, layer + BIAS_ONE)).astype(BF)
        branch = 0.0
        for g in range(2):
            u = dot(hidden_out[at, :], ups[g][...]) + biases[g][pl.ds(LAYERS + layer, 1), :]
            cdf = 0.5 * (1.0 + lax.erf(u * (0.5 ** 0.5)))
            density = jnp.exp(-0.5 * u * u) * ((2.0 * jnp.pi) ** -0.5)
            act = (u * cdf).astype(BF)
            act_out[g, at, :] = act
            slope_out[g, at, :] = (cdf + u * density).astype(BF)
            branch = branch + dot(act, downs[g][...])
        near_out[at, :] = branch.astype(BF)


def norm_back(grad, resid, gain):
    unit, root = unit_of(resid)
    scaled = grad * gain
    mean_e = jnp.mean(scaled, -1, keepdims=True)
    mean_en = jnp.mean(scaled * unit, -1, keepdims=True)
    pulled = root * (scaled - mean_e - unit * mean_en)
    return pulled, (jnp.sum(grad * unit, 0, keepdims=True), jnp.sum(grad, 0, keepdims=True),
                    jnp.sum(pulled, 0, keepdims=True))


def back_norm(grads, gain_row, resid, vec, full_out, short_out, sums_out):
    sums_out[...] = jnp.zeros(sums_out.shape, F32)
    for part, at in parts_of(resid.shape[0]):
        grad = grads[-1][at, :].astype(F32)
        if len(grads) > 1:
            grad = grad + summed(grads[0], grads[1], part)
        pulled, sums = norm_back(grad, resid[at, :], at_row(vec, gain_row))
        full_out[at, :] = pulled
        short_out[at, :] = pulled.astype(BF)
        for index, s in enumerate(sums):
            sums_out[pl.ds(index, 1), :] += s


def back_feed_kernel(layer, grads, *refs):
    resid, vec, up_own, up_other, down_own, down_other, slope = refs[grads:grads + 7]
    full_out, short_out, sums_out, pre_out, bias_out, near_out = refs[grads + 7:]
    back_norm(refs[:grads], layer + GAIN_TWO, resid, vec, full_out, short_out, sums_out)
    ups, downs = (up_own, up_other), (down_own, down_other)
    totals = [0.0, 0.0]
    for _, at in parts_of(resid.shape[0]):
        branch = 0.0
        for g in range(2):
            pre = (dot_nt(short_out[at, :], downs[g][...]) * slope[g, at, :].astype(F32)).astype(BF)
            pre_out[g, at, :] = pre
            totals[g] = totals[g] + jnp.sum(pre.astype(F32), 0, keepdims=True)
            branch = branch + dot_nt(pre, ups[g][...])
        near_out[at, :] = branch.astype(BF)
    for g in range(2):
        bias_out[g] = totals[g]


def back_attend_kernel(layer, *refs):
    grads, (resid, vec, out_own, out_other, q, used, lse) = refs[:3], refs[3:10]
    full_out, short_out, sums_out, dq_out, stay = refs[10:15]
    go = refs[15:19]
    back_norm(grads, layer + GAIN_ONE, resid, vec, full_out, short_out, sums_out)
    _, length, width = q.shape
    heads = width // HEAD
    for g in range(2):
        d_mixed_all = dot_nt(short_out[...], (out_own, out_other)[g][...]).astype(BF)
        for head in range(heads):
            cols = pl.ds(head * HEAD, HEAD)
            key, value = used[2 * g, :, cols], used[2 * g + 1, :, cols]
            query = q[g, :, cols]
            d_mixed = d_mixed_all[:, head * HEAD:(head + 1) * HEAD]
            probs = jnp.exp(dot_nt(key, query) - lse[pl.ds(g * heads + head, 1), :])
            d_probs = dot_nt(value, d_mixed)
            inner = jnp.sum(d_probs * probs, 0, keepdims=True)
            d_scores = (probs * (d_probs - inner)).astype(BF)
            d_value = dot(probs.astype(BF), d_mixed)
            d_key = dot(d_scores, query)
            dq_out[g, :, cols] = (dot_tn(d_scores, key) * SCALE).astype(BF)
            for k, grad in enumerate((d_key, d_value)):
                stay[g, :, pl.ds(k * width + head * HEAD, HEAD)] = grad[:length]
                go[2 * g + k][:, cols] = grad[length:].astype(BF)


def add_crossed_kernel(*refs):
    stay, out = refs[0], refs[-1]
    width = refs[1].shape[1]
    for g in range(2):
        for k in range(2):
            cols = pl.ds(k * width, width)
            out[g, :, cols] = (stay[g, :, cols] + refs[1 + 2 * (1 - g) + k][...].astype(F32)).astype(BF)


def back_qkv_kernel(dq, dkv, dkv_far, far, w_own, w_other, all_out, bias_out, *outs):
    split = dkv.shape[2]
    cols = pl.ds(0, all_out.shape[2])
    for g in range(2):
        all_out[g, :, pl.ds(0, split)] = jnp.where(
            far[g] > 0.5, dkv_far[g].astype(F32), dkv[g].astype(F32)).astype(BF)
        all_out[g, :, pl.ds(split, dq.shape[2])] = dq[g]
        bias_out[g] = jnp.sum(all_out[g].astype(F32), 0, keepdims=True)
    for part, at in parts_of(dq.shape[1]):
        branch = dot_nt(all_out[0, at, :], w_own[:, cols]) + dot_nt(all_out[1, at, :], w_other[:, cols])
        if len(outs) == 1:
            outs[0][at, :] = branch.astype(BF)
        else:
            outs[part][...] = branch.astype(outs[part].dtype)


def grad_feed_kernel(count, shares, *refs):
    here, away = refs[4 * count], refs[4 * count + 1:]
    feat = refs[0].shape[1]
    rows = feat // shares
    tile = feat // 2
    for g in range(2):
        for t in range(2):
            cols = pl.ds(t * tile, tile)
            up, down = 0.0, 0.0
            for m in range(count):
                hid, feed, pre, act = refs[4 * m:4 * m + 4]
                up = up + dot_tn(hid[:, cols], pre[g])
                down = down + dot_tn(act[g, :, cols], feed[...])
            for k, grad in enumerate((up, down)):
                if g == 0 or len(away) == 1:
                    (here, away[0])[g][k, cols, :] = grad.astype(BF)
                    continue
                for b in range(shares // 2):
                    away[t * (shares // 2) + b][k] = grad[b * rows:(b + 1) * rows].astype(BF)


def fold(block, width):
    return jnp.concatenate([block[:, c:c + width] for c in range(0, block.shape[1], width)], 0)


def unfold(block, rows):
    return jnp.concatenate([block[c:c + rows] for c in range(0, block.shape[0], rows)], 1)


def grad_attend_kernel(count, shares, vectors, *refs):
    smalls = refs[4 * count:4 * count + 2 * vectors]
    here, *away = refs[4 * count + 2 * vectors:]
    feat = refs[0].shape[1]
    split = refs[2].shape[2]
    width = split // 3
    rows, thin = feat // shares, width // shares
    stride = here.shape[0] // shares
    for g in range(2):
        acc, out = 0.0, 0.0
        for m in range(count):
            inputs, branch, d_qkv, mixed = refs[4 * m:4 * m + 4]
            acc = acc + dot_tn(inputs[...], d_qkv[g])
            out = out + dot_tn(mixed[g], branch[...])
        for b in range(shares):
            if g == 0 or len(away) == 1:
                ref, first = (here, away[0])[g], b * stride
            else:
                ref, first = away[b], 0
            at = pl.ds(first, rows)
            if vectors:
                ref[pl.ds(first + rows, stride - rows), :] = smalls[g][...].astype(BF)
            ref[at, pl.ds(0, split)] = acc[b * rows:(b + 1) * rows].astype(BF)
            ref[at, pl.ds(split, width)] = fold(out[b * thin:(b + 1) * thin, :], width).astype(BF)


def split_kernel(shares, order, feeds, attends, *refs):
    where, keep, send = refs[-3:]
    groups = [refs[1 + (1 + shares) * n - 1:(1 + shares) * (n + 1)] for n in range(feeds + attends)]
    for b in range(shares):
        spot = 0
        for here, *came in groups:
            rows = here.shape[-2] // shares
            for index in ((0,), (1,)) if len(here.shape) == 3 else ((),):
                mine = here[index + (pl.ds(b * rows, rows), slice(None))].astype(F32)
                value = mine + came[b][index + (slice(None), slice(None))].astype(F32)
                deal(where, b, order, keep, send, (spot,), value.astype(BF))
                spot += 1


def unfold_kernel(shares, *refs):
    for ref, out in zip(refs[:2], refs[2:]):
        width, feat = out.shape
        rows, thin = feat // shares, width // shares
        blocks = [unfold(ref[pl.ds(b * rows, rows), pl.ds(3 * width, width)].astype(F32), thin) for b in range(shares)]
        out[...] = jnp.concatenate(blocks, 0).astype(BF)


def pack_kernel(*refs):
    key, value, query, out = refs[:4]
    rows, width = key.shape
    payload = refs[-1]
    if len(refs) > 5:
        payload, small = refs[-2:]
    at = pl.ds(0, rows)
    for index, ref in enumerate((key, value, query)):
        payload[at, pl.ds(index * width, width)] = ref[...]
    payload[at, pl.ds(3 * width, width)] = fold(out[...].astype(F32), width).astype(BF)
    if len(refs) > 5:
        small[...] = jnp.zeros(small.shape, F32)
        for index, ref in enumerate(refs[4:-3]):
            small[pl.ds(LAYERS * index, LAYERS), pl.ds(0, ref.shape[1])] = ref[...].astype(F32)
        up = refs[-3]
        small[pl.ds(0, LAYERS), pl.ds(128, up.shape[1])] = up[...].astype(F32)
        payload[pl.ds(rows, small.shape[0]), :] = small[...].astype(BF)


def shares_kernel(key, value, query, out, up_early, down_early, up_late, down_late, early, late):
    early[0] = up_early[...]
    early[1] = down_early[...]
    pack_kernel(key, value, query, out, early.at[2])
    late[0] = up_late[...]
    late[1] = down_late[...]


def assemble_kernel(masks, per, up_per, *refs):
    count = len(masks)
    where = refs[2 * count]
    small_outs = len(refs) - 2 * count - 1 - 5 > 0
    if small_outs:
        spread, up_spread = refs[2 * count + 1:2 * count + 3]
        outs, (table, bias_own, bias_other), scratch = refs[2 * count + 3:-4], refs[-4:-1], refs[-1]
    else:
        outs, scratch = refs[2 * count + 1:-1], refs[-1]
    blk, grp = where[0], where[1]
    width, feat = outs[2].shape
    rows, thin = feat // count, width // count
    if small_outs:
        lane = lax.broadcasted_iota(jnp.int32, table.shape, 1)
        row = lax.broadcasted_iota(jnp.int32, table.shape, 0)
        six = 0.0
    for g in range(2):
        projection, hidden = 0.0, 0.0
        for index, mask in enumerate(masks):
            ref = refs[g * count + index]
            b = jnp.bitwise_xor(blk, mask)
            outs[g][pl.ds(pl.multiple_of(b * rows, rows), rows), :] = ref[pl.ds(0, rows), pl.ds(0, 3 * width)]
            block = ref[pl.ds(0, rows), pl.ds(3 * width, width)].astype(F32)
            scratch[pl.ds(pl.multiple_of(b * thin, thin), thin), :] = unfold(block, thin)
            if not small_outs:
                continue
            small = ref[pl.ds(rows, table.shape[0]), :]
            spreaded = dot(small[:, :per], spread[...])
            at = lane - (jnp.bitwise_xor(grp, g) * count + b) * per
            six = six + jnp.where((at >= 0) & (at < per), spreaded, 0.0)
            at = lane - b * per - jnp.where(row < LAYERS, 2 * width, width)
            projection = projection + jnp.where((at >= 0) & (at < per), spreaded, 0.0)
            at = lane - b * up_per
            hidden = hidden + jnp.where((at >= 0) & (at < up_per), dot(small[:, 128:128 + up_per], up_spread[...]), 0.0)
        outs[2 + g][...] = scratch[...].astype(BF)
        if small_outs:
            bias = (bias_own, bias_other)[g]
            bias[...] = jnp.zeros(bias.shape, F32)
            bias[pl.ds(0, LAYERS), :] = projection[:LAYERS] + projection[LAYERS:2 * LAYERS]
            bias[pl.ds(LAYERS, LAYERS), :] = hidden[:LAYERS]
    if small_outs:
        table[...] = six.astype(BF)


def small_kernel(layers, *refs):
    out, other = refs[-2:]
    out[...] = jnp.zeros(out.shape, F32)
    other[...] = jnp.zeros(other.shape, F32)
    per_layer = (len(refs) - 2) // layers
    for layer in range(layers):
        mine = refs[layer * per_layer:(layer + 1) * per_layer]
        sets = [mine[i:i + 4] for i in range(0, per_layer, 4)]
        base = 8 * layer
        for row, (which, index) in enumerate(((1, 2), (1, 0), (1, 1), (0, 2), (0, 0), (0, 1))):
            total = sum(s[which][pl.ds(index, 1), :] for s in sets)
            out[pl.ds(base + row, 1), :] = total
            other[pl.ds(base + row, 1), :] = total
        cols = pl.ds(0, sets[0][3].shape[2])
        for g, ref in enumerate((out, other)):
            ref[pl.ds(base + 6, 1), :] = sum(s[2][g] for s in sets)
            ref[pl.ds(base + 7, 1), cols] = sum(s[3][g] for s in sets)


def bits_of(count):
    return list(range(count.bit_length() - 1))


class Gather:
    def __init__(self, share):
        self.pieces = {0: share}

    def step(self, bits, after):
        held = dict(self.pieces)
        for mask, piece in held.items():
            if after is not None:
                piece, _ = lax.optimization_barrier((piece, after))
            for bit in bits:
                self.pieces[mask | bit] = send_xor(piece, "blk", bit)

    def over_y(self, masks):
        for mask in masks:
            self.pieces[mask | 1] = send_xor(self.pieces[mask], "blk", 1)

    def both(self, after):
        masks = sorted(self.pieces)
        own = [self.pieces[m] for m in masks]
        if after is not None:
            ready = [lax.optimization_barrier((piece, after))[0] for piece in own]
        else:
            ready = own
        return masks, own + [send_xor(piece, "grp", 1) for piece in ready]


class Scatter:
    def __init__(self, keep, send, order):
        self.keep = keep
        self.came = send_xor(send, "blk", order[0])
        self.order = order[1:]

    def halve(self, chain):
        shape = (self.keep.shape[0] // 2,) + self.keep.shape[1:]
        self.keep, send = run(halve_kernel, [self.keep, self.came], [(shape, BF)] * 2, "halve", chain=chain)
        self.came = send_xor(send, "blk", self.order[0])
        self.order = self.order[1:]

    def total(self):
        return self.keep[0].astype(F32) + self.came[0].astype(F32)


def sum_axis(block, axis, masks):
    for mask in masks:
        block = block + send_xor(block, axis, mask)
    return block


def fold_share(block, width):
    rows = block.shape[0]
    return jnp.moveaxis(block.reshape(rows, -1, width), 1, 0).reshape(-1, width)


def unfold_shares(columns, shares, feat):
    width = columns.shape[1]
    blocks = columns.reshape(shares, feat // width, -1, width)
    return jnp.moveaxis(blocks, 1, 2).reshape(-1, feat)


def stream(rows, grad_rows, shape, hid, weights, chain, result):
    half, feat = shape
    width = feat // 4
    lse_rows = -(-(2 * width // HEAD) // 8) * 8

    def stage(body, operands, outs, name):
        return run(body, operands, outs, name, chain=chain)

    def over_x(near):
        return [near, send_xor(near, "grp", 2)]

    def over_core(pieces):
        return [send_xor(piece, "grp", 1) for piece in pieces]

    wide, short = ((half, feat), F32), ((half, feat), BF)
    projected = [((2, half, 2 * width), BF), saved(((2, half, width), BF))]
    pieces = 4 * [((half, width), BF)]
    hidden_shape = saved(((2, half, hid), BF))
    sums_shape = ((8, feat), F32)
    kept = []
    for layer in range(LAYERS):
        w = weights[layer]
        if layer == 0:
            kv, q = stage(lambda *r: qkv_kernel(layer, *r), [rows, *w["qkv"], *w["bias"]], projected, "qkv")
        kv_far = send_xor(kv, "blk", 1)
        yield "qkv", layer
        chosen = list(stage(lambda *r: choose_kernel(*r[:3], *r[4:]), [kv, kv_far, w["far"], w["vec"]], pieces, "choose"))
        chosen += over_core(chosen)
        near, mixed, lse, used = stage(
            attend_kernel, [q] + chosen + [*w["out"]],
            [short, saved(((2, half, width), BF)), saved(((lse_rows, half), F32)),
             saved(((4, 2 * half, width), BF))], "attend")
        branch = over_x(near)
        yield "attend", layer
        resid_one, hidden, act, slope, near = stage(
            lambda *r: feed_kernel(layer, *r),
            branch + [rows, w["vec"]] + [in_hbm(b) for b in w["up"] + w["down"]] + [*w["bias"]],
            [saved(wide), saved(short), hidden_shape, hidden_shape, short], "feed")
        branch = over_x(near)
        yield "feed", layer
        before = (rows, q, used, lse, mixed, resid_one, hidden, act, slope)
        if layer < LAYERS - 1:
            after = weights[layer + 1]
            resid_two, rows, kv, q = stage(
                lambda *r: norm_two_qkv_kernel(layer, *r),
                branch + [resid_one, w["vec"], *after["qkv"], *after["bias"]],
                [saved(wide), saved(short)] + projected, "norm_two_qkv")
        else:
            resid_two, rows = stage(lambda *r: norm_two_kernel(layer, *r), branch + [resid_one, w["vec"]],
                                    [wide, short], "norm_two")
        result["outputs"].append(rows[:half // 2])
        kept.append(before + (resid_two,))

    grads = [grad_rows]
    for layer in reversed(range(LAYERS)):
        w = weights[layer]
        rows, q, used, lse, mixed, resid_one, hidden, act, slope, resid_two = kept[layer]
        d_two, feed, sums_two, d_pre, g_up, near = stage(
            lambda *r: back_feed_kernel(layer, len(grads), *r),
            grads + [resid_two, w["vec"], *w["up"], *w["down"], slope],
            [wide, saved(short), saved(sums_shape), hidden_shape, saved(((2, 1, hid), F32)), short], "back_feed")
        result["feed"][layer] = [hidden, feed, d_pre, act]
        branch = over_x(near)
        yield "back_feed", layer
        d_one, branch, sums_one, dq, stay, *go = stage(
            lambda *r: back_attend_kernel(layer, *r),
            branch + [d_two, resid_one, w["vec"], *w["out"], q, used, lse],
            [wide, saved(short), saved(sums_shape), ((2, half, width), BF), ((2, half, 2 * width), F32)] + pieces, "back_attend")
        dkv, = stage(add_crossed_kernel, [stay] + over_core(go), [((2, half, 2 * width), BF)], "add_crossed")
        dkv_far = send_xor(dkv, "blk", 1)
        yield "back_attend", layer
        outs = [short] if layer else [((half // 2, feat), F32), ((half // 2, feat), BF)]
        d_qkv, g_qkv, *outs = stage(
            back_qkv_kernel, [dq, dkv, dkv_far, w["far"], *w["qkv"]],
            [saved(((2, half, 3 * width), BF)), saved(((2, 1, 3 * width), F32))] + outs, "back_qkv")
        result["attend"][layer] = [rows, branch, d_qkv, mixed]
        result["smalls"][layer] = [sums_two, sums_one, g_up, g_qkv]
        if layer:
            grads = over_x(outs[0]) + [d_one]
        else:
            came = send_xor(outs[1], "grp", 2)
            result["grad"] = d_one[:half // 2] + outs[0] + came.astype(F32)
        yield "back_qkv", layer


def per_device(layer_input, w_query, w_key, w_value, b_query, b_value, w_out, b_out, gain_one,
               bias_one, w_up, b_up, w_down, b_down, gain_two, bias_two, head_table, grad_top):
    blk_count = lax.axis_size("blk")
    grp_count = lax.axis_size("grp")
    grp = lax.axis_index("grp")
    blk = lax.axis_index("blk")
    feat = w_out.shape[2]
    share_rows = w_query.shape[1]
    width = w_query.shape[2]
    heads = width // HEAD
    hid = w_up.shape[2]
    per = b_out.shape[1]
    up_per = b_up.shape[1]
    blk_masks = [1 << bit for bit in bits_of(blk_count)[::-1]]
    packed = blk_count == 8 and share_rows % 32 == 0 and per % 8 == 0
    block_own = blk % NB
    target = jnp.where(block_own == 0, head_table[:, :, 0], head_table[:, :, 1])
    far = (target != block_own).astype(F32)
    far = jnp.stack([lax.dynamic_slice_in_dim(far, g * heads, heads, 1) for g in (grp, grp ^ 1)], 1)
    far_cols = jnp.broadcast_to(far[:, :, None, :, None], (LAYERS, 2, 2, heads, HEAD)).reshape(LAYERS, 2, 1, 2 * width)

    start = layer_input[:, 0]
    row_top = jnp.concatenate([start, send_xor(start, "grp", 2)], 1)
    grad_start = grad_top[:, 0]
    grad_rows = jnp.concatenate([grad_start, send_xor(grad_start, "grp", 2)], 1)

    micros = range(layer_input.shape[0])
    count = len(micros)
    chain = Order()
    results = [{"outputs": [], "feed": {}, "attend": {}, "smalls": {}} for _ in micros]
    weights = [{"far": pick(far_cols, layer)} for layer in range(LAYERS)]
    where = (jnp.stack([blk, grp]).astype(jnp.int32), pl.BlockSpec((2,), lambda i: (0,), memory_space=pltpu.SMEM))
    grad_feed, grad_attend, tiny = {}, {}, []
    smalls = [b_query, b_value, b_out, gain_one, bias_one, b_down, gain_two, bias_two]
    small_rows = len(smalls) * LAYERS
    vec_shape = (small_rows, feat)

    def factors(name, layer):
        return [f for r in results for f in r[name][layer]]

    chunks = blk_count if packed else 1

    def sum_feed(layer):
        rest = [((2, feat // chunks, hid), BF)] * chunks
        grad_feed[layer] = run(lambda *r: grad_feed_kernel(count, chunks, *r), factors("feed", layer),
                               [((2, feat, hid), BF)] + rest, "grad_feed", 16, chain=chain)

    def sum_attend(layer):
        vectors = tiny if packed and layer == 0 else []
        high = feat + (len(vectors) // 2) * blk_count * 8 * LAYERS
        rest = [((high // chunks, feat), BF)] * chunks
        grad_attend[layer] = run(lambda *r: grad_attend_kernel(count, blk_count, len(vectors) // 2, *r),
                                 factors("attend", layer) + vectors, [((high, feat), BF)] + rest, "grad_attend", 16,
                                 chain=chain)

    def add_small():
        sums = sum([r["smalls"][layer] for layer in range(LAYERS) for r in results], [])
        tiny.extend(run(lambda *r: small_kernel(LAYERS, *r), sums, [((8 * LAYERS, feat), F32)] * 2, "small",
                        chain=chain))

    if packed:
        def pack(layer, *more, scratch=(), order=None):
            rows = share_rows + (small_rows if more else 0)
            return run(pack_kernel, [pick(a, layer) for a in (w_key, w_value, w_query, w_out)] + list(more),
                       [((rows, feat), BF)], "pack", 60, scratch, order)[0]

        first = Gather(pack(0, *smalls, b_up, scratch=[pltpu.VMEM(vec_shape, F32)]))
        first.step([1, 2, 4, 6], None)
        first.over_y([2, 4, 6])
        early, late = run(
            shares_kernel, [pick(a, 1) for a in (w_key, w_value, w_query, w_out)]
            + [pick(a, layer) for layer in range(LAYERS) for a in (w_up, w_down)],
            [((3, share_rows, feat), BF), ((2, share_rows, feat), BF)], "shares", 60)
        gathered = {"early": lax.all_gather(early, "blk", axis=1, tiled=True)}
        lanes = jnp.arange(feat)[None, :]
        spread = (lanes % per == jnp.arange(per)[:, None]).astype(BF)
        up_spread = (lanes % up_per == jnp.arange(up_per)[:, None]).astype(BF)

        def start_feed():
            block = lax.optimization_barrier((late, chain.token))[0]
            gathered["late"] = lax.all_gather(block, "blk", axis=1, tiled=True)

        def over_cores(name):
            block = gathered[name]
            return [block, send_xor(lax.optimization_barrier((block, chain.token))[0], "grp", 1)]

        def have_early():
            both = over_cores("early")
            outs = run(lambda *r: unfold_kernel(blk_count, *r), [pick(b, 2) for b in both], [((width, feat), BF)] * 2,
                       "unfold")
            weights[0].update(up=[pick(b, 0) for b in both], down=[pick(b, 1) for b in both])
            weights[1].update(qkv=[pick(b, 2) for b in both], out=outs)

        def have_late():
            both = over_cores("late")
            weights[1].update(up=[pick(b, 0) for b in both], down=[pick(b, 1) for b in both])

        sums_of = {}

        def scatter(key, grads, part=None):
            here, *away = grads
            came = [send_xor(piece, "grp", 1) for piece in away]
            if part is not None:
                groups, depth = [pick(a, part) for a in [here] + came], 1
            else:
                groups, depth = [here] + came, 2 if here.ndim == 3 else 1
            outs = [((blk_count // 2, depth, here.shape[-2] // blk_count, feat), BF)] * 2
            keep, send = run(lambda *r: split_kernel(blk_count, ORDERS[key], 1, 0, *r), groups + [where], outs, "split",
                             16, chain=chain)
            sums_of[key] = Scatter(keep, send, ORDERS[key])

        steps = {
            "A": lambda: sum_feed(1), "B": lambda: scatter("A", grad_feed[1]),
            "C": lambda: sum_attend(1), "D": lambda: scatter("C", grad_attend[1]),
            "a": lambda: sum_feed(0), "b": lambda: scatter("a", grad_feed[0], 0), "e": lambda: scatter("e", grad_feed[0], 1),
            "c": lambda: sum_attend(0), "d": lambda: scatter("c", grad_attend[0]), "m": add_small,
        }
        for letter, key in zip("FGfhg", "ACaec"):
            steps[letter] = lambda key=key: sums_of[key].halve(chain)

        masks, pieces = first.both(None)
        outs = run(lambda *r: assemble_kernel(masks, per, up_per, *r), pieces + [where, spread, up_spread],
                   [((feat, 3 * width), BF)] * 2 + [((width, feat), BF)] * 2 + [(vec_shape, BF)] + [((8, feat), F32)] * 2,
                   "assemble", scratch=[pltpu.VMEM((width, feat), F32)], chain=chain)
        weights[0].update(qkv=outs[:2], out=outs[2:4])
        table, *biases = outs[4:]
        vec = table + send_xor(table, "grp", 2)
        after = {
            ("attend", 0, 1): lambda: (have_early(), start_feed()),
            ("attend", 1, 1): have_late,
        }
    else:
        table = jnp.zeros(vec_shape, BF)
        rows = jnp.stack(smalls).reshape(small_rows, per)
        table = lax.dynamic_update_slice(table, rows, (0, (grp * blk_count + blk) * per))
        spots = jnp.zeros((8, feat), BF)
        spots = lax.dynamic_update_slice(spots, b_query, (0, 2 * width + blk * per))
        spots = lax.dynamic_update_slice(spots, b_value, (LAYERS, width + blk * per))
        spots = lax.dynamic_update_slice(spots, b_up, (2 * LAYERS, blk * up_per))
        table = sum_axis(table, "blk", blk_masks)
        spots = sum_axis(spots, "blk", blk_masks).astype(F32)
        bias = jnp.zeros((8, feat), F32)
        bias = bias.at[:LAYERS].set(spots[:LAYERS] + spots[LAYERS:2 * LAYERS])
        bias = bias.at[LAYERS:2 * LAYERS].set(spots[2 * LAYERS:3 * LAYERS])
        for layer in range(LAYERS):
            block = jnp.concatenate([w_key[layer], w_value[layer], w_query[layer],
                                     fold_share(w_out[layer], width)], 1)
            block = lax.all_gather(block, "blk", axis=0, tiled=True)
            pair = [block, send_xor(block, "grp", 1)]
            block = lax.all_gather(jnp.stack([w_up[layer], w_down[layer]]), "blk", axis=1, tiled=True)
            both = [block, send_xor(block, "grp", 1)]
            weights[layer].update(qkv=[b[:, :3 * width] for b in pair],
                                  out=[unfold_shares(b[:, 3 * width:], blk_count, feat) for b in pair],
                                  up=[pick(b, 0) for b in both], down=[pick(b, 1) for b in both])
        biases = [bias, send_xor(bias, "grp", 1)]
        vec = sum_axis(table, "grp", [2, 1])
        after = {}
        for layer in range(LAYERS):
            after["back_feed", layer, count - 1] = lambda layer=layer: sum_feed(layer)
            after["back_qkv", layer, count - 1] = lambda layer=layer: sum_attend(layer)

    vec = vec.astype(F32)
    for w in weights:
        w.update(vec=vec, bias=biases)
    streams = [stream(pick(row_top, m), pick(grad_rows, m), row_top.shape[1:], hid, weights, chain, results[m])
               for m in micros]
    done = False
    while not done:
        for m, one in enumerate(streams):
            label = next(one, None)
            done = label is None
            if not done and label + (m,) in after:
                after[label + (m,)]()
            if not done and packed:
                for letter in SLOTS.get(label + (m,), ""):
                    steps[letter]()
    if packed:
        late, up, down, attend, attend1 = [sums_of[key].total() for key in "AaecC"]
        grad_feed = {0: jnp.concatenate([up, down]), 1: late}
        grad_attend = {0: attend[0, :share_rows], 1: attend1[0]}
    else:
        for dim, sums in ((1, grad_feed), (0, grad_attend)):
            for layer in sums:
                block = sums[layer][0] + send_xor(sums[layer][1], "grp", 1)
                sums[layer] = lax.psum_scatter(block, "blk", scatter_dimension=dim, tiled=True).astype(F32)

    if packed:
        tiny = attend[0, share_rows:]
    else:
        add_small()
        tiny = sum_axis(tiny[0] + send_xor(tiny[1], "grp", 1), "blk", blk_masks)
    tiny = tiny.reshape(LAYERS, 8, feat)
    six = tiny[:, :SMALLS]
    six = lax.dynamic_slice_in_dim(six, (grp * blk_count + blk) * per, per, 2)
    g_b_up = lax.dynamic_slice_in_dim(tiny[:, 6], blk * up_per, up_per, 1)
    g_b_value = lax.dynamic_slice_in_dim(tiny[:, 7], width + blk * per, per, 1)
    g_b_query = lax.dynamic_slice_in_dim(tiny[:, 7], 2 * width + blk * per, per, 1)
    feeds = jnp.stack([grad_feed[layer] for layer in range(LAYERS)])
    attends = jnp.stack([grad_attend[layer] for layer in range(LAYERS)])
    g_out = jnp.stack([unfold_shares(attends[layer, :, 3 * width:], 1, feat) for layer in range(LAYERS)])
    return (
        jnp.stack([jnp.stack([r["outputs"][layer] for r in results]) for layer in range(LAYERS)])[:, :, None],
        jnp.stack([r["grad"] for r in results])[:, None],
        attends[:, :, 2 * width:3 * width],
        attends[:, :, :width],
        attends[:, :, width:2 * width],
        g_b_query,
        g_b_value,
        g_out,
        six[:, 0],
        six[:, 1],
        six[:, 2],
        feeds[:, 0],
        g_b_up,
        feeds[:, 1],
        six[:, 3],
        six[:, 4],
        six[:, 5],
    )


def solution(mesh):
    rows = P(None, "blk", "grp", None)
    cols = P(None, "blk", "grp")
    both = P(None, ("grp", "blk"))
    tall = P(None, ("grp", "blk"), None)
    return jax.shard_map(
        per_device,
        mesh=mesh,
        in_specs=(rows, cols, cols, cols, both, both, tall, both, both, both, cols, both, tall,
                  both, both, both, P(), rows),
        out_specs=(P(None, None, "blk", "grp", None), rows, cols, cols, cols, both, both, tall,
                   both, both, both, cols, both, tall, both, both, both),
        check_vma=False,
    )
```

```python
import jax
import jax.numpy as jnp
from jax import lax
from jax.experimental import pallas as pl
from jax.experimental.pallas import tpu as pltpu
from jax.sharding import PartitionSpec as P

HEAD = 64
NB = 2
LAYERS = 2
EPS = 1e-05
SCALE = HEAD ** -0.5
BF = jnp.bfloat16
F32 = jnp.float32
SMALLS = 6
HINT = 200000000
SLOTS = {
    ("back_feed", 1, 1): "A", ("back_qkv", 1, 0): "B", ("back_feed", 0, 0): "C", ("back_feed", 0, 1): "FD",
    ("back_attend", 0, 1): "a", ("back_qkv", 0, 0): "GF", ("back_qkv", 0, 1): "mcdbeghfGghf",
}
ORDERS = {"A": [2, 4, 1], "C": [2, 4, 1], "a": [1, 2, 4], "e": [2, 4, 1], "c": [1, 2, 4]}
KEEP = True
WEIGHTS = True
WEIGHT = {"qkv": .9, "choose": .5, "attend": 2.5, "feed": 2.6, "norm_two_qkv": 1.6, "norm_two": .6, "back_feed": 3.6,
          "back_attend": 5, "add_crossed": .6, "back_qkv": 1.2, "grad_feed": 5.5, "grad_attend": 3.7, "split": 1.8,
          "halve": .8, "assemble": 1.8, "place": 2, "pack": 1.2, "small": .8}
B_OUT, GAIN_ONE, BIAS_ONE, B_DOWN, GAIN_TWO, BIAS_TWO = [LAYERS * (2 + i) for i in range(SMALLS)]


def send_xor(block, axis, mask):
    count = lax.axis_size(axis)
    return lax.ppermute(block, axis, [(i, i ^ mask) for i in range(count)])


def dot(left, right):
    return lax.dot_general(left, right, (((1,), (0,)), ((), ())), preferred_element_type=F32)


def dot_tn(left, right):
    return lax.dot_general(left, right, (((0,), (0,)), ((), ())), preferred_element_type=F32)


def dot_nt(left, right):
    return lax.dot_general(left, right, (((1,), (1,)), ((), ())), preferred_element_type=F32)


def pick(array, index):
    tail = array.shape[1:]
    return array, pl.BlockSpec((None,) + tail, lambda i: (index,) + (0,) * len(tail))


def saved(out):
    return out + ("saved",)


def in_hbm(operand):
    array, spec = operand if isinstance(operand, tuple) else whole(operand)
    return (pltpu.with_memory_space_constraint(array, pltpu.HBM) if WEIGHTS else array), spec


def whole(array):
    return array, pl.BlockSpec(array.shape, lambda i: (0,) * array.ndim)


class Order:
    token = None
    on = True


def run(body, operands, outs, name, mib=16, scratch=(), chain=None):
    operands = [o if isinstance(o, tuple) else whole(o) for o in operands]
    reads = len(operands)
    outs = list(outs)
    writes = len(outs)
    extra = []
    if chain is not None and chain.token is not None:
        extra = [(chain.token, pl.BlockSpec(memory_space=pl.ANY))]
    if chain is not None and not chain.on:
        chain = None
    if chain is not None:
        outs.append(((8, 128), F32))
    kernel_outs = [pltpu.HBM(*o[:2]) if len(o) > 2 and KEEP else jax.ShapeDtypeStruct(*o[:2]) for o in outs]
    out_shape = [jax.ShapeDtypeStruct(*o[:2]) for o in outs]

    def trimmed(*refs):
        results = refs[reads + len(extra):]
        if chain is not None:
            results[writes][...] = jnp.zeros((8, 128), F32)
            results = results[:writes] + results[writes + 1:]
        body(*refs[:reads], *results)

    results = pl.pallas_call(
        trimmed,
        out_shape=kernel_outs,
        grid=(1,),
        in_specs=[spec for _, spec in operands + extra],
        out_specs=[pl.BlockSpec(o.shape, lambda i, nd=len(o.shape): (0,) * nd) for o in out_shape],
        scratch_shapes=list(scratch),
        compiler_params=pltpu.CompilerParams(vmem_limit_bytes=mib * 2 ** 20),
        cost_estimate=pl.CostEstimate(flops=int(HINT * WEIGHT.get(name, 1)), bytes_accessed=1, transcendentals=0),
        name=name,
    )(*[array for array, _ in operands + extra])
    if chain is not None:
        chain.token = results[writes]
    return results[:writes]


def deal(where, chunk, order, keep, send, index, value):
    distance = jnp.bitwise_xor(where[0], chunk)
    spot = 0
    for bit in order[1:]:
        spot = spot * 2 + (jnp.bitwise_and(distance, bit) // bit)
    gone = jnp.bitwise_and(distance, order[0]) != 0

    @pl.when(gone)
    def _():
        send[(spot,) + index] = value

    @pl.when(jnp.logical_not(gone))
    def _():
        keep[(spot,) + index] = value


def halve_kernel(kept, came, keep, send):
    count = keep.shape[0]
    for i in range(count):
        keep[i] = (kept[i].astype(F32) + came[i].astype(F32)).astype(BF)
        send[i] = (kept[count + i].astype(F32) + came[count + i].astype(F32)).astype(BF)


def unit_of(resid):
    middle = jnp.mean(resid, -1, keepdims=True)
    center = resid - middle
    spread = jnp.mean(center * center, -1, keepdims=True)
    root = lax.rsqrt(spread + EPS)
    return center * root, root


def summed(near, came, part):
    half = near.shape[0] // 2
    here = near[pl.ds(part * half, half), :].astype(F32)
    return here + came[pl.ds((1 - part) * half, half), :].astype(F32)


def parts_of(rows):
    return [(part, pl.ds(part * (rows // 2), rows // 2)) for part in range(2)]


def at_row(vec, row):
    return vec[pl.ds(row, 1), :]


def project(layer, at, rows, weights, biases, kv_out, q_out):
    split = kv_out.shape[2]
    cols = pl.ds(0, split + q_out.shape[2])
    for g in range(2):
        acc = dot(rows, weights[g][:, cols]) + biases[g][pl.ds(layer, 1), cols]
        kv_out[g, at, :] = acc[:, :split].astype(BF)
        q_out[g, at, :] = (acc[:, split:].astype(BF) * SCALE).astype(BF)


def qkv_kernel(layer, rows, w_own, w_other, b_own, b_other, kv_out, q_out):
    for _, at in parts_of(rows.shape[0]):
        project(layer, at, rows[at, :], (w_own, w_other), (b_own, b_other), kv_out, q_out)


def norm_two_rows(layer, part, at, near, came, resid_one, vec, resid_out, out):
    unit, _ = unit_of(resid_one[at, :])
    hidden = unit * at_row(vec, layer + GAIN_ONE) + at_row(vec, layer + BIAS_ONE)
    resid = hidden + summed(near, came, part) + at_row(vec, layer + B_DOWN)
    resid_out[at, :] = resid
    unit, _ = unit_of(resid)
    out[at, :] = (unit * at_row(vec, layer + GAIN_TWO) + at_row(vec, layer + BIAS_TWO)).astype(BF)


def norm_two_kernel(layer, near, came, resid_one, vec, resid_out, out):
    for part, at in parts_of(out.shape[0]):
        norm_two_rows(layer, part, at, near, came, resid_one, vec, resid_out, out)


def norm_two_qkv_kernel(layer, near, came, resid_one, vec, w_own, w_other, b_own, b_other,
                        resid_out, out, kv_out, q_out):
    for part, at in parts_of(out.shape[0]):
        norm_two_rows(layer, part, at, near, came, resid_one, vec, resid_out, out)
        project(layer + 1, at, out[at, :], (w_own, w_other), (b_own, b_other), kv_out, q_out)


def choose_kernel(kv, kv_far, far, *outs):
    width = outs[0].shape[1]
    for g in range(2):
        for k in range(2):
            cols = pl.ds(k * width, width)
            outs[2 * g + k][...] = jnp.where(
                far[g, :, cols] > 0.5, kv_far[g, :, cols].astype(F32), kv[g, :, cols].astype(F32)).astype(BF)


def attend_kernel(*refs):
    q, out_own, out_other, near, mixed, lse, used = refs[:1] + refs[9:]
    pieces, crossed = refs[1:5], refs[5:9]
    _, length, width = q.shape
    heads = width // HEAD
    for g in range(2):
        for k in range(2):
            used[2 * g + k, pl.ds(0, length), :] = pieces[2 * g + k][...]
            used[2 * g + k, pl.ds(length, length), :] = crossed[2 * (1 - g) + k][...]
        for head in range(heads):
            cols = pl.ds(head * HEAD, HEAD)
            key, value = used[2 * g, :, cols], used[2 * g + 1, :, cols]
            scores = dot_nt(key, q[g, :, cols])
            high = jnp.max(scores, 0, keepdims=True)
            expo = jnp.exp(scores - high)
            total = jnp.sum(expo, 0, keepdims=True)
            lse[pl.ds(g * heads + head, 1), :] = high + jnp.log(total)
            probs = (expo * (1.0 / total)).astype(BF)
            mixed[g, :, cols] = dot_tn(probs, value).astype(BF)
    near[...] = (dot(mixed[0], out_own[...]) + dot(mixed[1], out_other[...])).astype(BF)


def feed_kernel(layer, near, came, inputs, vec, up_own, up_other, down_own, down_other, b_own, b_other,
                resid_out, hidden_out, act_out, slope_out, near_out):
    ups, downs, biases = (up_own, up_other), (down_own, down_other), (b_own, b_other)
    for part, at in parts_of(near.shape[0]):
        resid = inputs[at, :].astype(F32) + summed(near, came, part) + at_row(vec, layer + B_OUT)
        resid_out[at, :] = resid
        unit, _ = unit_of(resid)
        hidden_out[at, :] = (unit * at_row(vec, layer + GAIN_ONE) + at_row(vec, layer + BIAS_ONE)).astype(BF)
        branch = 0.0
        for g in range(2):
            u = dot(hidden_out[at, :], ups[g][...]) + biases[g][pl.ds(LAYERS + layer, 1), :]
            cdf = 0.5 * (1.0 + lax.erf(u * (0.5 ** 0.5)))
            density = jnp.exp(-0.5 * u * u) * ((2.0 * jnp.pi) ** -0.5)
            act = (u * cdf).astype(BF)
            act_out[g, at, :] = act
            slope_out[g, at, :] = (cdf + u * density).astype(BF)
            branch = branch + dot(act, downs[g][...])
        near_out[at, :] = branch.astype(BF)


def norm_back(grad, resid, gain):
    unit, root = unit_of(resid)
    scaled = grad * gain
    mean_e = jnp.mean(scaled, -1, keepdims=True)
    mean_en = jnp.mean(scaled * unit, -1, keepdims=True)
    pulled = root * (scaled - mean_e - unit * mean_en)
    return pulled, (jnp.sum(grad * unit, 0, keepdims=True), jnp.sum(grad, 0, keepdims=True),
                    jnp.sum(pulled, 0, keepdims=True))


def back_norm(grads, gain_row, resid, vec, full_out, short_out, sums_out):
    sums_out[...] = jnp.zeros(sums_out.shape, F32)
    for part, at in parts_of(resid.shape[0]):
        grad = grads[-1][at, :].astype(F32)
        if len(grads) > 1:
            grad = grad + summed(grads[0], grads[1], part)
        pulled, sums = norm_back(grad, resid[at, :], at_row(vec, gain_row))
        full_out[at, :] = pulled
        short_out[at, :] = pulled.astype(BF)
        for index, s in enumerate(sums):
            sums_out[pl.ds(index, 1), :] += s


def back_feed_kernel(layer, grads, *refs):
    resid, vec, up_own, up_other, down_own, down_other, slope = refs[grads:grads + 7]
    full_out, short_out, sums_out, pre_out, bias_out, near_out = refs[grads + 7:]
    back_norm(refs[:grads], layer + GAIN_TWO, resid, vec, full_out, short_out, sums_out)
    ups, downs = (up_own, up_other), (down_own, down_other)
    totals = [0.0, 0.0]
    for _, at in parts_of(resid.shape[0]):
        branch = 0.0
        for g in range(2):
            pre = (dot_nt(short_out[at, :], downs[g][...]) * slope[g, at, :].astype(F32)).astype(BF)
            pre_out[g, at, :] = pre
            totals[g] = totals[g] + jnp.sum(pre.astype(F32), 0, keepdims=True)
            branch = branch + dot_nt(pre, ups[g][...])
        near_out[at, :] = branch.astype(BF)
    for g in range(2):
        bias_out[g] = totals[g]


def back_attend_kernel(layer, *refs):
    grads, (resid, vec, out_own, out_other, q, used, lse) = refs[:3], refs[3:10]
    full_out, short_out, sums_out, dq_out, stay = refs[10:15]
    go = refs[15:19]
    back_norm(grads, layer + GAIN_ONE, resid, vec, full_out, short_out, sums_out)
    _, length, width = q.shape
    heads = width // HEAD
    for g in range(2):
        d_mixed_all = dot_nt(short_out[...], (out_own, out_other)[g][...]).astype(BF)
        for head in range(heads):
            cols = pl.ds(head * HEAD, HEAD)
            key, value = used[2 * g, :, cols], used[2 * g + 1, :, cols]
            query = q[g, :, cols]
            d_mixed = d_mixed_all[:, head * HEAD:(head + 1) * HEAD]
            probs = jnp.exp(dot_nt(key, query) - lse[pl.ds(g * heads + head, 1), :])
            d_probs = dot_nt(value, d_mixed)
            inner = jnp.sum(d_probs * probs, 0, keepdims=True)
            d_scores = (probs * (d_probs - inner)).astype(BF)
            d_value = dot(probs.astype(BF), d_mixed)
            d_key = dot(d_scores, query)
            dq_out[g, :, cols] = (dot_tn(d_scores, key) * SCALE).astype(BF)
            for k, grad in enumerate((d_key, d_value)):
                stay[g, :, pl.ds(k * width + head * HEAD, HEAD)] = grad[:length]
                go[2 * g + k][:, cols] = grad[length:].astype(BF)


def add_crossed_kernel(*refs):
    stay, out = refs[0], refs[-1]
    width = refs[1].shape[1]
    for g in range(2):
        for k in range(2):
            cols = pl.ds(k * width, width)
            out[g, :, cols] = (stay[g, :, cols] + refs[1 + 2 * (1 - g) + k][...].astype(F32)).astype(BF)


def back_qkv_kernel(dq, dkv, dkv_far, far, w_own, w_other, all_out, bias_out, *outs):
    split = dkv.shape[2]
    cols = pl.ds(0, all_out.shape[2])
    for g in range(2):
        all_out[g, :, pl.ds(0, split)] = jnp.where(
            far[g] > 0.5, dkv_far[g].astype(F32), dkv[g].astype(F32)).astype(BF)
        all_out[g, :, pl.ds(split, dq.shape[2])] = dq[g]
        bias_out[g] = jnp.sum(all_out[g].astype(F32), 0, keepdims=True)
    for part, at in parts_of(dq.shape[1]):
        branch = dot_nt(all_out[0, at, :], w_own[:, cols]) + dot_nt(all_out[1, at, :], w_other[:, cols])
        if len(outs) == 1:
            outs[0][at, :] = branch.astype(BF)
        else:
            outs[part][...] = branch.astype(outs[part].dtype)


def grad_feed_kernel(count, shares, *refs):
    here, away = refs[4 * count], refs[4 * count + 1:]
    feat = refs[0].shape[1]
    rows = feat // shares
    tile = feat // 2
    for g in range(2):
        for t in range(2):
            cols = pl.ds(t * tile, tile)
            up, down = 0.0, 0.0
            for m in range(count):
                hid, feed, pre, act = refs[4 * m:4 * m + 4]
                up = up + dot_tn(hid[:, cols], pre[g])
                down = down + dot_tn(act[g, :, cols], feed[...])
            for k, grad in enumerate((up, down)):
                if g == 0 or len(away) == 1:
                    (here, away[0])[g][k, cols, :] = grad.astype(BF)
                    continue
                for b in range(shares // 2):
                    away[t * (shares // 2) + b][k] = grad[b * rows:(b + 1) * rows].astype(BF)


def fold(block, width):
    return jnp.concatenate([block[:, c:c + width] for c in range(0, block.shape[1], width)], 0)


def unfold(block, rows):
    return jnp.concatenate([block[c:c + rows] for c in range(0, block.shape[0], rows)], 1)


def grad_attend_kernel(count, shares, vectors, *refs):
    smalls = refs[4 * count:4 * count + 2 * vectors]
    here, *away = refs[4 * count + 2 * vectors:]
    feat = refs[0].shape[1]
    split = refs[2].shape[2]
    width = split // 3
    rows, thin = feat // shares, width // shares
    stride = here.shape[0] // shares
    for g in range(2):
        acc, out = 0.0, 0.0
        for m in range(count):
            inputs, branch, d_qkv, mixed = refs[4 * m:4 * m + 4]
            acc = acc + dot_tn(inputs[...], d_qkv[g])
            out = out + dot_tn(mixed[g], branch[...])
        for b in range(shares):
            if g == 0 or len(away) == 1:
                ref, first = (here, away[0])[g], b * stride
            else:
                ref, first = away[b], 0
            at = pl.ds(first, rows)
            if vectors:
                ref[pl.ds(first + rows, stride - rows), :] = smalls[g][...].astype(BF)
            ref[at, pl.ds(0, split)] = acc[b * rows:(b + 1) * rows].astype(BF)
            ref[at, pl.ds(split, width)] = fold(out[b * thin:(b + 1) * thin, :], width).astype(BF)


def split_kernel(shares, order, feeds, attends, *refs):
    where, keep, send = refs[-3:]
    groups = [refs[1 + (1 + shares) * n - 1:(1 + shares) * (n + 1)] for n in range(feeds + attends)]
    for b in range(shares):
        spot = 0
        for here, *came in groups:
            rows = here.shape[-2] // shares
            for index in ((0,), (1,)) if len(here.shape) == 3 else ((),):
                mine = here[index + (pl.ds(b * rows, rows), slice(None))].astype(F32)
                value = mine + came[b][index + (slice(None), slice(None))].astype(F32)
                deal(where, b, order, keep, send, (spot,), value.astype(BF))
                spot += 1


def unfold_kernel(shares, *refs):
    for ref, out in zip(refs[:2], refs[2:]):
        width, feat = out.shape
        rows, thin = feat // shares, width // shares
        blocks = [unfold(ref[pl.ds(b * rows, rows), pl.ds(3 * width, width)].astype(F32), thin) for b in range(shares)]
        out[...] = jnp.concatenate(blocks, 0).astype(BF)


def pack_kernel(*refs):
    key, value, query, out = refs[:4]
    rows, width = key.shape
    payload = refs[-1]
    if len(refs) > 5:
        payload, small = refs[-2:]
    at = pl.ds(0, rows)
    for index, ref in enumerate((key, value, query)):
        payload[at, pl.ds(index * width, width)] = ref[...]
    payload[at, pl.ds(3 * width, width)] = fold(out[...].astype(F32), width).astype(BF)
    if len(refs) > 5:
        small[...] = jnp.zeros(small.shape, F32)
        for index, ref in enumerate(refs[4:-3]):
            small[pl.ds(LAYERS * index, LAYERS), pl.ds(0, ref.shape[1])] = ref[...].astype(F32)
        up = refs[-3]
        small[pl.ds(0, LAYERS), pl.ds(128, up.shape[1])] = up[...].astype(F32)
        payload[pl.ds(rows, small.shape[0]), :] = small[...].astype(BF)


def shares_kernel(key, value, query, out, up_early, down_early, up_late, down_late, early, late):
    early[0] = up_early[...]
    early[1] = down_early[...]
    pack_kernel(key, value, query, out, early.at[2])
    late[0] = up_late[...]
    late[1] = down_late[...]


def assemble_kernel(masks, per, up_per, *refs):
    count = len(masks)
    where = refs[2 * count]
    small_outs = len(refs) - 2 * count - 1 - 5 > 0
    if small_outs:
        spread, up_spread = refs[2 * count + 1:2 * count + 3]
        outs, (table, bias_own, bias_other), scratch = refs[2 * count + 3:-4], refs[-4:-1], refs[-1]
    else:
        outs, scratch = refs[2 * count + 1:-1], refs[-1]
    blk, grp = where[0], where[1]
    width, feat = outs[2].shape
    rows, thin = feat // count, width // count
    if small_outs:
        lane = lax.broadcasted_iota(jnp.int32, table.shape, 1)
        row = lax.broadcasted_iota(jnp.int32, table.shape, 0)
        six = 0.0
    for g in range(2):
        projection, hidden = 0.0, 0.0
        for index, mask in enumerate(masks):
            ref = refs[g * count + index]
            b = jnp.bitwise_xor(blk, mask)
            outs[g][pl.ds(pl.multiple_of(b * rows, rows), rows), :] = ref[pl.ds(0, rows), pl.ds(0, 3 * width)]
            block = ref[pl.ds(0, rows), pl.ds(3 * width, width)].astype(F32)
            scratch[pl.ds(pl.multiple_of(b * thin, thin), thin), :] = unfold(block, thin)
            if not small_outs:
                continue
            small = ref[pl.ds(rows, table.shape[0]), :]
            spreaded = dot(small[:, :per], spread[...])
            at = lane - (jnp.bitwise_xor(grp, g) * count + b) * per
            six = six + jnp.where((at >= 0) & (at < per), spreaded, 0.0)
            at = lane - b * per - jnp.where(row < LAYERS, 2 * width, width)
            projection = projection + jnp.where((at >= 0) & (at < per), spreaded, 0.0)
            at = lane - b * up_per
            hidden = hidden + jnp.where((at >= 0) & (at < up_per), dot(small[:, 128:128 + up_per], up_spread[...]), 0.0)
        outs[2 + g][...] = scratch[...].astype(BF)
        if small_outs:
            bias = (bias_own, bias_other)[g]
            bias[...] = jnp.zeros(bias.shape, F32)
            bias[pl.ds(0, LAYERS), :] = projection[:LAYERS] + projection[LAYERS:2 * LAYERS]
            bias[pl.ds(LAYERS, LAYERS), :] = hidden[:LAYERS]
    if small_outs:
        table[...] = six.astype(BF)


def small_kernel(layers, *refs):
    out, other = refs[-2:]
    out[...] = jnp.zeros(out.shape, F32)
    other[...] = jnp.zeros(other.shape, F32)
    per_layer = (len(refs) - 2) // layers
    for layer in range(layers):
        mine = refs[layer * per_layer:(layer + 1) * per_layer]
        sets = [mine[i:i + 4] for i in range(0, per_layer, 4)]
        base = 8 * layer
        for row, (which, index) in enumerate(((1, 2), (1, 0), (1, 1), (0, 2), (0, 0), (0, 1))):
            total = sum(s[which][pl.ds(index, 1), :] for s in sets)
            out[pl.ds(base + row, 1), :] = total
            other[pl.ds(base + row, 1), :] = total
        cols = pl.ds(0, sets[0][3].shape[2])
        for g, ref in enumerate((out, other)):
            ref[pl.ds(base + 6, 1), :] = sum(s[2][g] for s in sets)
            ref[pl.ds(base + 7, 1), cols] = sum(s[3][g] for s in sets)


def bits_of(count):
    return list(range(count.bit_length() - 1))


class Gather:
    def __init__(self, share):
        self.pieces = {0: share}

    def step(self, bits, after):
        held = dict(self.pieces)
        for mask, piece in held.items():
            if after is not None:
                piece, _ = lax.optimization_barrier((piece, after))
            for bit in bits:
                self.pieces[mask | bit] = send_xor(piece, "blk", bit)

    def over_y(self, masks):
        for mask in masks:
            self.pieces[mask | 1] = send_xor(self.pieces[mask], "blk", 1)

    def both(self, after):
        masks = sorted(self.pieces)
        own = [self.pieces[m] for m in masks]
        if after is not None:
            ready = [lax.optimization_barrier((piece, after))[0] for piece in own]
        else:
            ready = own
        return masks, own + [send_xor(piece, "grp", 1) for piece in ready]


class Scatter:
    def __init__(self, keep, send, order):
        self.keep = keep
        self.came = send_xor(send, "blk", order[0])
        self.order = order[1:]

    def halve(self, chain):
        shape = (self.keep.shape[0] // 2,) + self.keep.shape[1:]
        self.keep, send = run(halve_kernel, [self.keep, self.came], [(shape, BF)] * 2, "halve", chain=chain)
        self.came = send_xor(send, "blk", self.order[0])
        self.order = self.order[1:]

    def total(self):
        return self.keep[0].astype(F32) + self.came[0].astype(F32)


def sum_axis(block, axis, masks):
    for mask in masks:
        block = block + send_xor(block, axis, mask)
    return block


def fold_share(block, width):
    rows = block.shape[0]
    return jnp.moveaxis(block.reshape(rows, -1, width), 1, 0).reshape(-1, width)


def unfold_shares(columns, shares, feat):
    width = columns.shape[1]
    blocks = columns.reshape(shares, feat // width, -1, width)
    return jnp.moveaxis(blocks, 1, 2).reshape(-1, feat)


def stream(rows, grad_rows, shape, hid, weights, chain, result):
    half, feat = shape
    width = feat // 4
    lse_rows = -(-(2 * width // HEAD) // 8) * 8

    def stage(body, operands, outs, name):
        return run(body, operands, outs, name, chain=chain)

    def over_x(near):
        return [near, send_xor(near, "grp", 2)]

    def over_core(pieces):
        return [send_xor(piece, "grp", 1) for piece in pieces]

    wide, short = ((half, feat), F32), ((half, feat), BF)
    projected = [((2, half, 2 * width), BF), ((2, half, width), BF)]
    pieces = 4 * [((half, width), BF)]
    hidden_shape = ((2, half, hid), BF)
    sums_shape = ((8, feat), F32)
    kept = []
    for layer in range(LAYERS):
        w = weights[layer]
        if layer == 0:
            kv, q = stage(lambda *r: qkv_kernel(layer, *r), [rows, *w["qkv"], *w["bias"]], projected, "qkv")
        kv_far = send_xor(kv, "blk", 1)
        yield "qkv", layer
        chosen = list(stage(lambda *r: choose_kernel(*r[:3], *r[4:]), [kv, kv_far, w["far"], w["vec"]], pieces, "choose"))
        chosen += over_core(chosen)
        near, mixed, lse, used = stage(
            attend_kernel, [q] + chosen + [*w["out"]],
            [short, saved(((2, half, width), BF)), ((lse_rows, half), F32), ((4, 2 * half, width), BF)], "attend")
        branch = over_x(near)
        yield "attend", layer
        resid_one, hidden, act, slope, near = stage(
            lambda *r: feed_kernel(layer, *r),
            branch + [in_hbm(b) for b in [rows, w["vec"]] + w["up"] + w["down"] + w["bias"]],
            [wide, saved(short), saved(hidden_shape), hidden_shape, short], "feed")
        branch = over_x(near)
        yield "feed", layer
        before = (rows, q, used, lse, mixed, resid_one, hidden, act, slope)
        if layer < LAYERS - 1:
            after = weights[layer + 1]
            resid_two, rows, kv, q = stage(
                lambda *r: norm_two_qkv_kernel(layer, *r),
                branch + [resid_one, w["vec"], *after["qkv"], *after["bias"]],
                [wide, short] + projected, "norm_two_qkv")
        else:
            resid_two, rows = stage(lambda *r: norm_two_kernel(layer, *r), branch + [resid_one, w["vec"]],
                                    [wide, short], "norm_two")
        result["outputs"].append(rows[:half // 2])
        kept.append(before + (resid_two,))

    grads = [grad_rows]
    for layer in reversed(range(LAYERS)):
        w = weights[layer]
        rows, q, used, lse, mixed, resid_one, hidden, act, slope, resid_two = kept[layer]
        d_two, feed, sums_two, d_pre, g_up, near = stage(
            lambda *r: back_feed_kernel(layer, len(grads), *r),
            grads + [resid_two, w["vec"], *w["up"], *w["down"], slope],
            [wide, short, sums_shape, hidden_shape, ((2, 1, hid), F32), short], "back_feed")
        result["feed"][layer] = [hidden, feed, d_pre, act]
        branch = over_x(near)
        yield "back_feed", layer
        d_one, branch, sums_one, dq, stay, *go = stage(
            lambda *r: back_attend_kernel(layer, *r),
            branch + [d_two, resid_one, w["vec"], *w["out"], q, used, lse],
            [wide, short, sums_shape, ((2, half, width), BF), ((2, half, 2 * width), F32)] + pieces, "back_attend")
        dkv, = stage(add_crossed_kernel, [stay] + over_core(go), [((2, half, 2 * width), BF)], "add_crossed")
        dkv_far = send_xor(dkv, "blk", 1)
        yield "back_attend", layer
        outs = [short] if layer else [((half // 2, feat), F32), ((half // 2, feat), BF)]
        d_qkv, g_qkv, *outs = stage(
            back_qkv_kernel, [dq, dkv, dkv_far, w["far"], *w["qkv"]],
            [((2, half, 3 * width), BF), ((2, 1, 3 * width), F32)] + outs, "back_qkv")
        result["attend"][layer] = [rows, branch, d_qkv, mixed]
        result["smalls"][layer] = [sums_two, sums_one, g_up, g_qkv]
        if layer:
            grads = over_x(outs[0]) + [d_one]
        else:
            came = send_xor(outs[1], "grp", 2)
            result["grad"] = d_one[:half // 2] + outs[0] + came.astype(F32)
        yield "back_qkv", layer


def per_device(layer_input, w_query, w_key, w_value, b_query, b_value, w_out, b_out, gain_one,
               bias_one, w_up, b_up, w_down, b_down, gain_two, bias_two, head_table, grad_top):
    blk_count = lax.axis_size("blk")
    grp_count = lax.axis_size("grp")
    grp = lax.axis_index("grp")
    blk = lax.axis_index("blk")
    feat = w_out.shape[2]
    share_rows = w_query.shape[1]
    width = w_query.shape[2]
    heads = width // HEAD
    hid = w_up.shape[2]
    per = b_out.shape[1]
    up_per = b_up.shape[1]
    blk_masks = [1 << bit for bit in bits_of(blk_count)[::-1]]
    packed = blk_count == 8 and share_rows % 32 == 0 and per % 8 == 0
    block_own = blk % NB
    target = jnp.where(block_own == 0, head_table[:, :, 0], head_table[:, :, 1])
    far = (target != block_own).astype(F32)
    far = jnp.stack([lax.dynamic_slice_in_dim(far, g * heads, heads, 1) for g in (grp, grp ^ 1)], 1)
    far_cols = jnp.broadcast_to(far[:, :, None, :, None], (LAYERS, 2, 2, heads, HEAD)).reshape(LAYERS, 2, 1, 2 * width)

    start = layer_input[:, 0]
    row_top = jnp.concatenate([start, send_xor(start, "grp", 2)], 1)
    grad_start = grad_top[:, 0]
    grad_rows = jnp.concatenate([grad_start, send_xor(grad_start, "grp", 2)], 1)

    micros = range(layer_input.shape[0])
    count = len(micros)
    chain = Order()
    results = [{"outputs": [], "feed": {}, "attend": {}, "smalls": {}} for _ in micros]
    weights = [{"far": pick(far_cols, layer)} for layer in range(LAYERS)]
    where = (jnp.stack([blk, grp]).astype(jnp.int32), pl.BlockSpec((2,), lambda i: (0,), memory_space=pltpu.SMEM))
    grad_feed, grad_attend, tiny = {}, {}, []
    smalls = [b_query, b_value, b_out, gain_one, bias_one, b_down, gain_two, bias_two]
    small_rows = len(smalls) * LAYERS
    vec_shape = (small_rows, feat)

    def factors(name, layer):
        return [f for r in results for f in r[name][layer]]

    chunks = blk_count if packed else 1

    def sum_feed(layer):
        rest = [((2, feat // chunks, hid), BF)] * chunks
        grad_feed[layer] = run(lambda *r: grad_feed_kernel(count, chunks, *r), factors("feed", layer),
                               [((2, feat, hid), BF)] + rest, "grad_feed", 16, chain=chain)

    def sum_attend(layer):
        vectors = tiny if packed and layer == 0 else []
        high = feat + (len(vectors) // 2) * blk_count * 8 * LAYERS
        rest = [((high // chunks, feat), BF)] * chunks
        grad_attend[layer] = run(lambda *r: grad_attend_kernel(count, blk_count, len(vectors) // 2, *r),
                                 factors("attend", layer) + vectors, [((high, feat), BF)] + rest, "grad_attend", 16,
                                 chain=chain)

    def add_small():
        sums = sum([r["smalls"][layer] for layer in range(LAYERS) for r in results], [])
        tiny.extend(run(lambda *r: small_kernel(LAYERS, *r), sums, [((8 * LAYERS, feat), F32)] * 2, "small",
                        chain=chain))

    if packed:
        def pack(layer, *more, scratch=(), order=None):
            rows = share_rows + (small_rows if more else 0)
            return run(pack_kernel, [pick(a, layer) for a in (w_key, w_value, w_query, w_out)] + list(more),
                       [((rows, feat), BF)], "pack", 60, scratch, order)[0]

        first = Gather(pack(0, *smalls, b_up, scratch=[pltpu.VMEM(vec_shape, F32)]))
        first.step([1, 2, 4, 6], None)
        first.over_y([2, 4, 6])
        early, late = run(
            shares_kernel, [pick(a, 1) for a in (w_key, w_value, w_query, w_out)]
            + [pick(a, layer) for layer in range(LAYERS) for a in (w_up, w_down)],
            [((3, share_rows, feat), BF), ((2, share_rows, feat), BF)], "shares", 60)
        gathered = {"early": lax.all_gather(early, "blk", axis=1, tiled=True)}
        lanes = jnp.arange(feat)[None, :]
        spread = (lanes % per == jnp.arange(per)[:, None]).astype(BF)
        up_spread = (lanes % up_per == jnp.arange(up_per)[:, None]).astype(BF)

        def start_feed():
            block = lax.optimization_barrier((late, chain.token))[0]
            gathered["late"] = lax.all_gather(block, "blk", axis=1, tiled=True)

        def over_cores(name):
            block = gathered[name]
            return [block, send_xor(lax.optimization_barrier((block, chain.token))[0], "grp", 1)]

        def have_early():
            both = over_cores("early")
            outs = run(lambda *r: unfold_kernel(blk_count, *r), [pick(b, 2) for b in both], [((width, feat), BF)] * 2,
                       "unfold")
            weights[0].update(up=[pick(b, 0) for b in both], down=[pick(b, 1) for b in both])
            weights[1].update(qkv=[pick(b, 2) for b in both], out=outs)

        def have_late():
            both = over_cores("late")
            weights[1].update(up=[pick(b, 0) for b in both], down=[pick(b, 1) for b in both])

        sums_of = {}

        def scatter(key, grads, part=None):
            here, *away = grads
            came = [send_xor(piece, "grp", 1) for piece in away]
            if part is not None:
                groups, depth = [pick(a, part) for a in [here] + came], 1
            else:
                groups, depth = [here] + came, 2 if here.ndim == 3 else 1
            outs = [((blk_count // 2, depth, here.shape[-2] // blk_count, feat), BF)] * 2
            keep, send = run(lambda *r: split_kernel(blk_count, ORDERS[key], 1, 0, *r), groups + [where], outs, "split",
                             16, chain=chain)
            sums_of[key] = Scatter(keep, send, ORDERS[key])

        steps = {
            "A": lambda: sum_feed(1), "B": lambda: scatter("A", grad_feed[1]),
            "C": lambda: sum_attend(1), "D": lambda: scatter("C", grad_attend[1]),
            "a": lambda: sum_feed(0), "b": lambda: scatter("a", grad_feed[0], 0), "e": lambda: scatter("e", grad_feed[0], 1),
            "c": lambda: sum_attend(0), "d": lambda: scatter("c", grad_attend[0]), "m": add_small,
        }
        for letter, key in zip("FGfhg", "ACaec"):
            steps[letter] = lambda key=key: sums_of[key].halve(chain)

        masks, pieces = first.both(None)
        outs = run(lambda *r: assemble_kernel(masks, per, up_per, *r), pieces + [where, spread, up_spread],
                   [((feat, 3 * width), BF)] * 2 + [((width, feat), BF)] * 2 + [(vec_shape, BF)] + [((8, feat), F32)] * 2,
                   "assemble", scratch=[pltpu.VMEM((width, feat), F32)], chain=chain)
        weights[0].update(qkv=outs[:2], out=outs[2:4])
        table, *biases = outs[4:]
        vec = table + send_xor(table, "grp", 2)
        after = {
            ("attend", 0, 1): lambda: (have_early(), start_feed()),
            ("attend", 1, 1): have_late,
        }
    else:
        table = jnp.zeros(vec_shape, BF)
        rows = jnp.stack(smalls).reshape(small_rows, per)
        table = lax.dynamic_update_slice(table, rows, (0, (grp * blk_count + blk) * per))
        spots = jnp.zeros((8, feat), BF)
        spots = lax.dynamic_update_slice(spots, b_query, (0, 2 * width + blk * per))
        spots = lax.dynamic_update_slice(spots, b_value, (LAYERS, width + blk * per))
        spots = lax.dynamic_update_slice(spots, b_up, (2 * LAYERS, blk * up_per))
        table = sum_axis(table, "blk", blk_masks)
        spots = sum_axis(spots, "blk", blk_masks).astype(F32)
        bias = jnp.zeros((8, feat), F32)
        bias = bias.at[:LAYERS].set(spots[:LAYERS] + spots[LAYERS:2 * LAYERS])
        bias = bias.at[LAYERS:2 * LAYERS].set(spots[2 * LAYERS:3 * LAYERS])
        for layer in range(LAYERS):
            block = jnp.concatenate([w_key[layer], w_value[layer], w_query[layer],
                                     fold_share(w_out[layer], width)], 1)
            block = lax.all_gather(block, "blk", axis=0, tiled=True)
            pair = [block, send_xor(block, "grp", 1)]
            block = lax.all_gather(jnp.stack([w_up[layer], w_down[layer]]), "blk", axis=1, tiled=True)
            both = [block, send_xor(block, "grp", 1)]
            weights[layer].update(qkv=[b[:, :3 * width] for b in pair],
                                  out=[unfold_shares(b[:, 3 * width:], blk_count, feat) for b in pair],
                                  up=[pick(b, 0) for b in both], down=[pick(b, 1) for b in both])
        biases = [bias, send_xor(bias, "grp", 1)]
        vec = sum_axis(table, "grp", [2, 1])
        after = {}
        for layer in range(LAYERS):
            after["back_feed", layer, count - 1] = lambda layer=layer: sum_feed(layer)
            after["back_qkv", layer, count - 1] = lambda layer=layer: sum_attend(layer)

    vec = vec.astype(F32)
    for w in weights:
        w.update(vec=vec, bias=biases)
    streams = [stream(pick(row_top, m), pick(grad_rows, m), row_top.shape[1:], hid, weights, chain, results[m])
               for m in micros]
    done = False
    while not done:
        for m, one in enumerate(streams):
            label = next(one, None)
            done = label is None
            if not done and label + (m,) in after:
                after[label + (m,)]()
            if not done and packed:
                for letter in SLOTS.get(label + (m,), ""):
                    steps[letter]()
    if packed:
        late, up, down, attend, attend1 = [sums_of[key].total() for key in "AaecC"]
        grad_feed = {0: jnp.concatenate([up, down]), 1: late}
        grad_attend = {0: attend[0, :share_rows], 1: attend1[0]}
    else:
        for dim, sums in ((1, grad_feed), (0, grad_attend)):
            for layer in sums:
                block = sums[layer][0] + send_xor(sums[layer][1], "grp", 1)
                sums[layer] = lax.psum_scatter(block, "blk", scatter_dimension=dim, tiled=True).astype(F32)

    if packed:
        tiny = attend[0, share_rows:]
    else:
        add_small()
        tiny = sum_axis(tiny[0] + send_xor(tiny[1], "grp", 1), "blk", blk_masks)
    tiny = tiny.reshape(LAYERS, 8, feat)
    six = tiny[:, :SMALLS]
    six = lax.dynamic_slice_in_dim(six, (grp * blk_count + blk) * per, per, 2)
    g_b_up = lax.dynamic_slice_in_dim(tiny[:, 6], blk * up_per, up_per, 1)
    g_b_value = lax.dynamic_slice_in_dim(tiny[:, 7], width + blk * per, per, 1)
    g_b_query = lax.dynamic_slice_in_dim(tiny[:, 7], 2 * width + blk * per, per, 1)
    feeds = jnp.stack([grad_feed[layer] for layer in range(LAYERS)])
    attends = jnp.stack([grad_attend[layer] for layer in range(LAYERS)])
    g_out = jnp.stack([unfold_shares(attends[layer, :, 3 * width:], 1, feat) for layer in range(LAYERS)])
    return (
        jnp.stack([jnp.stack([r["outputs"][layer] for r in results]) for layer in range(LAYERS)])[:, :, None],
        jnp.stack([r["grad"] for r in results])[:, None],
        attends[:, :, 2 * width:3 * width],
        attends[:, :, :width],
        attends[:, :, width:2 * width],
        g_b_query,
        g_b_value,
        g_out,
        six[:, 0],
        six[:, 1],
        six[:, 2],
        feeds[:, 0],
        g_b_up,
        feeds[:, 1],
        six[:, 3],
        six[:, 4],
        six[:, 5],
    )


def solution(mesh):
    rows = P(None, "blk", "grp", None)
    cols = P(None, "blk", "grp")
    both = P(None, ("grp", "blk"))
    tall = P(None, ("grp", "blk"), None)
    return jax.shard_map(
        per_device,
        mesh=mesh,
        in_specs=(rows, cols, cols, cols, both, both, tall, both, both, both, cols, both, tall,
                  both, both, both, P(), rows),
        out_specs=(P(None, None, "blk", "grp", None), rows, cols, cols, cols, both, both, tall,
                   both, both, both, cols, both, tall, both, both, both),
        check_vma=False,
    )
```

```python
import jax
import jax.numpy as jnp
from jax import lax
from jax.experimental import pallas as pl
from jax.experimental.pallas import tpu as pltpu
from jax.sharding import PartitionSpec as P

HEAD = 64
NB = 2
LAYERS = 2
EPS = 1e-05
SCALE = HEAD ** -0.5
BF = jnp.bfloat16
F32 = jnp.float32
SMALLS = 6
HINT = 200000000
SLOTS = {
    ("back_feed", 1, 1): "A", ("back_qkv", 1, 0): "B", ("back_feed", 0, 0): "C", ("back_feed", 0, 1): "FD",
    ("back_attend", 0, 1): "a", ("back_qkv", 0, 0): "GF", ("back_qkv", 0, 1): "mcdbeghfGghf",
}
ORDERS = {"A": [2, 4, 1], "C": [2, 4, 1], "a": [1, 2, 4], "e": [2, 4, 1], "c": [1, 2, 4]}
KEEP = True
WEIGHTS = True
WEIGHT = {"qkv": .9, "choose": .5, "attend": 2.5, "feed": 2.6, "norm_two_qkv": 1.6, "norm_two": .6, "back_feed": 3.6,
          "back_attend": 5, "add_crossed": .6, "back_qkv": 1.2, "grad_feed": 5.5, "grad_attend": 3.7, "split": 1.8,
          "halve": .8, "assemble": 1.8, "place": 2, "pack": 1.2, "small": .8}
B_OUT, GAIN_ONE, BIAS_ONE, B_DOWN, GAIN_TWO, BIAS_TWO = [LAYERS * (2 + i) for i in range(SMALLS)]


def send_xor(block, axis, mask):
    count = lax.axis_size(axis)
    return lax.ppermute(block, axis, [(i, i ^ mask) for i in range(count)])


def dot(left, right):
    return lax.dot_general(left, right, (((1,), (0,)), ((), ())), preferred_element_type=F32)


def dot_tn(left, right):
    return lax.dot_general(left, right, (((0,), (0,)), ((), ())), preferred_element_type=F32)


def dot_nt(left, right):
    return lax.dot_general(left, right, (((1,), (1,)), ((), ())), preferred_element_type=F32)


def pick(array, index):
    tail = array.shape[1:]
    return array, pl.BlockSpec((None,) + tail, lambda i: (index,) + (0,) * len(tail))


def saved(out):
    return out + ("saved",)


def in_hbm(operand):
    array, spec = operand if isinstance(operand, tuple) else whole(operand)
    return (pltpu.with_memory_space_constraint(array, pltpu.HBM) if WEIGHTS else array), spec


def whole(array):
    return array, pl.BlockSpec(array.shape, lambda i: (0,) * array.ndim)


class Order:
    token = None
    on = True


def run(body, operands, outs, name, mib=16, scratch=(), chain=None, unread=()):
    operands = [o if isinstance(o, tuple) else whole(o) for o in operands]
    reads = len(operands)
    outs = list(outs)
    writes = len(outs)
    extra = []
    if chain is not None and chain.token is not None:
        extra = [(chain.token, pl.BlockSpec(memory_space=pl.ANY))]
    extra = extra + [(array, pl.BlockSpec(memory_space=pl.ANY)) for array in unread]
    if chain is not None and not chain.on:
        chain = None
    if chain is not None:
        outs.append(((8, 128), F32))
    kernel_outs = [pltpu.HBM(*o[:2]) if len(o) > 2 and KEEP else jax.ShapeDtypeStruct(*o[:2]) for o in outs]
    out_shape = [jax.ShapeDtypeStruct(*o[:2]) for o in outs]

    def trimmed(*refs):
        results = refs[reads + len(extra):]
        if chain is not None:
            results[writes][...] = jnp.zeros((8, 128), F32)
            results = results[:writes] + results[writes + 1:]
        body(*refs[:reads], *results)

    results = pl.pallas_call(
        trimmed,
        out_shape=kernel_outs,
        grid=(1,),
        in_specs=[spec for _, spec in operands + extra],
        out_specs=[pl.BlockSpec(o.shape, lambda i, nd=len(o.shape): (0,) * nd) for o in out_shape],
        scratch_shapes=list(scratch),
        compiler_params=pltpu.CompilerParams(vmem_limit_bytes=mib * 2 ** 20),
        cost_estimate=pl.CostEstimate(flops=int(HINT * WEIGHT.get(name, 1)), bytes_accessed=1, transcendentals=0),
        name=name,
    )(*[array for array, _ in operands + extra])
    if chain is not None:
        chain.token = results[writes]
    return results[:writes]


def deal(where, chunk, order, keep, send, index, value):
    distance = jnp.bitwise_xor(where[0], chunk)
    spot = 0
    for bit in order[1:]:
        spot = spot * 2 + (jnp.bitwise_and(distance, bit) // bit)
    gone = jnp.bitwise_and(distance, order[0]) != 0

    @pl.when(gone)
    def _():
        send[(spot,) + index] = value

    @pl.when(jnp.logical_not(gone))
    def _():
        keep[(spot,) + index] = value


def halve_kernel(kept, came, keep, send):
    count = keep.shape[0]
    for i in range(count):
        keep[i] = (kept[i].astype(F32) + came[i].astype(F32)).astype(BF)
        send[i] = (kept[count + i].astype(F32) + came[count + i].astype(F32)).astype(BF)


def unit_of(resid):
    middle = jnp.mean(resid, -1, keepdims=True)
    center = resid - middle
    spread = jnp.mean(center * center, -1, keepdims=True)
    root = lax.rsqrt(spread + EPS)
    return center * root, root


def summed(near, came, part):
    half = near.shape[0] // 2
    here = near[pl.ds(part * half, half), :].astype(F32)
    return here + came[pl.ds((1 - part) * half, half), :].astype(F32)


def parts_of(rows):
    return [(part, pl.ds(part * (rows // 2), rows // 2)) for part in range(2)]


def at_row(vec, row):
    return vec[pl.ds(row, 1), :]


def project(layer, at, rows, weights, biases, kv_out, q_out):
    split = kv_out.shape[2]
    cols = pl.ds(0, split + q_out.shape[2])
    for g in range(2):
        acc = dot(rows, weights[g][:, cols]) + biases[g][pl.ds(layer, 1), cols]
        kv_out[g, at, :] = acc[:, :split].astype(BF)
        q_out[g, at, :] = (acc[:, split:].astype(BF) * SCALE).astype(BF)


def qkv_kernel(layer, rows, w_own, w_other, b_own, b_other, kv_out, q_out):
    for _, at in parts_of(rows.shape[0]):
        project(layer, at, rows[at, :], (w_own, w_other), (b_own, b_other), kv_out, q_out)


def norm_two_rows(layer, part, at, near, came, resid_one, vec, resid_out, out):
    unit, _ = unit_of(resid_one[at, :])
    hidden = unit * at_row(vec, layer + GAIN_ONE) + at_row(vec, layer + BIAS_ONE)
    resid = hidden + summed(near, came, part) + at_row(vec, layer + B_DOWN)
    resid_out[at, :] = resid
    unit, _ = unit_of(resid)
    out[at, :] = (unit * at_row(vec, layer + GAIN_TWO) + at_row(vec, layer + BIAS_TWO)).astype(BF)


def norm_two_kernel(layer, near, came, resid_one, vec, resid_out, out):
    for part, at in parts_of(out.shape[0]):
        norm_two_rows(layer, part, at, near, came, resid_one, vec, resid_out, out)


def norm_two_qkv_kernel(layer, near, came, resid_one, vec, w_own, w_other, b_own, b_other,
                        resid_out, out, kv_out, q_out):
    for part, at in parts_of(out.shape[0]):
        norm_two_rows(layer, part, at, near, came, resid_one, vec, resid_out, out)
        project(layer + 1, at, out[at, :], (w_own, w_other), (b_own, b_other), kv_out, q_out)


def choose_kernel(kv, kv_far, far, *outs):
    width = outs[0].shape[1]
    for g in range(2):
        for k in range(2):
            cols = pl.ds(k * width, width)
            outs[2 * g + k][...] = jnp.where(
                far[g, :, cols] > 0.5, kv_far[g, :, cols].astype(F32), kv[g, :, cols].astype(F32)).astype(BF)


def attend_kernel(*refs):
    q, out_own, out_other, near, mixed, lse, used = refs[:1] + refs[9:]
    pieces, crossed = refs[1:5], refs[5:9]
    _, length, width = q.shape
    heads = width // HEAD
    for g in range(2):
        for k in range(2):
            used[2 * g + k, pl.ds(0, length), :] = pieces[2 * g + k][...]
            used[2 * g + k, pl.ds(length, length), :] = crossed[2 * (1 - g) + k][...]
        for head in range(heads):
            cols = pl.ds(head * HEAD, HEAD)
            key, value = used[2 * g, :, cols], used[2 * g + 1, :, cols]
            scores = dot_nt(key, q[g, :, cols])
            high = jnp.max(scores, 0, keepdims=True)
            expo = jnp.exp(scores - high)
            total = jnp.sum(expo, 0, keepdims=True)
            lse[pl.ds(g * heads + head, 1), :] = high + jnp.log(total)
            probs = (expo * (1.0 / total)).astype(BF)
            mixed[g, :, cols] = dot_tn(probs, value).astype(BF)
    near[...] = (dot(mixed[0], out_own[...]) + dot(mixed[1], out_other[...])).astype(BF)


def feed_kernel(layer, near, came, inputs, vec, up_own, up_other, down_own, down_other, b_own, b_other,
                resid_out, hidden_out, act_out, slope_out, near_out):
    ups, downs, biases = (up_own, up_other), (down_own, down_other), (b_own, b_other)
    for part, at in parts_of(near.shape[0]):
        resid = inputs[at, :].astype(F32) + summed(near, came, part) + at_row(vec, layer + B_OUT)
        resid_out[at, :] = resid
        unit, _ = unit_of(resid)
        hidden_out[at, :] = (unit * at_row(vec, layer + GAIN_ONE) + at_row(vec, layer + BIAS_ONE)).astype(BF)
        branch = 0.0
        for g in range(2):
            u = dot(hidden_out[at, :], ups[g][...]) + biases[g][pl.ds(LAYERS + layer, 1), :]
            cdf = 0.5 * (1.0 + lax.erf(u * (0.5 ** 0.5)))
            density = jnp.exp(-0.5 * u * u) * ((2.0 * jnp.pi) ** -0.5)
            act = (u * cdf).astype(BF)
            act_out[g, at, :] = act
            slope_out[g, at, :] = (cdf + u * density).astype(BF)
            branch = branch + dot(act, downs[g][...])
        near_out[at, :] = branch.astype(BF)


def norm_back(grad, resid, gain):
    unit, root = unit_of(resid)
    scaled = grad * gain
    mean_e = jnp.mean(scaled, -1, keepdims=True)
    mean_en = jnp.mean(scaled * unit, -1, keepdims=True)
    pulled = root * (scaled - mean_e - unit * mean_en)
    return pulled, (jnp.sum(grad * unit, 0, keepdims=True), jnp.sum(grad, 0, keepdims=True),
                    jnp.sum(pulled, 0, keepdims=True))


def back_norm(grads, gain_row, resid, vec, full_out, short_out, sums_out):
    sums_out[...] = jnp.zeros(sums_out.shape, F32)
    for part, at in parts_of(resid.shape[0]):
        grad = grads[-1][at, :].astype(F32)
        if len(grads) > 1:
            grad = grad + summed(grads[0], grads[1], part)
        pulled, sums = norm_back(grad, resid[at, :], at_row(vec, gain_row))
        full_out[at, :] = pulled
        short_out[at, :] = pulled.astype(BF)
        for index, s in enumerate(sums):
            sums_out[pl.ds(index, 1), :] += s


def back_feed_kernel(layer, grads, *refs):
    resid, vec, up_own, up_other, down_own, down_other, slope = refs[grads:grads + 7]
    full_out, short_out, sums_out, pre_out, bias_out, near_out = refs[grads + 7:]
    back_norm(refs[:grads], layer + GAIN_TWO, resid, vec, full_out, short_out, sums_out)
    ups, downs = (up_own, up_other), (down_own, down_other)
    totals = [0.0, 0.0]
    for _, at in parts_of(resid.shape[0]):
        branch = 0.0
        for g in range(2):
            pre = (dot_nt(short_out[at, :], downs[g][...]) * slope[g, at, :].astype(F32)).astype(BF)
            pre_out[g, at, :] = pre
            totals[g] = totals[g] + jnp.sum(pre.astype(F32), 0, keepdims=True)
            branch = branch + dot_nt(pre, ups[g][...])
        near_out[at, :] = branch.astype(BF)
    for g in range(2):
        bias_out[g] = totals[g]


def back_attend_kernel(layer, *refs):
    grads, (resid, vec, out_own, out_other, q, used, lse) = refs[:3], refs[3:10]
    full_out, short_out, sums_out, dq_out, stay = refs[10:15]
    go = refs[15:19]
    back_norm(grads, layer + GAIN_ONE, resid, vec, full_out, short_out, sums_out)
    _, length, width = q.shape
    heads = width // HEAD
    for g in range(2):
        d_mixed_all = dot_nt(short_out[...], (out_own, out_other)[g][...]).astype(BF)
        for head in range(heads):
            cols = pl.ds(head * HEAD, HEAD)
            key, value = used[2 * g, :, cols], used[2 * g + 1, :, cols]
            query = q[g, :, cols]
            d_mixed = d_mixed_all[:, head * HEAD:(head + 1) * HEAD]
            probs = jnp.exp(dot_nt(key, query) - lse[pl.ds(g * heads + head, 1), :])
            d_probs = dot_nt(value, d_mixed)
            inner = jnp.sum(d_probs * probs, 0, keepdims=True)
            d_scores = (probs * (d_probs - inner)).astype(BF)
            d_value = dot(probs.astype(BF), d_mixed)
            d_key = dot(d_scores, query)
            dq_out[g, :, cols] = (dot_tn(d_scores, key) * SCALE).astype(BF)
            for k, grad in enumerate((d_key, d_value)):
                stay[g, :, pl.ds(k * width + head * HEAD, HEAD)] = grad[:length]
                go[2 * g + k][:, cols] = grad[length:].astype(BF)


def add_crossed_kernel(*refs):
    stay, out = refs[0], refs[-1]
    width = refs[1].shape[1]
    for g in range(2):
        for k in range(2):
            cols = pl.ds(k * width, width)
            out[g, :, cols] = (stay[g, :, cols] + refs[1 + 2 * (1 - g) + k][...].astype(F32)).astype(BF)


def back_qkv_kernel(dq, dkv, dkv_far, far, w_own, w_other, all_out, bias_out, *outs):
    split = dkv.shape[2]
    cols = pl.ds(0, all_out.shape[2])
    for g in range(2):
        all_out[g, :, pl.ds(0, split)] = jnp.where(
            far[g] > 0.5, dkv_far[g].astype(F32), dkv[g].astype(F32)).astype(BF)
        all_out[g, :, pl.ds(split, dq.shape[2])] = dq[g]
        bias_out[g] = jnp.sum(all_out[g].astype(F32), 0, keepdims=True)
    for part, at in parts_of(dq.shape[1]):
        branch = dot_nt(all_out[0, at, :], w_own[:, cols]) + dot_nt(all_out[1, at, :], w_other[:, cols])
        if len(outs) == 1:
            outs[0][at, :] = branch.astype(BF)
        else:
            outs[part][...] = branch.astype(outs[part].dtype)


def grad_feed_kernel(count, shares, *refs):
    here, away = refs[4 * count], refs[4 * count + 1:]
    feat = refs[0].shape[1]
    rows = feat // shares
    tile = feat // 2
    for g in range(2):
        for t in range(2):
            cols = pl.ds(t * tile, tile)
            up, down = 0.0, 0.0
            for m in range(count):
                hid, feed, pre, act = refs[4 * m:4 * m + 4]
                up = up + dot_tn(hid[:, cols], pre[g])
                down = down + dot_tn(act[g, :, cols], feed[...])
            for k, grad in enumerate((up, down)):
                if g == 0 or len(away) == 1:
                    (here, away[0])[g][k, cols, :] = grad.astype(BF)
                    continue
                for b in range(shares // 2):
                    away[t * (shares // 2) + b][k] = grad[b * rows:(b + 1) * rows].astype(BF)


def fold(block, width):
    return jnp.concatenate([block[:, c:c + width] for c in range(0, block.shape[1], width)], 0)


def unfold(block, rows):
    return jnp.concatenate([block[c:c + rows] for c in range(0, block.shape[0], rows)], 1)


def grad_attend_kernel(count, shares, vectors, *refs):
    smalls = refs[4 * count:4 * count + 2 * vectors]
    here, *away = refs[4 * count + 2 * vectors:]
    feat = refs[0].shape[1]
    split = refs[2].shape[2]
    width = split // 3
    rows, thin = feat // shares, width // shares
    stride = here.shape[0] // shares
    for g in range(2):
        acc, out = 0.0, 0.0
        for m in range(count):
            inputs, branch, d_qkv, mixed = refs[4 * m:4 * m + 4]
            acc = acc + dot_tn(inputs[...], d_qkv[g])
            out = out + dot_tn(mixed[g], branch[...])
        for b in range(shares):
            if g == 0 or len(away) == 1:
                ref, first = (here, away[0])[g], b * stride
            else:
                ref, first = away[b], 0
            at = pl.ds(first, rows)
            if vectors:
                ref[pl.ds(first + rows, stride - rows), :] = smalls[g][...].astype(BF)
            ref[at, pl.ds(0, split)] = acc[b * rows:(b + 1) * rows].astype(BF)
            ref[at, pl.ds(split, width)] = fold(out[b * thin:(b + 1) * thin, :], width).astype(BF)


def split_kernel(shares, order, feeds, attends, *refs):
    where, keep, send = refs[-3:]
    groups = [refs[1 + (1 + shares) * n - 1:(1 + shares) * (n + 1)] for n in range(feeds + attends)]
    for b in range(shares):
        spot = 0
        for here, *came in groups:
            rows = here.shape[-2] // shares
            for index in ((0,), (1,)) if len(here.shape) == 3 else ((),):
                mine = here[index + (pl.ds(b * rows, rows), slice(None))].astype(F32)
                value = mine + came[b][index + (slice(None), slice(None))].astype(F32)
                deal(where, b, order, keep, send, (spot,), value.astype(BF))
                spot += 1


def unfold_kernel(shares, *refs):
    for ref, out in zip(refs[:2], refs[2:]):
        width, feat = out.shape
        rows, thin = feat // shares, width // shares
        blocks = [unfold(ref[pl.ds(b * rows, rows), pl.ds(3 * width, width)].astype(F32), thin) for b in range(shares)]
        out[...] = jnp.concatenate(blocks, 0).astype(BF)


def pack_kernel(*refs):
    key, value, query, out = refs[:4]
    rows, width = key.shape
    payload = refs[-1]
    if len(refs) > 5:
        payload, small = refs[-2:]
    at = pl.ds(0, rows)
    for index, ref in enumerate((key, value, query)):
        payload[at, pl.ds(index * width, width)] = ref[...]
    payload[at, pl.ds(3 * width, width)] = fold(out[...].astype(F32), width).astype(BF)
    if len(refs) > 5:
        small[...] = jnp.zeros(small.shape, F32)
        for index, ref in enumerate(refs[4:-3]):
            small[pl.ds(LAYERS * index, LAYERS), pl.ds(0, ref.shape[1])] = ref[...].astype(F32)
        up = refs[-3]
        small[pl.ds(0, LAYERS), pl.ds(128, up.shape[1])] = up[...].astype(F32)
        payload[pl.ds(rows, small.shape[0]), :] = small[...].astype(BF)


def shares_kernel(key, value, query, out, up_early, down_early, up_late, down_late, early, attend, late):
    early[0] = up_early[...]
    early[1] = down_early[...]
    pack_kernel(key, value, query, out, attend)
    late[0] = up_late[...]
    late[1] = down_late[...]


def assemble_kernel(masks, per, up_per, *refs):
    count = len(masks)
    where = refs[2 * count]
    small_outs = len(refs) - 2 * count - 1 - 5 > 0
    if small_outs:
        spread, up_spread = refs[2 * count + 1:2 * count + 3]
        outs, (table, bias_own, bias_other), scratch = refs[2 * count + 3:-4], refs[-4:-1], refs[-1]
    else:
        outs, scratch = refs[2 * count + 1:-1], refs[-1]
    blk, grp = where[0], where[1]
    width, feat = outs[2].shape
    rows, thin = feat // count, width // count
    if small_outs:
        lane = lax.broadcasted_iota(jnp.int32, table.shape, 1)
        row = lax.broadcasted_iota(jnp.int32, table.shape, 0)
        six = 0.0
    for g in range(2):
        projection, hidden = 0.0, 0.0
        for index, mask in enumerate(masks):
            ref = refs[g * count + index]
            b = jnp.bitwise_xor(blk, mask)
            outs[g][pl.ds(pl.multiple_of(b * rows, rows), rows), :] = ref[pl.ds(0, rows), pl.ds(0, 3 * width)]
            block = ref[pl.ds(0, rows), pl.ds(3 * width, width)].astype(F32)
            scratch[pl.ds(pl.multiple_of(b * thin, thin), thin), :] = unfold(block, thin)
            if not small_outs:
                continue
            small = ref[pl.ds(rows, table.shape[0]), :]
            spreaded = dot(small[:, :per], spread[...])
            at = lane - (jnp.bitwise_xor(grp, g) * count + b) * per
            six = six + jnp.where((at >= 0) & (at < per), spreaded, 0.0)
            at = lane - b * per - jnp.where(row < LAYERS, 2 * width, width)
            projection = projection + jnp.where((at >= 0) & (at < per), spreaded, 0.0)
            at = lane - b * up_per
            hidden = hidden + jnp.where((at >= 0) & (at < up_per), dot(small[:, 128:128 + up_per], up_spread[...]), 0.0)
        outs[2 + g][...] = scratch[...].astype(BF)
        if small_outs:
            bias = (bias_own, bias_other)[g]
            bias[...] = jnp.zeros(bias.shape, F32)
            bias[pl.ds(0, LAYERS), :] = projection[:LAYERS] + projection[LAYERS:2 * LAYERS]
            bias[pl.ds(LAYERS, LAYERS), :] = hidden[:LAYERS]
    if small_outs:
        table[...] = six.astype(BF)


def small_kernel(layers, *refs):
    out, other = refs[-2:]
    out[...] = jnp.zeros(out.shape, F32)
    other[...] = jnp.zeros(other.shape, F32)
    per_layer = (len(refs) - 2) // layers
    for layer in range(layers):
        mine = refs[layer * per_layer:(layer + 1) * per_layer]
        sets = [mine[i:i + 4] for i in range(0, per_layer, 4)]
        base = 8 * layer
        for row, (which, index) in enumerate(((1, 2), (1, 0), (1, 1), (0, 2), (0, 0), (0, 1))):
            total = sum(s[which][pl.ds(index, 1), :] for s in sets)
            out[pl.ds(base + row, 1), :] = total
            other[pl.ds(base + row, 1), :] = total
        cols = pl.ds(0, sets[0][3].shape[2])
        for g, ref in enumerate((out, other)):
            ref[pl.ds(base + 6, 1), :] = sum(s[2][g] for s in sets)
            ref[pl.ds(base + 7, 1), cols] = sum(s[3][g] for s in sets)


def bits_of(count):
    return list(range(count.bit_length() - 1))


class Gather:
    def __init__(self, share):
        self.pieces = {0: share}

    def step(self, bits, after):
        held = dict(self.pieces)
        for mask, piece in held.items():
            if after is not None:
                piece, _ = lax.optimization_barrier((piece, after))
            for bit in bits:
                self.pieces[mask | bit] = send_xor(piece, "blk", bit)

    def over_y(self, masks):
        for mask in masks:
            self.pieces[mask | 1] = send_xor(self.pieces[mask], "blk", 1)

    def both(self, after):
        masks = sorted(self.pieces)
        own = [self.pieces[m] for m in masks]
        if after is not None:
            ready = [lax.optimization_barrier((piece, after))[0] for piece in own]
        else:
            ready = own
        return masks, own + [send_xor(piece, "grp", 1) for piece in ready]


class Scatter:
    def __init__(self, keep, send, order):
        self.keep = keep
        self.came = send_xor(send, "blk", order[0])
        self.order = order[1:]

    def halve(self, chain):
        shape = (self.keep.shape[0] // 2,) + self.keep.shape[1:]
        self.keep, send = run(halve_kernel, [self.keep, self.came], [(shape, BF)] * 2, "halve", chain=chain)
        self.came = send_xor(send, "blk", self.order[0])
        self.order = self.order[1:]

    def total(self):
        return self.keep[0].astype(F32) + self.came[0].astype(F32)


def sum_axis(block, axis, masks):
    for mask in masks:
        block = block + send_xor(block, axis, mask)
    return block


def fold_share(block, width):
    rows = block.shape[0]
    return jnp.moveaxis(block.reshape(rows, -1, width), 1, 0).reshape(-1, width)


def unfold_shares(columns, shares, feat):
    width = columns.shape[1]
    blocks = columns.reshape(shares, feat // width, -1, width)
    return jnp.moveaxis(blocks, 1, 2).reshape(-1, feat)


def stream(rows, grad_rows, shape, hid, weights, chain, result):
    half, feat = shape
    width = feat // 4
    lse_rows = -(-(2 * width // HEAD) // 8) * 8

    def stage(body, operands, outs, name, layer=None):
        return run(body, operands, outs, name, chain=chain, unread=result["unread"].get((name, layer), ()))

    def over_x(near):
        return [near, send_xor(near, "grp", 2)]

    def over_core(pieces):
        return [send_xor(piece, "grp", 1) for piece in pieces]

    wide, short = ((half, feat), F32), ((half, feat), BF)
    projected = [((2, half, 2 * width), BF), ((2, half, width), BF)]
    pieces = 4 * [((half, width), BF)]
    hidden_shape = ((2, half, hid), BF)
    sums_shape = ((8, feat), F32)
    kept = []
    for layer in range(LAYERS):
        w = weights[layer]
        if layer == 0:
            kv, q = stage(lambda *r: qkv_kernel(layer, *r), [rows, *w["qkv"], *w["bias"]], projected, "qkv")
        kv_far = send_xor(kv, "blk", 1)
        yield "qkv", layer
        chosen = list(stage(lambda *r: choose_kernel(*r[:3], *r[4:]), [kv, kv_far, w["far"], w["vec"]], pieces, "choose", layer))
        chosen += over_core(chosen)
        near, mixed, lse, used = stage(
            attend_kernel, [q] + chosen + [*w["out"]],
            [short, saved(((2, half, width), BF)), ((lse_rows, half), F32), ((4, 2 * half, width), BF)], "attend")
        branch = over_x(near)
        yield "attend", layer
        resid_one, hidden, act, slope, near = stage(
            lambda *r: feed_kernel(layer, *r),
            branch + [in_hbm(b) for b in [rows, w["vec"]] + w["up"] + w["down"] + w["bias"]],
            [wide, saved(short), saved(hidden_shape), hidden_shape, short], "feed", layer)
        branch = over_x(near)
        yield "feed", layer
        before = (rows, q, used, lse, mixed, resid_one, hidden, act, slope)
        if layer < LAYERS - 1:
            after = weights[layer + 1]
            resid_two, rows, kv, q = stage(
                lambda *r: norm_two_qkv_kernel(layer, *r),
                branch + [resid_one, w["vec"], *after["qkv"], *after["bias"]],
                [wide, short] + projected, "norm_two_qkv")
        else:
            resid_two, rows = stage(lambda *r: norm_two_kernel(layer, *r), branch + [resid_one, w["vec"]],
                                    [wide, short], "norm_two")
        result["outputs"].append(rows[:half // 2])
        kept.append(before + (resid_two,))

    grads = [grad_rows]
    for layer in reversed(range(LAYERS)):
        w = weights[layer]
        rows, q, used, lse, mixed, resid_one, hidden, act, slope, resid_two = kept[layer]
        d_two, feed, sums_two, d_pre, g_up, near = stage(
            lambda *r: back_feed_kernel(layer, len(grads), *r),
            grads + [resid_two, w["vec"], *w["up"], *w["down"], slope],
            [wide, short, sums_shape, hidden_shape, ((2, 1, hid), F32), short], "back_feed")
        result["feed"][layer] = [hidden, feed, d_pre, act]
        branch = over_x(near)
        yield "back_feed", layer
        d_one, branch, sums_one, dq, stay, *go = stage(
            lambda *r: back_attend_kernel(layer, *r),
            branch + [d_two, resid_one, w["vec"], *w["out"], q, used, lse],
            [wide, short, sums_shape, ((2, half, width), BF), ((2, half, 2 * width), F32)] + pieces, "back_attend")
        dkv, = stage(add_crossed_kernel, [stay] + over_core(go), [((2, half, 2 * width), BF)], "add_crossed")
        dkv_far = send_xor(dkv, "blk", 1)
        yield "back_attend", layer
        outs = [short] if layer else [((half // 2, feat), F32), ((half // 2, feat), BF)]
        d_qkv, g_qkv, *outs = stage(
            back_qkv_kernel, [dq, dkv, dkv_far, w["far"], *w["qkv"]],
            [((2, half, 3 * width), BF), ((2, 1, 3 * width), F32)] + outs, "back_qkv")
        result["attend"][layer] = [rows, branch, d_qkv, mixed]
        result["smalls"][layer] = [sums_two, sums_one, g_up, g_qkv]
        if layer:
            grads = over_x(outs[0]) + [d_one]
        else:
            came = send_xor(outs[1], "grp", 2)
            result["grad"] = d_one[:half // 2] + outs[0] + came.astype(F32)
        yield "back_qkv", layer


def per_device(layer_input, w_query, w_key, w_value, b_query, b_value, w_out, b_out, gain_one,
               bias_one, w_up, b_up, w_down, b_down, gain_two, bias_two, head_table, grad_top):
    blk_count = lax.axis_size("blk")
    grp_count = lax.axis_size("grp")
    grp = lax.axis_index("grp")
    blk = lax.axis_index("blk")
    feat = w_out.shape[2]
    share_rows = w_query.shape[1]
    width = w_query.shape[2]
    heads = width // HEAD
    hid = w_up.shape[2]
    per = b_out.shape[1]
    up_per = b_up.shape[1]
    blk_masks = [1 << bit for bit in bits_of(blk_count)[::-1]]
    packed = blk_count == 8 and share_rows % 32 == 0 and per % 8 == 0
    block_own = blk % NB
    target = jnp.where(block_own == 0, head_table[:, :, 0], head_table[:, :, 1])
    far = (target != block_own).astype(F32)
    far = jnp.stack([lax.dynamic_slice_in_dim(far, g * heads, heads, 1) for g in (grp, grp ^ 1)], 1)
    far_cols = jnp.broadcast_to(far[:, :, None, :, None], (LAYERS, 2, 2, heads, HEAD)).reshape(LAYERS, 2, 1, 2 * width)

    start = layer_input[:, 0]
    row_top = jnp.concatenate([start, send_xor(start, "grp", 2)], 1)
    grad_start = grad_top[:, 0]
    grad_rows = jnp.concatenate([grad_start, send_xor(grad_start, "grp", 2)], 1)

    micros = range(layer_input.shape[0])
    count = len(micros)
    chain = Order()
    results = [{"outputs": [], "feed": {}, "attend": {}, "smalls": {}, "unread": {}} for _ in micros]
    weights = [{"far": pick(far_cols, layer)} for layer in range(LAYERS)]
    where = (jnp.stack([blk, grp]).astype(jnp.int32), pl.BlockSpec((2,), lambda i: (0,), memory_space=pltpu.SMEM))
    grad_feed, grad_attend, tiny = {}, {}, []
    smalls = [b_query, b_value, b_out, gain_one, bias_one, b_down, gain_two, bias_two]
    small_rows = len(smalls) * LAYERS
    vec_shape = (small_rows, feat)

    def factors(name, layer):
        return [f for r in results for f in r[name][layer]]

    chunks = blk_count if packed else 1

    def sum_feed(layer):
        rest = [((2, feat // chunks, hid), BF)] * chunks
        grad_feed[layer] = run(lambda *r: grad_feed_kernel(count, chunks, *r), factors("feed", layer),
                               [((2, feat, hid), BF)] + rest, "grad_feed", 16, chain=chain)

    def sum_attend(layer):
        vectors = tiny if packed and layer == 0 else []
        high = feat + (len(vectors) // 2) * blk_count * 8 * LAYERS
        rest = [((high // chunks, feat), BF)] * chunks
        grad_attend[layer] = run(lambda *r: grad_attend_kernel(count, blk_count, len(vectors) // 2, *r),
                                 factors("attend", layer) + vectors, [((high, feat), BF)] + rest, "grad_attend", 16,
                                 chain=chain)

    def add_small():
        sums = sum([r["smalls"][layer] for layer in range(LAYERS) for r in results], [])
        tiny.extend(run(lambda *r: small_kernel(LAYERS, *r), sums, [((8 * LAYERS, feat), F32)] * 2, "small",
                        chain=chain))

    if packed:
        def pack(layer, *more, scratch=(), order=None):
            rows = share_rows + (small_rows if more else 0)
            return run(pack_kernel, [pick(a, layer) for a in (w_key, w_value, w_query, w_out)] + list(more),
                       [((rows, feat), BF)], "pack", 60, scratch, order)[0]

        first = Gather(pack(0, *smalls, b_up, scratch=[pltpu.VMEM(vec_shape, F32)]))
        first.step([1, 2, 4, 6], None)
        first.over_y([2, 4, 6])
        early, attend_share, late = run(
            shares_kernel, [pick(a, 1) for a in (w_key, w_value, w_query, w_out)]
            + [pick(a, layer) for layer in range(LAYERS) for a in (w_up, w_down)],
            [((2, share_rows, feat), BF), ((share_rows, feat), BF), ((2, share_rows, feat), BF)], "shares", 60)
        gathered = {"early": lax.all_gather(early, "blk", axis=1, tiled=True)}
        lanes = jnp.arange(feat)[None, :]
        spread = (lanes % per == jnp.arange(per)[:, None]).astype(BF)
        up_spread = (lanes % up_per == jnp.arange(up_per)[:, None]).astype(BF)

        def start_feed():
            block = lax.optimization_barrier((late, chain.token))[0]
            gathered["late"] = lax.all_gather(block, "blk", axis=1, tiled=True)

        def over_cores(name):
            block = gathered[name]
            return [block, send_xor(lax.optimization_barrier((block, chain.token))[0], "grp", 1)]

        def start_attend():
            flow = Gather(attend_share)
            flow.step([1, 2, 4, 6], chain.token)
            flow.over_y([2, 4, 6])
            gathered["attend1"] = flow
            results[1]["unread"]["choose", 0] = [flow.pieces[mask] for mask in (1, 2, 4, 6)]
            results[1]["unread"]["feed", 0] = [flow.pieces[mask] for mask in (3, 5, 7)]

        def have_early():
            both = over_cores("early")
            weights[0].update(up=[pick(b, 0) for b in both], down=[pick(b, 1) for b in both])

        def have_attend():
            masks, pieces = gathered["attend1"].both(chain.token)
            outs = run(lambda *r: assemble_kernel(masks, per, up_per, *r), pieces + [where],
                       [((feat, 3 * width), BF)] * 2 + [((width, feat), BF)] * 2, "assemble",
                       scratch=[pltpu.VMEM((width, feat), F32)], chain=chain)
            weights[1].update(qkv=outs[:2], out=outs[2:])

        def have_late():
            both = over_cores("late")
            weights[1].update(up=[pick(b, 0) for b in both], down=[pick(b, 1) for b in both])

        sums_of = {}

        def scatter(key, grads, part=None):
            here, *away = grads
            came = [send_xor(piece, "grp", 1) for piece in away]
            if part is not None:
                groups, depth = [pick(a, part) for a in [here] + came], 1
            else:
                groups, depth = [here] + came, 2 if here.ndim == 3 else 1
            outs = [((blk_count // 2, depth, here.shape[-2] // blk_count, feat), BF)] * 2
            keep, send = run(lambda *r: split_kernel(blk_count, ORDERS[key], 1, 0, *r), groups + [where], outs, "split",
                             16, chain=chain)
            sums_of[key] = Scatter(keep, send, ORDERS[key])

        steps = {
            "A": lambda: sum_feed(1), "B": lambda: scatter("A", grad_feed[1]),
            "C": lambda: sum_attend(1), "D": lambda: scatter("C", grad_attend[1]),
            "a": lambda: sum_feed(0), "b": lambda: scatter("a", grad_feed[0], 0), "e": lambda: scatter("e", grad_feed[0], 1),
            "c": lambda: sum_attend(0), "d": lambda: scatter("c", grad_attend[0]), "m": add_small,
        }
        for letter, key in zip("FGfhg", "ACaec"):
            steps[letter] = lambda key=key: sums_of[key].halve(chain)

        masks, pieces = first.both(None)
        outs = run(lambda *r: assemble_kernel(masks, per, up_per, *r), pieces + [where, spread, up_spread],
                   [((feat, 3 * width), BF)] * 2 + [((width, feat), BF)] * 2 + [(vec_shape, BF)] + [((8, feat), F32)] * 2,
                   "assemble", scratch=[pltpu.VMEM((width, feat), F32)], chain=chain)
        weights[0].update(qkv=outs[:2], out=outs[2:4])
        table, *biases = outs[4:]
        vec = table + send_xor(table, "grp", 2)
        after = {
            ("qkv", 0, 1): start_attend,
            ("attend", 0, 1): lambda: (have_early(), start_feed()),
            ("feed", 0, 1): have_attend,
            ("attend", 1, 1): have_late,
        }
    else:
        table = jnp.zeros(vec_shape, BF)
        rows = jnp.stack(smalls).reshape(small_rows, per)
        table = lax.dynamic_update_slice(table, rows, (0, (grp * blk_count + blk) * per))
        spots = jnp.zeros((8, feat), BF)
        spots = lax.dynamic_update_slice(spots, b_query, (0, 2 * width + blk * per))
        spots = lax.dynamic_update_slice(spots, b_value, (LAYERS, width + blk * per))
        spots = lax.dynamic_update_slice(spots, b_up, (2 * LAYERS, blk * up_per))
        table = sum_axis(table, "blk", blk_masks)
        spots = sum_axis(spots, "blk", blk_masks).astype(F32)
        bias = jnp.zeros((8, feat), F32)
        bias = bias.at[:LAYERS].set(spots[:LAYERS] + spots[LAYERS:2 * LAYERS])
        bias = bias.at[LAYERS:2 * LAYERS].set(spots[2 * LAYERS:3 * LAYERS])
        for layer in range(LAYERS):
            block = jnp.concatenate([w_key[layer], w_value[layer], w_query[layer],
                                     fold_share(w_out[layer], width)], 1)
            block = lax.all_gather(block, "blk", axis=0, tiled=True)
            pair = [block, send_xor(block, "grp", 1)]
            block = lax.all_gather(jnp.stack([w_up[layer], w_down[layer]]), "blk", axis=1, tiled=True)
            both = [block, send_xor(block, "grp", 1)]
            weights[layer].update(qkv=[b[:, :3 * width] for b in pair],
                                  out=[unfold_shares(b[:, 3 * width:], blk_count, feat) for b in pair],
                                  up=[pick(b, 0) for b in both], down=[pick(b, 1) for b in both])
        biases = [bias, send_xor(bias, "grp", 1)]
        vec = sum_axis(table, "grp", [2, 1])
        after = {}
        for layer in range(LAYERS):
            after["back_feed", layer, count - 1] = lambda layer=layer: sum_feed(layer)
            after["back_qkv", layer, count - 1] = lambda layer=layer: sum_attend(layer)

    vec = vec.astype(F32)
    for w in weights:
        w.update(vec=vec, bias=biases)
    streams = [stream(pick(row_top, m), pick(grad_rows, m), row_top.shape[1:], hid, weights, chain, results[m])
               for m in micros]
    done = False
    while not done:
        for m, one in enumerate(streams):
            label = next(one, None)
            done = label is None
            if not done and label + (m,) in after:
                after[label + (m,)]()
            if not done and packed:
                for letter in SLOTS.get(label + (m,), ""):
                    steps[letter]()
    if packed:
        late, up, down, attend, attend1 = [sums_of[key].total() for key in "AaecC"]
        grad_feed = {0: jnp.concatenate([up, down]), 1: late}
        grad_attend = {0: attend[0, :share_rows], 1: attend1[0]}
    else:
        for dim, sums in ((1, grad_feed), (0, grad_attend)):
            for layer in sums:
                block = sums[layer][0] + send_xor(sums[layer][1], "grp", 1)
                sums[layer] = lax.psum_scatter(block, "blk", scatter_dimension=dim, tiled=True).astype(F32)

    if packed:
        tiny = attend[0, share_rows:]
    else:
        add_small()
        tiny = sum_axis(tiny[0] + send_xor(tiny[1], "grp", 1), "blk", blk_masks)
    tiny = tiny.reshape(LAYERS, 8, feat)
    six = tiny[:, :SMALLS]
    six = lax.dynamic_slice_in_dim(six, (grp * blk_count + blk) * per, per, 2)
    g_b_up = lax.dynamic_slice_in_dim(tiny[:, 6], blk * up_per, up_per, 1)
    g_b_value = lax.dynamic_slice_in_dim(tiny[:, 7], width + blk * per, per, 1)
    g_b_query = lax.dynamic_slice_in_dim(tiny[:, 7], 2 * width + blk * per, per, 1)
    feeds = jnp.stack([grad_feed[layer] for layer in range(LAYERS)])
    attends = jnp.stack([grad_attend[layer] for layer in range(LAYERS)])
    g_out = jnp.stack([unfold_shares(attends[layer, :, 3 * width:], 1, feat) for layer in range(LAYERS)])
    return (
        jnp.stack([jnp.stack([r["outputs"][layer] for r in results]) for layer in range(LAYERS)])[:, :, None],
        jnp.stack([r["grad"] for r in results])[:, None],
        attends[:, :, 2 * width:3 * width],
        attends[:, :, :width],
        attends[:, :, width:2 * width],
        g_b_query,
        g_b_value,
        g_out,
        six[:, 0],
        six[:, 1],
        six[:, 2],
        feeds[:, 0],
        g_b_up,
        feeds[:, 1],
        six[:, 3],
        six[:, 4],
        six[:, 5],
    )


def solution(mesh):
    rows = P(None, "blk", "grp", None)
    cols = P(None, "blk", "grp")
    both = P(None, ("grp", "blk"))
    tall = P(None, ("grp", "blk"), None)
    return jax.shard_map(
        per_device,
        mesh=mesh,
        in_specs=(rows, cols, cols, cols, both, both, tall, both, both, both, cols, both, tall,
                  both, both, both, P(), rows),
        out_specs=(P(None, None, "blk", "grp", None), rows, cols, cols, cols, both, both, tall,
                   both, both, both, cols, both, tall, both, both, both),
        check_vma=False,
    )
```

```python
import jax
import jax.numpy as jnp
from jax import lax
from jax.experimental import pallas as pl
from jax.experimental.pallas import tpu as pltpu
from jax.sharding import PartitionSpec as P

HEAD = 64
NB = 2
LAYERS = 2
EPS = 1e-05
SCALE = HEAD ** -0.5
BF = jnp.bfloat16
F32 = jnp.float32
SMALLS = 6
HINT = 200000000
SLOTS = {
    ("back_feed", 1, 1): "A", ("back_qkv", 1, 0): "B", ("back_feed", 0, 0): "C", ("back_feed", 0, 1): "FD",
    ("back_attend", 0, 1): "a", ("back_qkv", 0, 0): "GF", ("back_qkv", 0, 1): "mcdbeghfGghf",
}
ORDERS = {"A": [2, 4, 1], "C": [2, 4, 1], "a": [1, 2, 4], "e": [2, 4, 1], "c": [1, 2, 4]}
KEEP = True
WEIGHTS = True
WEIGHT = {"qkv": .9, "choose": .5, "attend": 2.5, "feed": 2.6, "norm_two_qkv": 1.6, "norm_two": .6, "back_feed": 3.6,
          "back_attend": 5, "add_crossed": .6, "back_qkv": 1.2, "grad_feed": 5.5, "grad_attend": 3.7, "split": 1.8,
          "halve": .8, "assemble": 1.8, "place": 2, "pack": 1.2, "small": .8}
B_OUT, GAIN_ONE, BIAS_ONE, B_DOWN, GAIN_TWO, BIAS_TWO = [LAYERS * (2 + i) for i in range(SMALLS)]


def send_xor(block, axis, mask):
    count = lax.axis_size(axis)
    return lax.ppermute(block, axis, [(i, i ^ mask) for i in range(count)])


def dot(left, right):
    return lax.dot_general(left, right, (((1,), (0,)), ((), ())), preferred_element_type=F32)


def dot_tn(left, right):
    return lax.dot_general(left, right, (((0,), (0,)), ((), ())), preferred_element_type=F32)


def dot_nt(left, right):
    return lax.dot_general(left, right, (((1,), (1,)), ((), ())), preferred_element_type=F32)


def pick(array, index):
    tail = array.shape[1:]
    return array, pl.BlockSpec((None,) + tail, lambda i: (index,) + (0,) * len(tail))


def saved(out):
    return out + ("saved",)


def in_hbm(operand):
    array, spec = operand if isinstance(operand, tuple) else whole(operand)
    return (pltpu.with_memory_space_constraint(array, pltpu.HBM) if WEIGHTS else array), spec


def whole(array):
    return array, pl.BlockSpec(array.shape, lambda i: (0,) * array.ndim)


class Order:
    token = None
    on = True


def run(body, operands, outs, name, mib=16, scratch=(), chain=None, unread=()):
    operands = [o if isinstance(o, tuple) else whole(o) for o in operands]
    reads = len(operands)
    outs = list(outs)
    writes = len(outs)
    extra = []
    if chain is not None and chain.token is not None:
        extra = [(chain.token, pl.BlockSpec(memory_space=pl.ANY))]
    extra = extra + [(array, pl.BlockSpec(memory_space=pl.ANY)) for array in unread]
    if chain is not None and not chain.on:
        chain = None
    if chain is not None:
        outs.append(((8, 128), F32))
    kernel_outs = [pltpu.HBM(*o[:2]) if len(o) > 2 and KEEP else jax.ShapeDtypeStruct(*o[:2]) for o in outs]
    out_shape = [jax.ShapeDtypeStruct(*o[:2]) for o in outs]

    def trimmed(*refs):
        results = refs[reads + len(extra):]
        if chain is not None:
            results[writes][...] = jnp.zeros((8, 128), F32)
            results = results[:writes] + results[writes + 1:]
        body(*refs[:reads], *results)

    results = pl.pallas_call(
        trimmed,
        out_shape=kernel_outs,
        grid=(1,),
        in_specs=[spec for _, spec in operands + extra],
        out_specs=[pl.BlockSpec(o.shape, lambda i, nd=len(o.shape): (0,) * nd) for o in out_shape],
        scratch_shapes=list(scratch),
        compiler_params=pltpu.CompilerParams(vmem_limit_bytes=mib * 2 ** 20),
        cost_estimate=pl.CostEstimate(flops=int(HINT * WEIGHT.get(name, 1)), bytes_accessed=1, transcendentals=0),
        name=name,
    )(*[array for array, _ in operands + extra])
    if chain is not None:
        chain.token = results[writes]
    return results[:writes]


def deal(where, chunk, order, keep, send, index, value):
    distance = jnp.bitwise_xor(where[0], chunk)
    spot = 0
    for bit in order[1:]:
        spot = spot * 2 + (jnp.bitwise_and(distance, bit) // bit)
    gone = jnp.bitwise_and(distance, order[0]) != 0

    @pl.when(gone)
    def _():
        send[(spot,) + index] = value

    @pl.when(jnp.logical_not(gone))
    def _():
        keep[(spot,) + index] = value


def halve_kernel(kept, came, keep, send):
    count = keep.shape[0]
    for i in range(count):
        keep[i] = (kept[i].astype(F32) + came[i].astype(F32)).astype(BF)
        send[i] = (kept[count + i].astype(F32) + came[count + i].astype(F32)).astype(BF)


def unit_of(resid):
    middle = jnp.mean(resid, -1, keepdims=True)
    center = resid - middle
    spread = jnp.mean(center * center, -1, keepdims=True)
    root = lax.rsqrt(spread + EPS)
    return center * root, root


def summed(near, came, part):
    half = near.shape[0] // 2
    here = near[pl.ds(part * half, half), :].astype(F32)
    return here + came[pl.ds((1 - part) * half, half), :].astype(F32)


def parts_of(rows):
    return [(part, pl.ds(part * (rows // 2), rows // 2)) for part in range(2)]


def at_row(vec, row):
    return vec[pl.ds(row, 1), :]


def project(layer, at, rows, weights, biases, kv_out, q_out):
    split = kv_out.shape[2]
    cols = pl.ds(0, split + q_out.shape[2])
    for g in range(2):
        acc = dot(rows, weights[g][:, cols]) + biases[g][pl.ds(layer, 1), cols]
        kv_out[g, at, :] = acc[:, :split].astype(BF)
        q_out[g, at, :] = (acc[:, split:].astype(BF) * SCALE).astype(BF)


def qkv_kernel(layer, rows, w_own, w_other, b_own, b_other, kv_out, q_out):
    for _, at in parts_of(rows.shape[0]):
        project(layer, at, rows[at, :], (w_own, w_other), (b_own, b_other), kv_out, q_out)


def norm_two_rows(layer, part, at, near, came, resid_one, vec, resid_out, out):
    unit, _ = unit_of(resid_one[at, :])
    hidden = unit * at_row(vec, layer + GAIN_ONE) + at_row(vec, layer + BIAS_ONE)
    resid = hidden + summed(near, came, part) + at_row(vec, layer + B_DOWN)
    resid_out[at, :] = resid
    unit, _ = unit_of(resid)
    out[at, :] = (unit * at_row(vec, layer + GAIN_TWO) + at_row(vec, layer + BIAS_TWO)).astype(BF)


def norm_two_kernel(layer, near, came, resid_one, vec, resid_out, out):
    for part, at in parts_of(out.shape[0]):
        norm_two_rows(layer, part, at, near, came, resid_one, vec, resid_out, out)


def norm_two_qkv_kernel(layer, near, came, resid_one, vec, w_own, w_other, b_own, b_other,
                        resid_out, out, kv_out, q_out):
    for part, at in parts_of(out.shape[0]):
        norm_two_rows(layer, part, at, near, came, resid_one, vec, resid_out, out)
        project(layer + 1, at, out[at, :], (w_own, w_other), (b_own, b_other), kv_out, q_out)


def choose_kernel(kv, kv_far, far, *outs):
    width = outs[0].shape[1]
    for g in range(2):
        for k in range(2):
            cols = pl.ds(k * width, width)
            outs[2 * g + k][...] = jnp.where(
                far[g, :, cols] > 0.5, kv_far[g, :, cols].astype(F32), kv[g, :, cols].astype(F32)).astype(BF)


def attend_kernel(*refs):
    q, out_own, out_other, near, mixed, lse, used = refs[:1] + refs[9:]
    pieces, crossed = refs[1:5], refs[5:9]
    _, length, width = q.shape
    heads = width // HEAD
    for g in range(2):
        for k in range(2):
            used[2 * g + k, pl.ds(0, length), :] = pieces[2 * g + k][...]
            used[2 * g + k, pl.ds(length, length), :] = crossed[2 * (1 - g) + k][...]
        for head in range(heads):
            cols = pl.ds(head * HEAD, HEAD)
            key, value = used[2 * g, :, cols], used[2 * g + 1, :, cols]
            scores = dot_nt(key, q[g, :, cols])
            high = jnp.max(scores, 0, keepdims=True)
            expo = jnp.exp(scores - high)
            total = jnp.sum(expo, 0, keepdims=True)
            lse[pl.ds(g * heads + head, 1), :] = high + jnp.log(total)
            probs = (expo * (1.0 / total)).astype(BF)
            mixed[g, :, cols] = dot_tn(probs, value).astype(BF)
    near[...] = (dot(mixed[0], out_own[...]) + dot(mixed[1], out_other[...])).astype(BF)


def feed_kernel(layer, near, came, inputs, vec, up_own, up_other, down_own, down_other, b_own, b_other,
                resid_out, hidden_out, act_out, slope_out, near_out):
    ups, downs, biases = (up_own, up_other), (down_own, down_other), (b_own, b_other)
    for part, at in parts_of(near.shape[0]):
        resid = inputs[at, :].astype(F32) + summed(near, came, part) + at_row(vec, layer + B_OUT)
        resid_out[at, :] = resid
        unit, _ = unit_of(resid)
        hidden_out[at, :] = (unit * at_row(vec, layer + GAIN_ONE) + at_row(vec, layer + BIAS_ONE)).astype(BF)
        branch = 0.0
        for g in range(2):
            u = dot(hidden_out[at, :], ups[g][...]) + biases[g][pl.ds(LAYERS + layer, 1), :]
            cdf = 0.5 * (1.0 + lax.erf(u * (0.5 ** 0.5)))
            density = jnp.exp(-0.5 * u * u) * ((2.0 * jnp.pi) ** -0.5)
            act = (u * cdf).astype(BF)
            act_out[g, at, :] = act
            slope_out[g, at, :] = (cdf + u * density).astype(BF)
            branch = branch + dot(act, downs[g][...])
        near_out[at, :] = branch.astype(BF)


def norm_back(grad, resid, gain):
    unit, root = unit_of(resid)
    scaled = grad * gain
    mean_e = jnp.mean(scaled, -1, keepdims=True)
    mean_en = jnp.mean(scaled * unit, -1, keepdims=True)
    pulled = root * (scaled - mean_e - unit * mean_en)
    return pulled, (jnp.sum(grad * unit, 0, keepdims=True), jnp.sum(grad, 0, keepdims=True),
                    jnp.sum(pulled, 0, keepdims=True))


def back_norm(grads, gain_row, resid, vec, full_out, short_out, sums_out):
    sums_out[...] = jnp.zeros(sums_out.shape, F32)
    for part, at in parts_of(resid.shape[0]):
        grad = grads[-1][at, :].astype(F32)
        if len(grads) > 1:
            grad = grad + summed(grads[0], grads[1], part)
        pulled, sums = norm_back(grad, resid[at, :], at_row(vec, gain_row))
        full_out[at, :] = pulled
        short_out[at, :] = pulled.astype(BF)
        for index, s in enumerate(sums):
            sums_out[pl.ds(index, 1), :] += s


def back_feed_kernel(layer, grads, *refs):
    resid, vec, up_own, up_other, down_own, down_other, slope = refs[grads:grads + 7]
    full_out, short_out, sums_out, pre_out, bias_out, near_out = refs[grads + 7:]
    back_norm(refs[:grads], layer + GAIN_TWO, resid, vec, full_out, short_out, sums_out)
    ups, downs = (up_own, up_other), (down_own, down_other)
    totals = [0.0, 0.0]
    for _, at in parts_of(resid.shape[0]):
        branch = 0.0
        for g in range(2):
            pre = (dot_nt(short_out[at, :], downs[g][...]) * slope[g, at, :].astype(F32)).astype(BF)
            pre_out[g, at, :] = pre
            totals[g] = totals[g] + jnp.sum(pre.astype(F32), 0, keepdims=True)
            branch = branch + dot_nt(pre, ups[g][...])
        near_out[at, :] = branch.astype(BF)
    for g in range(2):
        bias_out[g] = totals[g]


def back_attend_kernel(layer, *refs):
    grads, (resid, vec, out_own, out_other, q, used, lse) = refs[:3], refs[3:10]
    full_out, short_out, sums_out, dq_out, stay = refs[10:15]
    go = refs[15:19]
    back_norm(grads, layer + GAIN_ONE, resid, vec, full_out, short_out, sums_out)
    _, length, width = q.shape
    heads = width // HEAD
    for g in range(2):
        d_mixed_all = dot_nt(short_out[...], (out_own, out_other)[g][...]).astype(BF)
        for head in range(heads):
            cols = pl.ds(head * HEAD, HEAD)
            key, value = used[2 * g, :, cols], used[2 * g + 1, :, cols]
            query = q[g, :, cols]
            d_mixed = d_mixed_all[:, head * HEAD:(head + 1) * HEAD]
            probs = jnp.exp(dot_nt(key, query) - lse[pl.ds(g * heads + head, 1), :])
            d_probs = dot_nt(value, d_mixed)
            inner = jnp.sum(d_probs * probs, 0, keepdims=True)
            d_scores = (probs * (d_probs - inner)).astype(BF)
            d_value = dot(probs.astype(BF), d_mixed)
            d_key = dot(d_scores, query)
            dq_out[g, :, cols] = (dot_tn(d_scores, key) * SCALE).astype(BF)
            for k, grad in enumerate((d_key, d_value)):
                stay[g, :, pl.ds(k * width + head * HEAD, HEAD)] = grad[:length]
                go[2 * g + k][:, cols] = grad[length:].astype(BF)


def add_crossed_kernel(*refs):
    stay, out = refs[0], refs[-1]
    width = refs[1].shape[1]
    for g in range(2):
        for k in range(2):
            cols = pl.ds(k * width, width)
            out[g, :, cols] = (stay[g, :, cols] + refs[1 + 2 * (1 - g) + k][...].astype(F32)).astype(BF)


def back_qkv_kernel(dq, dkv, dkv_far, far, w_own, w_other, all_out, bias_out, *outs):
    split = dkv.shape[2]
    cols = pl.ds(0, all_out.shape[2])
    for g in range(2):
        all_out[g, :, pl.ds(0, split)] = jnp.where(
            far[g] > 0.5, dkv_far[g].astype(F32), dkv[g].astype(F32)).astype(BF)
        all_out[g, :, pl.ds(split, dq.shape[2])] = dq[g]
        bias_out[g] = jnp.sum(all_out[g].astype(F32), 0, keepdims=True)
    for part, at in parts_of(dq.shape[1]):
        branch = dot_nt(all_out[0, at, :], w_own[:, cols]) + dot_nt(all_out[1, at, :], w_other[:, cols])
        if len(outs) == 1:
            outs[0][at, :] = branch.astype(BF)
        else:
            outs[part][...] = branch.astype(outs[part].dtype)


def grad_feed_kernel(count, shares, *refs):
    here, away = refs[4 * count], refs[4 * count + 1:]
    feat = refs[0].shape[1]
    rows = feat // shares
    tile = feat // 2
    for g in range(2):
        for t in range(2):
            cols = pl.ds(t * tile, tile)
            up, down = 0.0, 0.0
            for m in range(count):
                hid, feed, pre, act = refs[4 * m:4 * m + 4]
                up = up + dot_tn(hid[:, cols], pre[g])
                down = down + dot_tn(act[g, :, cols], feed[...])
            for k, grad in enumerate((up, down)):
                if g == 0 or len(away) == 1:
                    (here, away[0])[g][k, cols, :] = grad.astype(BF)
                    continue
                for b in range(shares // 2):
                    away[t * (shares // 2) + b][k] = grad[b * rows:(b + 1) * rows].astype(BF)


def fold(block, width):
    return jnp.concatenate([block[:, c:c + width] for c in range(0, block.shape[1], width)], 0)


def unfold(block, rows):
    return jnp.concatenate([block[c:c + rows] for c in range(0, block.shape[0], rows)], 1)


def grad_attend_kernel(count, shares, vectors, *refs):
    smalls = refs[4 * count:4 * count + 2 * vectors]
    here, *away = refs[4 * count + 2 * vectors:]
    feat = refs[0].shape[1]
    split = refs[2].shape[2]
    width = split // 3
    rows, thin = feat // shares, width // shares
    stride = here.shape[0] // shares
    for g in range(2):
        acc, out = 0.0, 0.0
        for m in range(count):
            inputs, branch, d_qkv, mixed = refs[4 * m:4 * m + 4]
            acc = acc + dot_tn(inputs[...], d_qkv[g])
            out = out + dot_tn(mixed[g], branch[...])
        for b in range(shares):
            if g == 0 or len(away) == 1:
                ref, first = (here, away[0])[g], b * stride
            else:
                ref, first = away[b], 0
            at = pl.ds(first, rows)
            if vectors:
                ref[pl.ds(first + rows, stride - rows), :] = smalls[g][...].astype(BF)
            ref[at, pl.ds(0, split)] = acc[b * rows:(b + 1) * rows].astype(BF)
            ref[at, pl.ds(split, width)] = fold(out[b * thin:(b + 1) * thin, :], width).astype(BF)


def split_kernel(shares, order, feeds, attends, *refs):
    where, keep, send = refs[-3:]
    groups = [refs[1 + (1 + shares) * n - 1:(1 + shares) * (n + 1)] for n in range(feeds + attends)]
    for b in range(shares):
        spot = 0
        for here, *came in groups:
            rows = here.shape[-2] // shares
            for index in ((0,), (1,)) if len(here.shape) == 3 else ((),):
                mine = here[index + (pl.ds(b * rows, rows), slice(None))].astype(F32)
                value = mine + came[b][index + (slice(None), slice(None))].astype(F32)
                deal(where, b, order, keep, send, (spot,), value.astype(BF))
                spot += 1


def unfold_kernel(shares, *refs):
    for ref, out in zip(refs[:2], refs[2:]):
        width, feat = out.shape
        rows, thin = feat // shares, width // shares
        blocks = [unfold(ref[pl.ds(b * rows, rows), pl.ds(3 * width, width)].astype(F32), thin) for b in range(shares)]
        out[...] = jnp.concatenate(blocks, 0).astype(BF)


def pack_kernel(*refs):
    key, value, query, out = refs[:4]
    rows, width = key.shape
    payload = refs[-1]
    if len(refs) > 5:
        payload, small = refs[-2:]
    at = pl.ds(0, rows)
    for index, ref in enumerate((key, value, query)):
        payload[at, pl.ds(index * width, width)] = ref[...]
    payload[at, pl.ds(3 * width, width)] = fold(out[...].astype(F32), width).astype(BF)
    if len(refs) > 5:
        small[...] = jnp.zeros(small.shape, F32)
        for index, ref in enumerate(refs[4:-3]):
            small[pl.ds(LAYERS * index, LAYERS), pl.ds(0, ref.shape[1])] = ref[...].astype(F32)
        up = refs[-3]
        small[pl.ds(0, LAYERS), pl.ds(128, up.shape[1])] = up[...].astype(F32)
        payload[pl.ds(rows, small.shape[0]), :] = small[...].astype(BF)


def shares_kernel(key, value, query, out, up_early, down_early, up_late, down_late, early, attend, late):
    early[0] = up_early[...]
    early[1] = down_early[...]
    pack_kernel(key, value, query, out, attend)
    late[0] = up_late[...]
    late[1] = down_late[...]


def assemble_kernel(masks, per, up_per, *refs):
    count = len(masks)
    where = refs[2 * count]
    small_outs = len(refs) - 2 * count - 1 - 5 > 0
    if small_outs:
        spread, up_spread = refs[2 * count + 1:2 * count + 3]
        outs, (table, bias_own, bias_other), scratch = refs[2 * count + 3:-4], refs[-4:-1], refs[-1]
    else:
        outs, scratch = refs[2 * count + 1:-1], refs[-1]
    blk, grp = where[0], where[1]
    width, feat = outs[2].shape
    rows, thin = feat // count, width // count
    if small_outs:
        lane = lax.broadcasted_iota(jnp.int32, table.shape, 1)
        row = lax.broadcasted_iota(jnp.int32, table.shape, 0)
        six = 0.0
    for g in range(2):
        projection, hidden = 0.0, 0.0
        for index, mask in enumerate(masks):
            ref = refs[g * count + index]
            b = jnp.bitwise_xor(blk, mask)
            outs[g][pl.ds(pl.multiple_of(b * rows, rows), rows), :] = ref[pl.ds(0, rows), pl.ds(0, 3 * width)]
            block = ref[pl.ds(0, rows), pl.ds(3 * width, width)].astype(F32)
            scratch[pl.ds(pl.multiple_of(b * thin, thin), thin), :] = unfold(block, thin)
            if not small_outs:
                continue
            small = ref[pl.ds(rows, table.shape[0]), :]
            spreaded = dot(small[:, :per], spread[...])
            at = lane - (jnp.bitwise_xor(grp, g) * count + b) * per
            six = six + jnp.where((at >= 0) & (at < per), spreaded, 0.0)
            at = lane - b * per - jnp.where(row < LAYERS, 2 * width, width)
            projection = projection + jnp.where((at >= 0) & (at < per), spreaded, 0.0)
            at = lane - b * up_per
            hidden = hidden + jnp.where((at >= 0) & (at < up_per), dot(small[:, 128:128 + up_per], up_spread[...]), 0.0)
        outs[2 + g][...] = scratch[...].astype(BF)
        if small_outs:
            bias = (bias_own, bias_other)[g]
            bias[...] = jnp.zeros(bias.shape, F32)
            bias[pl.ds(0, LAYERS), :] = projection[:LAYERS] + projection[LAYERS:2 * LAYERS]
            bias[pl.ds(LAYERS, LAYERS), :] = hidden[:LAYERS]
    if small_outs:
        table[...] = six.astype(BF)


def small_kernel(layers, *refs):
    out, other = refs[-2:]
    out[...] = jnp.zeros(out.shape, F32)
    other[...] = jnp.zeros(other.shape, F32)
    per_layer = (len(refs) - 2) // layers
    for layer in range(layers):
        mine = refs[layer * per_layer:(layer + 1) * per_layer]
        sets = [mine[i:i + 4] for i in range(0, per_layer, 4)]
        base = 8 * layer
        for row, (which, index) in enumerate(((1, 2), (1, 0), (1, 1), (0, 2), (0, 0), (0, 1))):
            total = sum(s[which][pl.ds(index, 1), :] for s in sets)
            out[pl.ds(base + row, 1), :] = total
            other[pl.ds(base + row, 1), :] = total
        cols = pl.ds(0, sets[0][3].shape[2])
        for g, ref in enumerate((out, other)):
            ref[pl.ds(base + 6, 1), :] = sum(s[2][g] for s in sets)
            ref[pl.ds(base + 7, 1), cols] = sum(s[3][g] for s in sets)


def bits_of(count):
    return list(range(count.bit_length() - 1))


class Gather:
    def __init__(self, share):
        self.pieces = {0: share}

    def step(self, bits, after):
        held = dict(self.pieces)
        for mask, piece in held.items():
            if after is not None:
                piece, _ = lax.optimization_barrier((piece, after))
            for bit in bits:
                self.pieces[mask | bit] = send_xor(piece, "blk", bit)

    def over_y(self, masks):
        for mask in masks:
            self.pieces[mask | 1] = send_xor(self.pieces[mask], "blk", 1)

    def both(self, after):
        masks = sorted(self.pieces)
        own = [self.pieces[m] for m in masks]
        if after is not None:
            ready = [lax.optimization_barrier((piece, after))[0] for piece in own]
        else:
            ready = own
        return masks, own + [send_xor(piece, "grp", 1) for piece in ready]


class Scatter:
    def __init__(self, keep, send, order):
        self.keep = keep
        self.came = send_xor(send, "blk", order[0])
        self.order = order[1:]

    def halve(self, chain):
        shape = (self.keep.shape[0] // 2,) + self.keep.shape[1:]
        self.keep, send = run(halve_kernel, [self.keep, self.came], [(shape, BF)] * 2, "halve", chain=chain)
        self.came = send_xor(send, "blk", self.order[0])
        self.order = self.order[1:]

    def total(self):
        return self.keep[0].astype(F32) + self.came[0].astype(F32)


def sum_axis(block, axis, masks):
    for mask in masks:
        block = block + send_xor(block, axis, mask)
    return block


def fold_share(block, width):
    rows = block.shape[0]
    return jnp.moveaxis(block.reshape(rows, -1, width), 1, 0).reshape(-1, width)


def unfold_shares(columns, shares, feat):
    width = columns.shape[1]
    blocks = columns.reshape(shares, feat // width, -1, width)
    return jnp.moveaxis(blocks, 1, 2).reshape(-1, feat)


def stream(rows, grad_rows, shape, hid, weights, chain, result):
    half, feat = shape
    width = feat // 4
    lse_rows = -(-(2 * width // HEAD) // 8) * 8

    def stage(body, operands, outs, name, layer=None):
        return run(body, operands, outs, name, chain=chain, unread=result["unread"].get((name, layer), ()))

    def over_x(near):
        return [near, send_xor(near, "grp", 2)]

    def over_core(pieces):
        return [send_xor(piece, "grp", 1) for piece in pieces]

    wide, short = ((half, feat), F32), ((half, feat), BF)
    projected = [((2, half, 2 * width), BF), ((2, half, width), BF)]
    pieces = 4 * [((half, width), BF)]
    hidden_shape = ((2, half, hid), BF)
    sums_shape = ((8, feat), F32)
    kept = []
    for layer in range(LAYERS):
        w = weights[layer]
        if layer == 0:
            kv, q = stage(lambda *r: qkv_kernel(layer, *r), [rows, *w["qkv"], *w["bias"]], projected, "qkv")
        kv_far = send_xor(kv, "blk", 1)
        yield "qkv", layer
        chosen = list(stage(lambda *r: choose_kernel(*r[:3], *r[4:]), [kv, kv_far, w["far"], w["vec"]], pieces, "choose", layer))
        chosen += over_core(chosen)
        near, mixed, lse, used = stage(
            attend_kernel, [q] + chosen + [*w["out"]],
            [short, saved(((2, half, width), BF)), ((lse_rows, half), F32), ((4, 2 * half, width), BF)], "attend")
        branch = over_x(near)
        yield "attend", layer
        resid_one, hidden, act, slope, near = stage(
            lambda *r: feed_kernel(layer, *r),
            branch + [in_hbm(b) for b in [rows, w["vec"]] + w["up"] + w["down"] + w["bias"]],
            [wide, saved(short), saved(hidden_shape), hidden_shape, short], "feed", layer)
        branch = over_x(near)
        yield "feed", layer
        before = (rows, q, used, lse, mixed, resid_one, hidden, act, slope)
        if layer < LAYERS - 1:
            after = weights[layer + 1]
            resid_two, rows, kv, q = stage(
                lambda *r: norm_two_qkv_kernel(layer, *r),
                branch + [resid_one, w["vec"], *after["qkv"], *after["bias"]],
                [wide, short] + projected, "norm_two_qkv")
        else:
            resid_two, rows = stage(lambda *r: norm_two_kernel(layer, *r), branch + [resid_one, w["vec"]],
                                    [wide, short], "norm_two")
        result["outputs"].append(rows[:half // 2])
        kept.append(before + (resid_two,))

    grads = [grad_rows]
    for layer in reversed(range(LAYERS)):
        w = weights[layer]
        rows, q, used, lse, mixed, resid_one, hidden, act, slope, resid_two = kept[layer]
        d_two, feed, sums_two, d_pre, g_up, near = stage(
            lambda *r: back_feed_kernel(layer, len(grads), *r),
            grads + [resid_two, w["vec"], *w["up"], *w["down"], slope],
            [wide, short, sums_shape, hidden_shape, ((2, 1, hid), F32), short], "back_feed")
        result["feed"][layer] = [hidden, feed, d_pre, act]
        branch = over_x(near)
        yield "back_feed", layer
        d_one, branch, sums_one, dq, stay, *go = stage(
            lambda *r: back_attend_kernel(layer, *r),
            branch + [d_two, resid_one, w["vec"], *w["out"], q, used, lse],
            [wide, short, sums_shape, ((2, half, width), BF), ((2, half, 2 * width), F32)] + pieces, "back_attend")
        dkv, = stage(add_crossed_kernel, [stay] + over_core(go), [((2, half, 2 * width), BF)], "add_crossed")
        dkv_far = send_xor(dkv, "blk", 1)
        yield "back_attend", layer
        outs = [short] if layer else [((half // 2, feat), F32), ((half // 2, feat), BF)]
        d_qkv, g_qkv, *outs = stage(
            back_qkv_kernel, [dq, dkv, dkv_far, w["far"], *w["qkv"]],
            [((2, half, 3 * width), BF), ((2, 1, 3 * width), F32)] + outs, "back_qkv")
        result["attend"][layer] = [rows, branch, d_qkv, mixed]
        result["smalls"][layer] = [sums_two, sums_one, g_up, g_qkv]
        if layer:
            grads = over_x(outs[0]) + [d_one]
        else:
            came = send_xor(outs[1], "grp", 2)
            result["grad"] = d_one[:half // 2] + outs[0] + came.astype(F32)
        yield "back_qkv", layer


def per_device(layer_input, w_query, w_key, w_value, b_query, b_value, w_out, b_out, gain_one,
               bias_one, w_up, b_up, w_down, b_down, gain_two, bias_two, head_table, grad_top):
    blk_count = lax.axis_size("blk")
    grp_count = lax.axis_size("grp")
    grp = lax.axis_index("grp")
    blk = lax.axis_index("blk")
    feat = w_out.shape[2]
    share_rows = w_query.shape[1]
    width = w_query.shape[2]
    heads = width // HEAD
    hid = w_up.shape[2]
    per = b_out.shape[1]
    up_per = b_up.shape[1]
    blk_masks = [1 << bit for bit in bits_of(blk_count)[::-1]]
    packed = blk_count == 8 and share_rows % 32 == 0 and per % 8 == 0
    block_own = blk % NB
    target = jnp.where(block_own == 0, head_table[:, :, 0], head_table[:, :, 1])
    far = (target != block_own).astype(F32)
    far = jnp.stack([lax.dynamic_slice_in_dim(far, g * heads, heads, 1) for g in (grp, grp ^ 1)], 1)
    far_cols = jnp.broadcast_to(far[:, :, None, :, None], (LAYERS, 2, 2, heads, HEAD)).reshape(LAYERS, 2, 1, 2 * width)

    start = layer_input[:, 0]
    row_top = jnp.concatenate([start, send_xor(start, "grp", 2)], 1)
    grad_start = grad_top[:, 0]
    grad_rows = jnp.concatenate([grad_start, send_xor(grad_start, "grp", 2)], 1)

    micros = range(layer_input.shape[0])
    count = len(micros)
    chain = Order()
    results = [{"outputs": [], "feed": {}, "attend": {}, "smalls": {}, "unread": {}} for _ in micros]
    weights = [{"far": pick(far_cols, layer)} for layer in range(LAYERS)]
    where = (jnp.stack([blk, grp]).astype(jnp.int32), pl.BlockSpec((2,), lambda i: (0,), memory_space=pltpu.SMEM))
    grad_feed, grad_attend, tiny = {}, {}, []
    smalls = [b_query, b_value, b_out, gain_one, bias_one, b_down, gain_two, bias_two]
    small_rows = len(smalls) * LAYERS
    vec_shape = (small_rows, feat)

    def factors(name, layer):
        return [f for r in results for f in r[name][layer]]

    chunks = blk_count if packed else 1

    def sum_feed(layer):
        rest = [((2, feat // chunks, hid), BF)] * chunks
        grad_feed[layer] = run(lambda *r: grad_feed_kernel(count, chunks, *r), factors("feed", layer),
                               [((2, feat, hid), BF)] + rest, "grad_feed", 16, chain=chain)

    def sum_attend(layer):
        vectors = tiny if packed and layer == 0 else []
        high = feat + (len(vectors) // 2) * blk_count * 8 * LAYERS
        rest = [((high // chunks, feat), BF)] * chunks
        grad_attend[layer] = run(lambda *r: grad_attend_kernel(count, blk_count, len(vectors) // 2, *r),
                                 factors("attend", layer) + vectors, [((high, feat), BF)] + rest, "grad_attend", 16,
                                 chain=chain)

    def add_small():
        sums = sum([r["smalls"][layer] for layer in range(LAYERS) for r in results], [])
        tiny.extend(run(lambda *r: small_kernel(LAYERS, *r), sums, [((8 * LAYERS, feat), F32)] * 2, "small",
                        chain=chain))

    if packed:
        def pack(layer, *more, scratch=(), order=None):
            rows = share_rows + (small_rows if more else 0)
            return run(pack_kernel, [pick(a, layer) for a in (w_key, w_value, w_query, w_out)] + list(more),
                       [((rows, feat), BF)], "pack", 60, scratch, order)[0]

        first = Gather(pack(0, *smalls, b_up, scratch=[pltpu.VMEM(vec_shape, F32)]))
        first.step([1, 2, 4, 6], None)
        first.over_y([2, 4, 6])
        early, attend_share, late = run(
            shares_kernel, [pick(a, 1) for a in (w_key, w_value, w_query, w_out)]
            + [pick(a, layer) for layer in range(LAYERS) for a in (w_up, w_down)],
            [((2, share_rows, feat), BF), ((share_rows, feat), BF), ((2, share_rows, feat), BF)], "shares", 60)
        gathered = {"early": lax.all_gather(early, "blk", axis=1, tiled=True)}
        lanes = jnp.arange(feat)[None, :]
        spread = (lanes % per == jnp.arange(per)[:, None]).astype(BF)
        up_spread = (lanes % up_per == jnp.arange(up_per)[:, None]).astype(BF)

        def start_feed():
            block = lax.optimization_barrier((late, chain.token))[0]
            gathered["late"] = lax.all_gather(block, "blk", axis=1, tiled=True)

        def over_cores(name):
            block = gathered[name]
            return [block, send_xor(lax.optimization_barrier((block, chain.token))[0], "grp", 1)]

        def start_attend():
            flow = Gather(attend_share)
            flow.step([1, 2, 4, 6], chain.token)
            flow.over_y([2, 4, 6])
            gathered["attend1"] = flow
            results[1]["unread"]["feed", 0] = [flow.pieces[mask] for mask in (1, 2, 4, 6)]

        def have_early():
            both = over_cores("early")
            weights[0].update(up=[pick(b, 0) for b in both], down=[pick(b, 1) for b in both])

        def have_attend():
            masks, pieces = gathered["attend1"].both(chain.token)
            outs = run(lambda *r: assemble_kernel(masks, per, up_per, *r), pieces + [where],
                       [((feat, 3 * width), BF)] * 2 + [((width, feat), BF)] * 2, "assemble",
                       scratch=[pltpu.VMEM((width, feat), F32)], chain=chain)
            weights[1].update(qkv=outs[:2], out=outs[2:])

        def have_late():
            both = over_cores("late")
            weights[1].update(up=[pick(b, 0) for b in both], down=[pick(b, 1) for b in both])

        sums_of = {}

        def scatter(key, grads, part=None):
            here, *away = grads
            came = [send_xor(piece, "grp", 1) for piece in away]
            if part is not None:
                groups, depth = [pick(a, part) for a in [here] + came], 1
            else:
                groups, depth = [here] + came, 2 if here.ndim == 3 else 1
            outs = [((blk_count // 2, depth, here.shape[-2] // blk_count, feat), BF)] * 2
            keep, send = run(lambda *r: split_kernel(blk_count, ORDERS[key], 1, 0, *r), groups + [where], outs, "split",
                             16, chain=chain)
            sums_of[key] = Scatter(keep, send, ORDERS[key])

        steps = {
            "A": lambda: sum_feed(1), "B": lambda: scatter("A", grad_feed[1]),
            "C": lambda: sum_attend(1), "D": lambda: scatter("C", grad_attend[1]),
            "a": lambda: sum_feed(0), "b": lambda: scatter("a", grad_feed[0], 0), "e": lambda: scatter("e", grad_feed[0], 1),
            "c": lambda: sum_attend(0), "d": lambda: scatter("c", grad_attend[0]), "m": add_small,
        }
        for letter, key in zip("FGfhg", "ACaec"):
            steps[letter] = lambda key=key: sums_of[key].halve(chain)

        masks, pieces = first.both(None)
        outs = run(lambda *r: assemble_kernel(masks, per, up_per, *r), [in_hbm(p) for p in pieces] + [where, spread, up_spread],
                   [((feat, 3 * width), BF)] * 2 + [((width, feat), BF)] * 2 + [(vec_shape, BF)] + [((8, feat), F32)] * 2,
                   "assemble", scratch=[pltpu.VMEM((width, feat), F32)], chain=chain)
        weights[0].update(qkv=outs[:2], out=outs[2:4])
        table, *biases = outs[4:]
        vec = table + send_xor(table, "grp", 2)
        after = {
            ("attend", 0, 1): lambda: (have_early(), start_feed(), start_attend()),
            ("feed", 0, 1): have_attend,
            ("attend", 1, 1): have_late,
        }
    else:
        table = jnp.zeros(vec_shape, BF)
        rows = jnp.stack(smalls).reshape(small_rows, per)
        table = lax.dynamic_update_slice(table, rows, (0, (grp * blk_count + blk) * per))
        spots = jnp.zeros((8, feat), BF)
        spots = lax.dynamic_update_slice(spots, b_query, (0, 2 * width + blk * per))
        spots = lax.dynamic_update_slice(spots, b_value, (LAYERS, width + blk * per))
        spots = lax.dynamic_update_slice(spots, b_up, (2 * LAYERS, blk * up_per))
        table = sum_axis(table, "blk", blk_masks)
        spots = sum_axis(spots, "blk", blk_masks).astype(F32)
        bias = jnp.zeros((8, feat), F32)
        bias = bias.at[:LAYERS].set(spots[:LAYERS] + spots[LAYERS:2 * LAYERS])
        bias = bias.at[LAYERS:2 * LAYERS].set(spots[2 * LAYERS:3 * LAYERS])
        for layer in range(LAYERS):
            block = jnp.concatenate([w_key[layer], w_value[layer], w_query[layer],
                                     fold_share(w_out[layer], width)], 1)
            block = lax.all_gather(block, "blk", axis=0, tiled=True)
            pair = [block, send_xor(block, "grp", 1)]
            block = lax.all_gather(jnp.stack([w_up[layer], w_down[layer]]), "blk", axis=1, tiled=True)
            both = [block, send_xor(block, "grp", 1)]
            weights[layer].update(qkv=[b[:, :3 * width] for b in pair],
                                  out=[unfold_shares(b[:, 3 * width:], blk_count, feat) for b in pair],
                                  up=[pick(b, 0) for b in both], down=[pick(b, 1) for b in both])
        biases = [bias, send_xor(bias, "grp", 1)]
        vec = sum_axis(table, "grp", [2, 1])
        after = {}
        for layer in range(LAYERS):
            after["back_feed", layer, count - 1] = lambda layer=layer: sum_feed(layer)
            after["back_qkv", layer, count - 1] = lambda layer=layer: sum_attend(layer)

    vec = vec.astype(F32)
    for w in weights:
        w.update(vec=vec, bias=biases)
    streams = [stream(pick(row_top, m), pick(grad_rows, m), row_top.shape[1:], hid, weights, chain, results[m])
               for m in micros]
    done = False
    while not done:
        for m, one in enumerate(streams):
            label = next(one, None)
            done = label is None
            if not done and label + (m,) in after:
                after[label + (m,)]()
            if not done and packed:
                for letter in SLOTS.get(label + (m,), ""):
                    steps[letter]()
    if packed:
        late, up, down, attend, attend1 = [sums_of[key].total() for key in "AaecC"]
        grad_feed = {0: jnp.concatenate([up, down]), 1: late}
        grad_attend = {0: attend[0, :share_rows], 1: attend1[0]}
    else:
        for dim, sums in ((1, grad_feed), (0, grad_attend)):
            for layer in sums:
                block = sums[layer][0] + send_xor(sums[layer][1], "grp", 1)
                sums[layer] = lax.psum_scatter(block, "blk", scatter_dimension=dim, tiled=True).astype(F32)

    if packed:
        tiny = attend[0, share_rows:]
    else:
        add_small()
        tiny = sum_axis(tiny[0] + send_xor(tiny[1], "grp", 1), "blk", blk_masks)
    tiny = tiny.reshape(LAYERS, 8, feat)
    six = tiny[:, :SMALLS]
    six = lax.dynamic_slice_in_dim(six, (grp * blk_count + blk) * per, per, 2)
    g_b_up = lax.dynamic_slice_in_dim(tiny[:, 6], blk * up_per, up_per, 1)
    g_b_value = lax.dynamic_slice_in_dim(tiny[:, 7], width + blk * per, per, 1)
    g_b_query = lax.dynamic_slice_in_dim(tiny[:, 7], 2 * width + blk * per, per, 1)
    feeds = jnp.stack([grad_feed[layer] for layer in range(LAYERS)])
    attends = jnp.stack([grad_attend[layer] for layer in range(LAYERS)])
    g_out = jnp.stack([unfold_shares(attends[layer, :, 3 * width:], 1, feat) for layer in range(LAYERS)])
    return (
        jnp.stack([jnp.stack([r["outputs"][layer] for r in results]) for layer in range(LAYERS)])[:, :, None],
        jnp.stack([r["grad"] for r in results])[:, None],
        attends[:, :, 2 * width:3 * width],
        attends[:, :, :width],
        attends[:, :, width:2 * width],
        g_b_query,
        g_b_value,
        g_out,
        six[:, 0],
        six[:, 1],
        six[:, 2],
        feeds[:, 0],
        g_b_up,
        feeds[:, 1],
        six[:, 3],
        six[:, 4],
        six[:, 5],
    )


def solution(mesh):
    rows = P(None, "blk", "grp", None)
    cols = P(None, "blk", "grp")
    both = P(None, ("grp", "blk"))
    tall = P(None, ("grp", "blk"), None)
    return jax.shard_map(
        per_device,
        mesh=mesh,
        in_specs=(rows, cols, cols, cols, both, both, tall, both, both, both, cols, both, tall,
                  both, both, both, P(), rows),
        out_specs=(P(None, None, "blk", "grp", None), rows, cols, cols, cols, both, both, tall,
                   both, both, both, cols, both, tall, both, both, both),
        check_vma=False,
    )
```
